32 devices in a mesh: dp: 4 (over y, x), vocab: 8 (over z, core).
Axes of the slice: x: 2, y: 2, z: 4, core: 2. Of those that a mesh axis runs over, the one named last changes fastest.
Arguments:
- token_ids: int32 [32768], P(('dp', 'vocab')), may hold values from 0 to 32127, as said below
- seq_lengths: int32 [64], P(('dp', 'vocab')), may hold values from 1 to 512, 24576 in all
- table: bfloat16 [32128, 768], P('vocab'), may hold values from -6 to 6
- gain_one: float32 [768], replicated, may hold values from 0.5 to 1.5
- w_query: bfloat16 [768, 768], replicated, may hold values from -0.078125 to 0.078125
- w_key: bfloat16 [768, 768], replicated, may hold values from -0.078125 to 0.078125
- w_value: bfloat16 [768, 768], replicated, may hold values from -0.21875 to 0.21875
- w_out: bfloat16 [768, 768], replicated, may hold values from -2.5 to 2.5
- gain_two: float32 [768], replicated, may hold values from 0.5 to 1.5
- w_in: bfloat16 [768, 3072], replicated, may hold values from -0.21875 to 0.21875
- w_down: bfloat16 [3072, 768], replicated, may hold values from -0.109375 to 0.109375
- rel_bias: float32 [32, 12], replicated, may hold values from -6 to 6
- cotangent: bfloat16 [32768, 768], P(('dp', 'vocab')), may hold values from -6 to 6
Outputs:
- mixed_out: bfloat16 [32768, 768], P(('dp', 'vocab'))
- row_grad: float32 [32768, 768], P(('dp', 'vocab'))
- table_grad: float32 [32128, 768], P('vocab')
- gain_one_grad: float32 [768], replicated
- query_grad: float32 [768, 768], P('dp', 'vocab')
- key_grad: float32 [768, 768], P('dp', 'vocab')
- value_grad: float32 [768, 768], P('dp', 'vocab')
- out_grad: float32 [768, 768], P('dp', 'vocab')
- gain_two_grad: float32 [768], replicated
- in_grad: float32 [768, 3072], P('dp', 'vocab')
- down_grad: float32 [3072, 768], P('dp', 'vocab')
- bias_grad: float32 [32, 12], replicated
The draws below stay inside these ranges and needn't reach their ends.
Inputs may be any that keep to these rules, and one draw needn't show every extreme that they name: `token_ids`: ids are table rows. Among the 1024 ids of one device at most 256 lie in the range of one index o of vocab (ids o * 4016 to o * 4016 + 4015), and exactly 256 lie in one such range: the 128 ids of the instruction that opens each of the device's sequences, the same in all of them.
All inputs are finite; a program needn't handle non-finite values. No bound on the sum of `seq_lengths` on one device may be relied on, other than what follows from the above.
Results may differ from the reference program's by a relative error of at most 0.015.
Values may be sent and summed in bfloat16 or wider, within the bound.
No kernel may reach another device: no remote copies, remote signals or barrier semaphores. Data moves between devices by JAX's collectives and lax.ppermute only.
A program may use at most 256 MiB of HBM per device.

```python
import math
import jax
import jax.numpy as jnp
import numpy as np
from jax import lax

D = 768
FF = 3072
HEADS = 12
VOCAB = 32128
BUCKETS = 32
SEQ = 512
SEQ_DEV = 2
NSEQ = 64
TOKENS = 32768
CAP = 256
N_DP = 4
N_VOCAB = 8


def draw_token_ids(key, part):
    key = jax.random.fold_in(key, 11)
    shard_rows = VOCAB // N_VOCAB
    instr_len = CAP // SEQ_DEV
    spare_slots = (N_VOCAB - 1) * CAP
    rest_len = SEQ_DEV * (SEQ - instr_len)

    def one_block(block_key):
        subkeys = jax.random.split(block_key, 4)
        hot_owner = jax.random.randint(subkeys[0], (), 0, N_VOCAB, dtype=jnp.int32)
        instr_ids = hot_owner * shard_rows + jax.random.randint(subkeys[1], (instr_len,), 0, shard_rows, dtype=jnp.int32)
        others = jnp.arange(spare_slots, dtype=jnp.int32) // CAP
        others = others + (others >= hot_owner).astype(jnp.int32)
        others = jax.random.permutation(subkeys[2], others)[:rest_len]
        offsets = jax.random.randint(subkeys[3], (rest_len,), 0, shard_rows, dtype=jnp.int32)
        rest_ids = (others * shard_rows + offsets).reshape(SEQ_DEV, SEQ - instr_len)
        head_ids = jnp.broadcast_to(instr_ids[None, :], (SEQ_DEV, instr_len))
        return jnp.concatenate([head_ids, rest_ids], axis=1).reshape(-1)
    blocks = jax.vmap(one_block)(jax.random.split(key, N_DP * N_VOCAB))
    return blocks.reshape(-1).astype(jnp.int32)


def strengthened(drawn, key, source, target, shards_of, factor):
    def block_of(axis_at):
        return (jnp.arange(drawn.shape[axis_at]) // (drawn.shape[axis_at] // shards_of)).reshape((-1,) + (1,) * (drawn.ndim - 1 - axis_at))

    first = jax.random.permutation(key, shards_of)[block_of(target)]
    second = (block_of(target) + shards_of // 2) % shards_of
    return jnp.where((block_of(source) == first) | (block_of(source) == second), factor * drawn, drawn)


def block_levels(own_key, dims, shards, low, high):
    def one(axis_at, blocks):
        heights = jax.random.uniform(jax.random.fold_in(jax.random.fold_in(own_key, 6), axis_at), (blocks,), jnp.float32, low / len(shards), high / len(shards))
        return jnp.repeat(jnp.exp(heights), dims[axis_at] // blocks).reshape((-1,) + (1,) * (len(dims) - axis_at - 1))

    factor_of = one(*shards[0])
    for cut in shards[1:]:
        factor_of = factor_of * one(*cut)
    return factor_of


def length_profile(number_of, total, reach, lean):
    portions = [(1 << 20) // math.isqrt(grade ** lean) + 1 for grade in range(2, number_of + 1)]
    rest, holding = total - reach - (number_of - 1), [1] * (number_of - 1)
    while rest > 0:
        free = [i for i in range(number_of - 1) if holding[i] < reach]
        pool, remaining = sum([portions[i] for i in free]), rest
        for i in free:
            extra = min(reach - holding[i], max(1, remaining * portions[i] // pool), rest)
            holding[i] = holding[i] + extra
            rest = rest - extra
    return np.array([reach] + holding)


def uneven_parts(rng, number_of, total, most, slope):
    if number_of == 2:
        one = jax.random.randint(rng, (), max(1, total - most), min(most, total - 1) + 1)
        return jnp.stack([one, total - one])
    lengths = jnp.asarray(length_profile(number_of, total, most, slope), jnp.int32)
    pairs = (number_of - 1) // 2
    giver, receiver = lengths[1:1 + 2 * pairs:2], lengths[2:2 + 2 * pairs:2]
    slack = jnp.minimum(giver - 1, most - receiver)
    shifted = jax.random.randint(jax.random.fold_in(rng, 1), (pairs,), 0, 1 << 20) % (slack + 1)
    lengths = lengths.at[1:1 + 2 * pairs:2].set(giver - shifted).at[2:2 + 2 * pairs:2].set(receiver + shifted)
    return lengths[jax.random.permutation(jax.random.fold_in(rng, 2), number_of)]


def noise(stream_key, shape, deviation, limit, cuts=(), kind=jnp.bfloat16):
    values = jax.random.normal(stream_key, shape, jnp.float32) * deviation
    if len(cuts) > 0:
        values = block_levels(stream_key, shape, cuts, -0.22, 0.18) * values
    return jnp.clip(values, min=-limit, max=limit).astype(kind)


def noise_with(key, shape, deviation, most, shards, heavy, kind=jnp.bfloat16):
    drawn = deviation * jax.random.normal(key, shape, jnp.float32)
    if shards:
        drawn = drawn * block_levels(key, shape, shards, -0.22, 0.18)
    return jnp.clip(strengthened(drawn, jax.random.fold_in(key, 3), *heavy), -most, most).astype(kind)


def setup_inputs(seed: int = 0) -> dict:
    seeds = jax.random.split(jax.random.key(seed), 14)
    return {
        "token_ids": draw_token_ids(jax.random.fold_in(seeds[13], 71), 0),
        "seq_lengths": uneven_parts(seeds[1], NSEQ, NSEQ * SEQ * 3 // 4, SEQ, 2).astype(jnp.int32),
        "table": noise(seeds[2], (VOCAB, D), 1.0, 6.0, ((0, 8),)),
        "gain_one": jnp.clip(1.0 + 0.1 * jax.random.normal(seeds[3], (D,), jnp.float32), 0.5, 1.5),
        "w_query": noise(seeds[4], (D, D), (8 * D) ** -0.5, 0.078125),
        "w_key": noise(seeds[5], (D, D), (8 * D) ** -0.5, 0.078125),
        "w_value": noise(seeds[6], (D, D), D ** -0.5, 0.21875),
        "w_out": noise(seeds[7], (D, D), (max(1, D // 128)) ** -0.5, 2.5),
        "gain_two": jnp.clip(1.0 + 0.1 * jax.random.normal(seeds[8], (D,), jnp.float32), 0.5, 1.5),
        "w_in": noise(seeds[9], (D, FF), D ** -0.5, 0.21875),
        "w_down": noise(seeds[10], (FF, D), FF ** -0.5, 0.109375),
        "rel_bias": noise(seeds[11], (BUCKETS, HEADS), 1.0, 6.0, (), jnp.float32),
        "cotangent": noise_with(seeds[12], (TOKENS, D), 1.0, 6.0, ((0, 32),), (0, 1, 32, 2.75)),
    }


@jax.custom_vjp
def low(v):
    return lax.optimization_barrier(v.astype(jnp.bfloat16)).astype(jnp.float32)

@jax.custom_vjp
def low_back(v):
    return v

def low_keep(v):
    return (low(v), None)

def low_pass(kept, grad):
    return (grad,)

def back_keep(v):
    return (v, None)

def back_low(kept, grad):
    return (low(grad),)
low.defvjp(low_keep, low_pass)
low_back.defvjp(back_keep, back_low)
EPS = 1e-06
PRECISE = lax.Precision.HIGHEST
MASKED = -1e+30
THRESHOLDS = (12, 16, 23, 32, 46, 64, 91)

def norm_apply(values, gain_vec):
    scaling = lax.rsqrt(lax.optimization_barrier(jnp.mean(values * values, axis=-1, keepdims=True)) + EPS)
    return values * scaling * gain_vec

def gelu_tanh(values):
    return jax.nn.gelu(values, approximate=True)

def bucket_index(length):
    places = jnp.arange(length, dtype=jnp.int32)
    offset = places[None, :] - places[:, None]
    distance = jnp.abs(offset)
    far_bucket = jnp.full_like(distance, 8)
    for threshold in THRESHOLDS:
        far_bucket = far_bucket + (distance >= threshold).astype(jnp.int32)
    upper = jnp.where(offset > 0, 16, 0).astype(jnp.int32)
    return upper + jnp.where(distance < 8, distance, far_bucket)

def attend(pieces, bias_full):
    query_in, keys_in, values_in, length = pieces
    raw_scores = low_back(jnp.einsum('qhe,khe->hqk', query_in, keys_in, precision=PRECISE))
    seq_len = query_in.shape[0]
    allowed = jnp.arange(seq_len, dtype=jnp.int32)[None, None, :] < length
    scores = jnp.where(allowed, raw_scores + bias_full, MASKED)
    probs_low = low(jax.nn.softmax(scores, axis=-1))
    return jnp.einsum('hqk,khe->qhe', probs_low, values_in, precision=PRECISE)

def layer_block(x_rows, weights, lengths_block, buckets):
    gain_one, w_query, w_key, w_value, w_out, gain_two, w_in, w_down, rel_bias = weights
    seq_count = lengths_block.shape[0]
    tok_count, model_width = x_rows.shape
    seq_len = tok_count // seq_count
    head_count = rel_bias.shape[1]
    block_shape = (seq_count, seq_len, head_count, model_width // head_count)
    hidden = low(norm_apply(x_rows, gain_one))
    query_all = low_back(low(jnp.dot(hidden, w_query, precision=PRECISE)))
    keys_all = low_back(low(jnp.dot(hidden, w_key, precision=PRECISE)))
    values_all = low_back(low(jnp.dot(hidden, w_value, precision=PRECISE)))
    bias_full = jnp.transpose(rel_bias[buckets], (2, 0, 1))

    def one_sequence(pieces):
        return attend(pieces, bias_full)
    context = lax.map(jax.checkpoint(one_sequence), (query_all.reshape(block_shape), keys_all.reshape(block_shape), values_all.reshape(block_shape), lengths_block))
    context = low_back(low(context.reshape(tok_count, model_width)))
    middle = x_rows + low_back(jnp.dot(context, w_out, precision=PRECISE))
    hidden_two = low(norm_apply(middle, gain_two))
    pre_act = low_back(jnp.dot(hidden_two, w_in, precision=PRECISE))
    act_low = low(gelu_tanh(pre_act))
    return middle + low_back(jnp.dot(act_low, w_down, precision=PRECISE))

def reference(token_ids, seq_lengths, table, gain_one, w_query, w_key, w_value, w_out, gain_two, w_in, w_down, rel_bias, cotangent):
    table_full = table.astype(jnp.float32)
    weights = (gain_one.astype(jnp.float32), w_query.astype(jnp.float32), w_key.astype(jnp.float32), w_value.astype(jnp.float32), w_out.astype(jnp.float32), gain_two.astype(jnp.float32), w_in.astype(jnp.float32), w_down.astype(jnp.float32), rel_bias.astype(jnp.float32))

    def lookup(table_in):
        return table_in[token_ids]
    x_all, pull_table = jax.vjp(lookup, table_full)
    seq_total = seq_lengths.shape[0]
    group_size = math.gcd(seq_total, max(1, 4096 // SEQ))
    step_count = seq_total // group_size
    buckets = bucket_index(SEQ)
    x_groups = x_all.reshape(step_count, group_size * SEQ, D)
    cot_groups = cotangent.astype(jnp.float32).reshape(step_count, group_size * SEQ, D)
    len_groups = seq_lengths.reshape(step_count, group_size)
    zero_grads = jax.tree.map(jnp.zeros_like, weights)

    def group_step(running, pieces):
        x_part, cot_part, len_part = pieces

        def forward(rows_in, weights_in):
            return layer_block(rows_in, weights_in, len_part, buckets)
        out_part, pull_layer = jax.vjp(forward, x_part, weights)
        d_rows, d_weights = pull_layer(cot_part)
        running = jax.tree.map(jnp.add, running, d_weights)
        return (running, (out_part.astype(jnp.bfloat16), d_rows))
    totals, (mixed_out, row_grad) = lax.scan(group_step, zero_grads, (x_groups, cot_groups, len_groups))
    mixed_out = mixed_out.reshape(TOKENS, D)
    row_grad = row_grad.reshape(TOKENS, D)
    table_grad = pull_table(row_grad)[0]
    return (mixed_out, row_grad, table_grad, totals[0], totals[1], totals[2], totals[3], totals[4], totals[5], totals[6], totals[7], totals[8])
```

```python
from functools import partial

import jax
import jax.numpy as jnp
import numpy as np
from jax import lax
from jax.experimental import pallas as pl
from jax.experimental.pallas import tpu as pltpu
from jax.sharding import PartitionSpec as P

EPS = 1e-06
PRECISE = lax.Precision.HIGHEST
MASKED = -1e30
THRESHOLDS = (12, 16, 23, 32, 46, 64, 91)
LANES = 128
NOWHERE = 1 << 30
BF = jnp.bfloat16
F32 = jnp.float32
NN = (((1,), (0,)), ((), ()))
NT = (((1,), (1,)), ((), ()))
TN = (((0,), (0,)), ((), ()))


def mm(left, right, dims=NN):
    return lax.dot_general(left, right, dims, preferred_element_type=F32)


def params(**more):
    return pltpu.CompilerParams(vmem_limit_bytes=56 << 20, **more)


def cost(macs, moved):
    return pl.CostEstimate(flops=2 * macs, bytes_accessed=moved, transcendentals=0)


def whole(shape):
    return pl.BlockSpec(shape, lambda *_: (0,) * len(shape), pipeline_mode=pl.Buffered(1))


def bucket_of(offset):
    distance = np.abs(offset)
    far = 8 + sum((distance >= t).astype(np.int32) for t in THRESHOLDS)
    return np.where(offset > 0, 16, 0) + np.where(distance < 8, distance, far)


def band_offsets():
    lane = np.arange(4 * LANES)
    return np.where(lane < 3 * LANES, lane, lane - 4 * LANES) - LANES


def band_onehot(buckets):
    return (bucket_of(band_offsets())[:, None] == np.arange(buckets)[None, :]).astype(np.float32)


def route_kernel(me_ref, ids_row_ref, ids_col_ref, slot_row_ref, slot_col_ref, ask_ref, *, seq_len, opening, shard, owners, cap, width):
    me = me_ref[0]
    tokens = ids_row_ref.shape[1]
    ids_row, ids_col = ids_row_ref[...], ids_col_ref[...]
    owner_row, owner_col = jnp.zeros_like(ids_row), jnp.zeros_like(ids_col)
    for o in range(1, owners):
        owner_row += (ids_row >= o * shard).astype(jnp.int32)
        owner_col += (ids_col >= o * shard).astype(jnp.int32)

    def places(shape, axis):
        t = lax.broadcasted_iota(jnp.int32, shape, axis)
        within = lax.rem(t, seq_len)
        repeated = (within < opening) & (t >= seq_len)
        return t, jnp.where(within < opening, within, t), jnp.logical_not(repeated)

    t_row, at_row, first_row = places((1, tokens), 1)
    t_col, at_col, first_col = places((tokens, 1), 0)
    key_row = jnp.where(first_row, owner_row, -1)
    key_col = jnp.where(first_col, owner_col, -1)
    rank_col = jnp.sum(((key_row == owner_col) & (t_row < at_col)).astype(jnp.int32), axis=1, keepdims=True)
    rank_row = jnp.sum(((key_col == owner_row) & (t_col < at_row)).astype(jnp.int32), axis=0, keepdims=True)
    slot_row_ref[...] = jnp.where(rank_row < cap, (owner_row ^ me) * cap + rank_row, NOWHERE)
    slot_col_ref[...] = jnp.where(rank_col < cap, (owner_col ^ me) * cap + rank_col, NOWHERE)
    over = (jnp.max(rank_row) >= cap).astype(jnp.int32)
    place_col = jnp.where(first_col & (rank_col < cap), owner_col * width + rank_col, -1)
    step = 4 * LANES
    for start in range(0, owners * width, step):
        lane = lax.broadcasted_iota(jnp.int32, (1, step), 1) + start
        asked = jnp.sum(jnp.where(place_col == lane, ids_col + 1, 0), axis=0, keepdims=True) - 1
        ask_ref[:, start : start + step] = jnp.where(lax.rem(lane, width) == width - 1, over, asked)


def route(token_ids, me, seq_len, opening, shard, owners, cap, width):
    tokens = token_ids.shape[0]
    body = partial(route_kernel, seq_len=seq_len, opening=opening, shard=shard, owners=owners, cap=cap, width=width)
    return pl.pallas_call(
        body,
        in_specs=[pl.BlockSpec(memory_space=pltpu.SMEM), pl.BlockSpec(memory_space=pltpu.VMEM), pl.BlockSpec(memory_space=pltpu.VMEM)],
        out_shape=[
            jax.ShapeDtypeStruct((1, tokens), jnp.int32),
            jax.ShapeDtypeStruct((tokens, 1), jnp.int32),
            jax.ShapeDtypeStruct((1, owners * width), jnp.int32),
        ],
        compiler_params=params(),
        name="route",
    )(me, token_ids.reshape(1, -1), token_ids.reshape(-1, 1))


def project_kernel(slot_ref, rows_refs, gain_ref, wq_ref, wk_ref, wv_ref, x_ref, hidden_ref, q_ref, k_ref, v_ref):
    slot = slot_ref[...]
    x = None
    start = 0
    for rows_ref in rows_refs:
        lane = lax.broadcasted_iota(jnp.int32, (slot.shape[0], rows_ref.shape[0]), 1) + start
        part = mm((lane == slot).astype(F32).astype(BF), rows_ref[...])
        x = part if x is None else x + part
        start += rows_ref.shape[0]
    x_ref[...] = x.astype(BF)
    scale = lax.rsqrt(jnp.mean(x * x, axis=1, keepdims=True) + EPS)
    hidden = (x * scale * gain_ref[...]).astype(BF)
    hidden_ref[...] = hidden
    q_ref[...] = mm(hidden, wq_ref[...]).astype(BF)
    k_ref[...] = mm(hidden, wk_ref[...]).astype(BF)
    v_ref[...] = mm(hidden, wv_ref[...]).astype(BF)


def project(slot_col, rows, gain, w_query, w_key, w_value):
    tokens, width = slot_col.shape[0], gain.shape[1]
    tile = min(256, tokens)
    out = pl.BlockSpec((tile, width), lambda t: (t, 0))
    count = sum(r.shape[0] for r in rows)
    return pl.pallas_call(
        project_kernel,
        grid=(tokens // tile,),
        in_specs=[pl.BlockSpec((tile, 1), lambda t: (t, 0)), [whole(r.shape) for r in rows], whole(gain.shape)]
        + [whole(w_query.shape)] * 3,
        out_specs=[out] * 5,
        out_shape=[jax.ShapeDtypeStruct((tokens, width), BF)] * 5,
        compiler_params=params(),
        cost_estimate=cost(tokens * width * (3 * width + count), 14 * tokens * width),
        name="project",
    )(slot_col, rows, gain, w_query, w_key, w_value)


def band_kernel(line_ref, band_ref):
    line = jnp.broadcast_to(line_ref[0], (LANES, line_ref.shape[2]))
    band_ref[0] = pltpu.roll(line, 0, 1, stride=1, stride_axis=0)[:, : 3 * LANES]


def make_band(rel_bias):
    heads = rel_bias.shape[1]
    line = jnp.dot(band_onehot(rel_bias.shape[0]), rel_bias, precision=PRECISE).T.reshape(heads, 1, -1)
    return pl.pallas_call(
        band_kernel,
        grid=(heads,),
        in_specs=[pl.BlockSpec((1,) + line.shape[1:], lambda h: (h, 0, 0))],
        out_specs=pl.BlockSpec((1, LANES, 3 * LANES), lambda h: (h, 0, 0)),
        out_shape=jax.ShapeDtypeStruct((heads, LANES, 3 * LANES), F32),
        compiler_params=params(),
        name="band",
    )(line)


def attend_kernel(len_ref, far_ref, q_ref, k_ref, v_ref, band_ref, ctx_ref, p_ref):
    pair = pl.program_id(1)
    q, k, v = q_ref[...], k_ref[...], v_ref[...]
    seq_len = q.shape[0]
    blocks = seq_len // LANES
    last = far_ref.shape[0] // 2 - 1
    half = lax.broadcasted_iota(jnp.int32, (1, LANES), 1) // (LANES // 2)
    key_at = lax.broadcasted_iota(jnp.int32, (1, seq_len), 1)
    mask = jnp.where(key_at < len_ref[pl.program_id(0)], 0.0, MASKED)
    none = jnp.zeros((), BF)
    ctx = jnp.zeros((seq_len, LANES), F32)
    for h in range(2):
        k_own, v_own = jnp.where(half == h, k, none), jnp.where(half == h, v, none)
        left, right = far_ref[last, 2 * pair + h], far_ref[2 * last + 1, 2 * pair + h]
        for i in range(blocks):
            raw = mm(q[i * LANES : (i + 1) * LANES], k_own, NT)
            tiles = []
            for j in range(blocks):
                cols = slice(j * LANES, (j + 1) * LANES)
                d = j - i
                if abs(d) <= 1:
                    tiles.append(raw[:, cols] + band_ref[h, :, (d + 1) * LANES : (d + 2) * LANES] + mask[:, cols])
                else:
                    tiles.append(raw[:, cols] + (mask[:, cols] + (left if d < 0 else right)))
            scores = jnp.concatenate(tiles, axis=1)
            grown = jnp.exp(scores - jnp.max(scores, axis=1, keepdims=True))
            total = jnp.sum(grown, axis=1, keepdims=True)
            p_ref[0, h, i * LANES : (i + 1) * LANES, :] = (grown * (1.0 / total)).astype(BF)
        ctx = ctx + mm(p_ref[0, h], v_own)
    ctx_ref[...] = ctx.astype(BF)


def attend(q, k, v, lengths, rel_bias, band):
    seqs, heads = lengths.shape[0], rel_bias.shape[1]
    tokens, width = q.shape
    seq_len = tokens // seqs
    block = pl.BlockSpec((seq_len, LANES), lambda s, p, *_: (s, p))
    return pl.pallas_call(
        attend_kernel,
        grid_spec=pltpu.PrefetchScalarGridSpec(
            num_scalar_prefetch=2,
            grid=(seqs, heads // 2),
            in_specs=[block] * 3 + [pl.BlockSpec((2,) + band.shape[1:], lambda s, p, *_: (p, 0, 0))],
            out_specs=[block, pl.BlockSpec((1, 2, seq_len, seq_len), lambda s, p, *_: (s, p, 0, 0))],
        ),
        out_shape=[
            jax.ShapeDtypeStruct((tokens, width), BF),
            jax.ShapeDtypeStruct((seqs, heads, seq_len, seq_len), BF),
        ],
        compiler_params=params(),
        cost_estimate=cost(tokens * seq_len * width * 8, 2 * tokens * seq_len * heads),
        name="attend",
    )(lengths, rel_bias, q, k, v, band)


def attend_back_kernel(q_ref, k_ref, v_ref, do_ref, p_ref, dq_ref, dk_ref, dv_ref, line_ref, ds_ref, band_ref, far_ref):
    seq_at = pl.program_id(1)
    q, k, v, do = q_ref[...], k_ref[...], v_ref[...], do_ref[...]
    seq_len = q.shape[0]
    blocks = seq_len // LANES
    half = lax.broadcasted_iota(jnp.int32, (1, LANES), 1) // (LANES // 2)
    none = jnp.zeros((), BF)

    @pl.when(seq_at == 0)
    def _():
        band_ref[...] = jnp.zeros_like(band_ref)
        far_ref[...] = jnp.zeros_like(far_ref)

    dq = dk = dv = jnp.zeros((seq_len, LANES), F32)
    for h in range(2):
        k_own, v_own = jnp.where(half == h, k, none), jnp.where(half == h, v, none)
        q_own, do_own = jnp.where(half == h, q, none), jnp.where(half == h, do, none)
        near = [jnp.zeros((LANES, LANES), F32) for _ in range(3)]
        far = [jnp.zeros((8, LANES), F32) for _ in range(2)]
        for i in range(blocks):
            rows = slice(i * LANES, (i + 1) * LANES)
            probs = p_ref[0, h, rows, :].astype(F32)
            weighed = probs * mm(do[rows], v_own, NT)
            ds = weighed - probs * jnp.sum(weighed, axis=1, keepdims=True)
            for j in range(blocks):
                d = j - i
                tile = ds[:, j * LANES : (j + 1) * LANES]
                if abs(d) <= 1:
                    near[d + 1] = near[d + 1] + tile
                else:
                    side = 0 if d < 0 else 1
                    far[side] = far[side] + jnp.sum(tile.reshape(LANES // 8, 8, LANES), axis=0)
            ds_ref[rows, :] = ds.astype(BF)
        for d in range(3):
            band_ref[h, :, d * LANES : (d + 1) * LANES] += near[d]
        for side in range(2):
            far_ref[h, :, side * LANES : (side + 1) * LANES] += far[side]
        d_low = ds_ref[...]
        dk = dk + mm(d_low, q_own, TN)
        dv = dv + mm(p_ref[0, h], do_own, TN)
        dq = dq + mm(d_low, k_own)
    dq_ref[...], dk_ref[...], dv_ref[...] = dq.astype(BF), dk.astype(BF), dv.astype(BF)

    @pl.when(seq_at == pl.num_programs(1) - 1)
    def _():
        row = lax.broadcasted_iota(jnp.int32, (8, 1), 0)
        for h in range(2):
            padded = jnp.concatenate([band_ref[h], jnp.zeros((LANES, LANES), F32)], axis=1)
            turned = padded[:8]
            for start in range(8, LANES, 8):
                turned = turned + pltpu.roll(padded[start : start + 8], 4 * LANES - start, 1)
            for bit in (1, 2, 4):
                turned = jnp.where(row & bit > 0, pltpu.roll(turned, 4 * LANES - bit, 1), turned)
            line_ref[0, h : h + 1, :] = jnp.sum(turned, axis=0, keepdims=True)
            line_ref[0, 2 + h : 3 + h, : 2 * LANES] = jnp.sum(far_ref[h], axis=0, keepdims=True)


def attend_back(q, k, v, d_context, probs):
    seqs, heads, seq_len, _ = probs.shape
    tokens, width = q.shape
    block = pl.BlockSpec((seq_len, LANES), lambda p, s: (s, p))
    dq, dk, dv, lines = pl.pallas_call(
        attend_back_kernel,
        grid=(heads // 2, seqs),
        in_specs=[block] * 4 + [pl.BlockSpec((1, 2, seq_len, seq_len), lambda p, s: (s, p, 0, 0))],
        out_specs=[block] * 3 + [pl.BlockSpec((1, 8, 4 * LANES), lambda p, s: (p, 0, 0))],
        out_shape=[jax.ShapeDtypeStruct((tokens, width), BF)] * 3
        + [jax.ShapeDtypeStruct((heads // 2, 8, 4 * LANES), F32)],
        scratch_shapes=[
            pltpu.VMEM((seq_len, seq_len), BF),
            pltpu.VMEM((2, LANES, 3 * LANES), F32),
            pltpu.VMEM((2, 8, 2 * LANES), F32),
        ],
        compiler_params=params(),
        cost_estimate=cost(tokens * seq_len * width * 12, 2 * tokens * seq_len * heads),
        name="attend_back",
    )(q, k, v, d_context, probs)
    near = lines[:, 0:2, :].reshape(heads, -1)
    far = jnp.sum(lines[:, 2:4, : 2 * LANES].reshape(heads, 2, LANES), axis=2)
    return dq, dk, dv, near, far


def middle_kernel(x_ref, ctx_ref, cot_ref, gain_ref, w_out_ref, w_in_ref, w_down_ref, mixed_ref, act_ref, d_pre_ref, hidden_t_ref, d_mid_ref, d_att_ref, d_ctx_ref, gain_grad_ref, *, chunk):
    mid = x_ref[...].astype(F32) + mm(ctx_ref[...], w_out_ref[...])
    gain = gain_ref[...]
    scale = lax.rsqrt(jnp.mean(mid * mid, axis=1, keepdims=True) + EPS)
    hidden_full = mid * scale * gain
    hidden = hidden_full.astype(BF)
    hidden_t_ref[...] = hidden_full.T.astype(BF)
    cot = cot_ref[...]
    mixed, d_hidden = mid, jnp.zeros_like(mid)
    slope = float(np.sqrt(2 / np.pi))
    for start in range(0, w_in_ref.shape[1], chunk):
        cols = slice(start, start + chunk)
        pre = mm(hidden, w_in_ref[:, cols])
        d_act = mm(cot, w_down_ref[cols, :], NT)
        square = pre * pre
        bent = jnp.tanh(slope * pre * (1.0 + 0.044715 * square))
        open_half = 0.5 + 0.5 * bent
        act = (pre * open_half).astype(BF)
        curve = (0.5 * slope) * pre * (1.0 - bent * bent) * (1.0 + (3 * 0.044715) * square)
        d_pre = (d_act * (open_half + curve)).astype(BF)
        act_ref[:, cols] = act
        d_pre_ref[:, cols] = d_pre
        mixed = mixed + mm(act, w_down_ref[cols, :])
        d_hidden = d_hidden + mm(d_pre, w_in_ref[:, cols], NT)
    mixed_ref[...] = mixed.astype(BF)
    u = d_hidden * gain
    swing = jnp.mean(u * mid, axis=1, keepdims=True)
    d_mid = cot.astype(F32) + scale * u - mid * (scale * scale * scale * swing)
    d_mid_ref[...] = d_mid
    d_att = d_mid.astype(BF)
    d_att_ref[...] = d_att
    d_ctx_ref[...] = mm(d_att, w_out_ref[...], NT).astype(BF)

    @pl.when(pl.program_id(0) == 0)
    def _():
        gain_grad_ref[...] = jnp.zeros_like(gain_grad_ref)

    gain_grad_ref[...] += jnp.sum((d_hidden * mid * scale).reshape(-1, 8, mid.shape[1]), axis=0)


def middle_part(x, ctx, cot, gain, w_out, w_in, w_down):
    tokens, width = x.shape
    wide = w_in.shape[1]
    tile = min(256, tokens)
    rows = pl.BlockSpec((tile, width), lambda t: (t, 0))
    wide_rows = pl.BlockSpec((tile, wide), lambda t: (t, 0))
    return pl.pallas_call(
        partial(middle_kernel, chunk=min(768, wide)),
        grid=(tokens // tile,),
        in_specs=[rows] * 3 + [whole(a.shape) for a in (gain, w_out, w_in, w_down)],
        out_specs=[rows, wide_rows, wide_rows, pl.BlockSpec((width, tile), lambda t: (0, t)), rows, rows, rows]
        + [pl.BlockSpec((8, width), lambda t: (0, 0))],
        out_shape=[
            jax.ShapeDtypeStruct((tokens, width), BF),
            jax.ShapeDtypeStruct((tokens, wide), BF),
            jax.ShapeDtypeStruct((tokens, wide), BF),
            jax.ShapeDtypeStruct((width, tokens), BF),
            jax.ShapeDtypeStruct((tokens, width), F32),
            jax.ShapeDtypeStruct((tokens, width), BF),
            jax.ShapeDtypeStruct((tokens, width), BF),
            jax.ShapeDtypeStruct((8, width), F32),
        ],
        compiler_params=params(),
        cost_estimate=cost(tokens * width * (4 * wide + 2 * width), 4 * width * wide + 8 * tokens * (wide + width)),
        name="middle",
    )(x, ctx, cot, gain, w_out, w_in, w_down)


def wide_grads_kernel(core_ref, hidden_t_ref, cot_t_ref, d_pre_ref, act_ref, in_keep_ref, in_send_ref, down_keep_ref, down_send_ref, parts_ref, *, groups, owners):
    core = core_ref[0]
    step = pl.program_id(0)
    in_part = mm(hidden_t_ref[...], d_pre_ref[...]).astype(BF).reshape(groups, 1, -1, d_pre_ref.shape[1])

    @pl.when(lax.rem(step, 2) == core)
    def _():
        in_keep_ref[...] = in_part

    @pl.when(lax.rem(step, 2) != core)
    def _():
        in_send_ref[...] = in_part

    parts_ref[...] = mm(cot_t_ref[...], act_ref[...]).astype(BF).reshape(parts_ref.shape)
    for z in range(owners // 2):
        down_keep_ref[0, z, 0] = parts_ref[2 * z + core]
        down_send_ref[0, z, 0] = parts_ref[2 * z + 1 - core]


def wide_grads(core, hidden_t, cot_t, d_pre, act, groups, owners):
    width, tokens = hidden_t.shape
    wide = act.shape[1]
    lanes, zs = wide // owners, owners // 2
    cols = pl.BlockSpec((tokens, lanes), lambda v, *_: (0, v))
    in_out = pl.BlockSpec((groups, 1, width // groups, lanes), lambda v, *_: (0, v // 2, 0, 0))
    halves = owners // groups
    down_out = pl.BlockSpec((1, zs, 1, width // owners, lanes), lambda v, *_: (v // halves, 0, v % halves, 0, 0))
    in_shape = jax.ShapeDtypeStruct((groups, zs, width // groups, lanes), BF)
    down_shape = jax.ShapeDtypeStruct((groups, zs, halves, width // owners, lanes), BF)
    return pl.pallas_call(
        partial(wide_grads_kernel, groups=groups, owners=owners),
        grid_spec=pltpu.PrefetchScalarGridSpec(
            num_scalar_prefetch=1,
            grid=(owners,),
            in_specs=[whole(hidden_t.shape), whole(cot_t.shape), cols, cols],
            out_specs=[in_out, in_out, down_out, down_out],
            scratch_shapes=[pltpu.VMEM((owners, width // owners, lanes), BF)],
        ),
        out_shape=[in_shape, in_shape, down_shape, down_shape],
        compiler_params=params(),
        cost_estimate=cost(2 * tokens * width * wide, 4 * wide * (tokens + width)),
        name="wide_grads",
    )(core, hidden_t, cot_t, d_pre, act)


def square_grads_kernel(core_ref, left_refs, right_refs, keep_ref, send_ref, parts_ref, *, groups, owners):
    core = core_ref[0]
    for n, (left_ref, right_ref) in enumerate(zip(left_refs, right_refs)):
        parts_ref[n] = mm(left_ref[...], right_ref[...], TN).astype(BF).reshape(parts_ref.shape[1:])
    lanes = right_refs[0].shape[1] // groups
    for z in range(owners // 2):
        for target_ref, v in ((keep_ref, 2 * z + core), (send_ref, 2 * z + 1 - core)):
            first, second = parts_ref[0, v], parts_ref[1, v]
            for d in range(groups):
                cols = slice(d * lanes, (d + 1) * lanes)
                target_ref[d, z] = jnp.concatenate([first[:, cols], second[:, cols]], axis=1)


def square_grads(core, lefts, rights, groups, owners):
    tokens, width = rights[0].shape
    shape = (groups, owners // 2, width // owners, 2 * width // groups)
    full = [whole((tokens, width))] * 2
    return pl.pallas_call(
        partial(square_grads_kernel, groups=groups, owners=owners),
        in_specs=[pl.BlockSpec(memory_space=pltpu.SMEM), [pl.BlockSpec(memory_space=pltpu.VMEM)] * 2, [pl.BlockSpec(memory_space=pltpu.VMEM)] * 2],
        out_shape=[jax.ShapeDtypeStruct(shape, BF)] * 2,
        scratch_shapes=[pltpu.VMEM((2, owners, width // owners, width), BF)],
        compiler_params=params(),
        cost_estimate=cost(2 * tokens * width * width, 12 * tokens * width),
        name="square_grads",
    )(core, lefts, rights)


def rows_kernel(slot_ref, x_ref, d_mid_ref, dq_ref, dk_ref, dv_ref, gain_ref, wq_ref, wk_ref, wv_ref, row_ref, gain_grad_ref, out_refs, total_ref):
    d_hidden = mm(dq_ref[...], wq_ref[...], NT) + mm(dk_ref[...], wk_ref[...], NT) + mm(dv_ref[...], wv_ref[...], NT)
    x = x_ref[...].astype(F32)
    scale = lax.rsqrt(jnp.mean(x * x, axis=1, keepdims=True) + EPS)
    u = d_hidden * gain_ref[...]
    swing = jnp.mean(u * x, axis=1, keepdims=True)
    row = d_mid_ref[...] + scale * u - x * (scale * scale * scale * swing)
    row_ref[...] = row
    at = pl.program_id(0)

    @pl.when(at == 0)
    def _():
        gain_grad_ref[...] = jnp.zeros_like(gain_grad_ref)
        total_ref[...] = jnp.zeros_like(total_ref)

    gain_grad_ref[...] += jnp.sum((d_hidden * x * scale).reshape(-1, 8, x.shape[1]), axis=0)
    slot = slot_ref[...]
    place = lax.broadcasted_iota(jnp.int32, (total_ref.shape[0], slot.shape[1]), 0)
    total_ref[...] += mm((place == slot).astype(F32).astype(BF), row.astype(BF))

    @pl.when(at == pl.num_programs(0) - 1)
    def _():
        start = 0
        for out_ref in out_refs:
            out_ref[...] = total_ref[start : start + out_ref.shape[0], :].astype(BF)
            start += out_ref.shape[0]


def rows_back(slot_row, x, d_mid, dq, dk, dv, gain, w_query, w_key, w_value, owners, cap):
    tokens, width = x.shape
    tile = min(256, tokens)
    rows = pl.BlockSpec((tile, width), lambda t: (t, 0))
    return pl.pallas_call(
        rows_kernel,
        grid=(tokens // tile,),
        in_specs=[pl.BlockSpec((1, tile), lambda t: (0, t))] + [rows] * 5 + [whole(gain.shape)] + [whole(w_query.shape)] * 3,
        out_specs=[rows, pl.BlockSpec((8, width), lambda t: (0, 0)), [whole((cap, width))] * owners],
        out_shape=[
            jax.ShapeDtypeStruct((tokens, width), F32),
            jax.ShapeDtypeStruct((8, width), F32),
            [jax.ShapeDtypeStruct((cap, width), BF)] * owners,
        ],
        scratch_shapes=[pltpu.VMEM((owners * cap, width), F32)],
        compiler_params=params(),
        cost_estimate=cost(tokens * width * (3 * width + owners * cap), 20 * tokens * width),
        name="rows_back",
    )(slot_row, x, d_mid, dq, dk, dv, gain, w_query, w_key, w_value)


def place_kernel(target_refs, rows_refs, out_ref):
    base = pl.program_id(0) * out_ref.shape[0]
    total = None
    for target_ref, rows_ref in zip(target_refs, rows_refs):
        row = lax.broadcasted_iota(jnp.int32, (out_ref.shape[0], rows_ref.shape[0]), 0) + base
        part = mm((row == target_ref[...]).astype(F32).astype(BF), rows_ref[...])
        total = part if total is None else total + part
    out_ref[...] = total


def place_rows(targets, rows, shard):
    width = rows[0].shape[1]
    tile = min(512, shard)
    count = sum(r.shape[0] for r in rows)
    return pl.pallas_call(
        place_kernel,
        grid=(pl.cdiv(shard, tile),),
        in_specs=[[whole(t.shape) for t in targets], [whole(r.shape) for r in rows]],
        out_specs=pl.BlockSpec((tile, width), lambda t: (t, 0)),
        out_shape=jax.ShapeDtypeStruct((shard, width), F32),
        compiler_params=params(),
        cost_estimate=cost(shard * width * count, 4 * shard * width + 2 * count * width),
        name="place_rows",
    )(targets, rows)


def swap(value, axis, bit):
    count = lax.axis_size(axis)
    return lax.ppermute(value, axis, [(i, i ^ bit) for i in range(count)])


def add_low(first, second):
    return (first.astype(F32) + second.astype(F32)).astype(BF)


def pick(blocks, at):
    return lax.dynamic_index_in_dim(blocks, at, 0, keepdims=False)


def exchange(blocks):
    owners = lax.axis_size("vocab")
    if owners <= 8:
        return [blocks[0]] + [swap(blocks[k], "vocab", k) for k in range(1, owners)]
    order = lax.axis_index("vocab") ^ jnp.arange(owners)
    sent = jnp.take(jnp.stack(blocks), order, axis=0)
    came = lax.all_to_all(sent, "vocab", split_axis=0, concat_axis=0, tiled=True)
    return list(jnp.take(came, order, axis=0))


def gather_dp(block):
    half = block.shape[0] // 2
    by_x, by_y = swap(block, "dp", 1), swap(block, "dp", 2)
    far_low = swap(by_x[:half], "dp", 2)
    far_high = swap(by_y[half:], "dp", 1)
    return [block, by_x, by_y, far_low, far_high]


def reduce_shares(keep, came, first, second):
    place = lax.axis_index("dp")
    bit = {1: place % 2, 2: place // 2}
    part = add_low(keep, came)
    part = part.reshape((2, 2) + part.shape[1:])
    if first == 1:
        part = jnp.moveaxis(part, 1, 0)
    part = add_low(pick(part, bit[first]), swap(pick(part, 1 - bit[first]), "dp", first))
    part = add_low(pick(part, bit[second]), swap(pick(part, 1 - bit[second]), "dp", second))
    z = lax.axis_index("vocab") // 2
    total = pick(part, z).astype(F32)
    for k in range(1, lax.axis_size("vocab") // 2):
        total = total + swap(pick(part, z ^ k), "vocab", 2 * k).astype(F32)
    return total


def sum_all(value):
    for axis in ("vocab", "dp"):
        bit = 1
        while bit < lax.axis_size(axis):
            value = value + swap(value, axis, bit)
            bit *= 2
    return value


def spare_slots(token_ids, seq_len, opening, shard, owners, cap, spare):
    tokens = token_ids.shape[0]
    t = jnp.arange(tokens, dtype=jnp.int32)
    within = t % seq_len
    at = jnp.where(within < opening, within, t)
    first = (within >= opening) | (t < seq_len)
    owner = token_ids // shard
    same = (owner[:, None] == owner[None, :]) & first[None, :] & (t[None, :] < at[:, None])
    rank = jnp.sum(same.astype(jnp.int32), axis=1) - cap
    slot = jnp.where(rank >= 0, owner * spare + rank, owners * spare)
    request = jnp.full((owners * spare + 1,), -1, jnp.int32).at[slot].set(token_ids)[:-1]
    asked = lax.all_to_all(request.reshape(owners, spare), "vocab", split_axis=0, concat_axis=0, tiled=True)
    return slot, asked


def body(
    token_ids,
    seq_lengths,
    table,
    gain_one,
    w_query,
    w_key,
    w_value,
    w_out,
    gain_two,
    w_in,
    w_down,
    rel_bias,
    cotangent,
):
    owners, groups = lax.axis_size("vocab"), lax.axis_size("dp")
    me = lax.axis_index("vocab").astype(jnp.int32)
    core = (me % 2).reshape(1)
    shard, width = table.shape
    tokens, seqs = token_ids.shape[0], seq_lengths.shape[0]
    seq_len = tokens // seqs
    heads = rel_bias.shape[1]
    most = 2 * tokens // owners
    opening = most // seqs
    cap = min(most, -(-(9 * most // 16) // 16) * 16)
    spare = most - cap
    lanes = -(-(cap + 1) // LANES) * LANES
    gain_one_row, gain_two_row = gain_one.reshape(1, -1), gain_two.reshape(1, -1)

    slot_row, slot_col, ask = route(token_ids, me.reshape(1), seq_len, opening, shard, owners, cap, lanes)
    asked = lax.all_to_all(ask.reshape(owners, lanes), "vocab", split_axis=0, concat_axis=0, tiled=True)
    asked = jnp.take(asked, me ^ jnp.arange(owners), axis=0)
    by_x = swap(asked, "dp", 1)
    by_y = swap(jnp.stack([asked, by_x]), "dp", 2)
    asked_all = jnp.stack([asked, by_x, by_y[0], by_y[1]])
    overflow = jnp.max(asked_all[:, :, lanes - 1]) > 0 if spare else None
    base = me * shard
    targets = jnp.where(asked_all[:, :, :cap] >= 0, asked_all[:, :, :cap] - base, -1)
    local = jnp.clip(asked[:, :cap] - base, 0, shard - 1)
    picked = [jnp.take(table, local[k], axis=0, mode="clip") for k in range(owners)]
    rows = exchange(picked)

    band = make_band(rel_bias)
    cot_t = cotangent.T

    def project_plain(*rows_in):
        return project(slot_col, list(rows_in), gain_one_row, w_query, w_key, w_value)

    def spare_rows(args):
        return spare_slots(token_ids, seq_len, opening, shard, owners, cap, spare)

    def project_spare(*rows_in):
        slot, asked_more = spare_rows(None)
        found = jnp.take(table, jnp.clip(asked_more - base, 0, shard - 1), axis=0)
        came = lax.all_to_all(found, "vocab", split_axis=0, concat_axis=0, tiled=True).reshape(-1, width)
        more = jnp.take(came, jnp.clip(slot, 0, owners * spare - 1), axis=0)
        more = jnp.where((slot < owners * spare)[:, None], more, jnp.zeros((), BF))
        marked = jnp.where(slot < owners * spare, owners * cap + jnp.arange(tokens, dtype=jnp.int32), slot_col[:, 0])
        return project(marked[:, None], list(rows_in) + [more], gain_one_row, w_query, w_key, w_value)

    if spare:
        x, hidden, q, k, v = lax.cond(overflow, project_spare, project_plain, *rows)
    else:
        x, hidden, q, k, v = project_plain(*rows)

    ctx, probs = attend(q, k, v, seq_lengths, rel_bias, band)
    mixed_out, act, d_pre, hidden_t, d_mid, d_att, d_ctx, gain_two_part = middle_part(
        x, ctx, cotangent, gain_two_row, w_out, w_in, w_down
    )
    packed = owners == 8 and groups == 4 and (width // groups) % 64 == 0 and (w_in.shape[1] // owners) % LANES == 0
    if packed:
        in_keep, in_send, down_keep, down_send = wide_grads(core, hidden_t, cot_t, d_pre, act, groups, owners)
        in_came, down_came = swap(in_send, "vocab", 1), swap(down_send, "vocab", 1)
        in_share = reduce_shares(in_keep, in_came, 1, 2)
        down_share = reduce_shares(down_keep, down_came, 2, 1)

    dq, dk, dv, near, far = attend_back(q, k, v, d_ctx, probs)
    row_grad, gain_one_part, outgoing = rows_back(
        slot_row, x, d_mid, dq, dk, dv, gain_one_row, w_query, w_key, w_value, owners, cap
    )
    arrived = exchange(outgoing)

    if owners == 8:
        batches = [(0, 2), (2, 4), (4, 6), (6, 8)]
    else:
        batches = [(0, owners)]
    placed_targets, placed_rows = [], []
    for low, high in batches:
        parts = gather_dp(jnp.concatenate(arrived[low:high], axis=0))
        wanted = targets[:, low:high].reshape(groups, 1, -1)
        half = wanted.shape[2] // 2
        placed_rows += parts
        placed_targets += [wanted[0], wanted[1], wanted[2], wanted[3][:, :half], wanted[3][:, half:]]

    def place_plain(*args):
        n = len(args) // 2
        return place_rows(list(args[:n]), list(args[n:]), shard)

    def place_spare(*args):
        slot, asked_more = spare_rows(None)
        sent = jnp.zeros((owners * spare + 1, width), F32).at[slot].add(row_grad)[:-1]
        came = lax.all_to_all(
            sent.astype(BF).reshape(owners, spare, width), "vocab", split_axis=0, concat_axis=0, tiled=True
        )
        target = jnp.where(asked_more >= 0, asked_more - base, shard).reshape(-1)
        part = jnp.zeros((shard, width), F32).at[target].add(came.reshape(-1, width).astype(F32), mode="drop")
        return place_plain(*args) + lax.psum(part, "dp")

    if spare:
        table_grad = lax.cond(overflow, place_spare, place_plain, *placed_targets, *placed_rows)
    else:
        table_grad = place_plain(*placed_targets, *placed_rows)

    if packed:
        qk_keep, qk_send = square_grads(core, [dq, dk], [hidden, hidden], groups, owners)
        vo_keep, vo_send = square_grads(core, [dv, d_att], [hidden, ctx], groups, owners)
        qk_share = reduce_shares(qk_keep, swap(qk_send, "vocab", 1), 1, 2)
        vo_share = reduce_shares(vo_keep, swap(vo_send, "vocab", 1), 2, 1)
        part = width // groups
        query_grad, key_grad = qk_share[:, :part].T, qk_share[:, part:].T
        value_grad, out_grad = vo_share[:, :part].T, vo_share[:, part:].T
        in_grad = in_share
        down_grad = jnp.swapaxes(down_share, 1, 2).reshape(-1, width // owners)
    else:
        def spread(left, right):
            full = jnp.einsum("td,te->de", left, right, preferred_element_type=F32)
            part = lax.psum_scatter(full, "vocab", scatter_dimension=1, tiled=True).astype(BF)
            return lax.psum_scatter(part, "dp", scatter_dimension=0, tiled=True).astype(F32)

        query_grad, key_grad, value_grad = spread(hidden, dq), spread(hidden, dk), spread(hidden, dv)
        out_grad = spread(ctx, d_att)
        in_grad = spread(hidden_t.T, d_pre)
        down_grad = spread(act, cotangent)

    buckets = rel_bias.shape[0]
    bias_part = jnp.dot(near, band_onehot(buckets), precision=PRECISE)
    last = buckets // 2 - 1
    bias_part = bias_part.at[:, last].add(far[:, 0]).at[:, 2 * last + 1].add(far[:, 1])
    small = jnp.concatenate(
        [jnp.sum(gain_one_part, axis=0), jnp.sum(gain_two_part, axis=0), bias_part.T.reshape(-1)]
    )
    small = jnp.pad(small, (0, -small.shape[0] % (8 * LANES))).reshape(-1, LANES)
    small = sum_all(small).reshape(-1)
    gain_one_grad, gain_two_grad = small[:width], small[width : 2 * width]
    bias_grad = small[2 * width : 2 * width + buckets * heads].reshape(buckets, heads)
    return (
        mixed_out,
        row_grad,
        table_grad,
        gain_one_grad,
        query_grad,
        key_grad,
        value_grad,
        out_grad,
        gain_two_grad,
        in_grad,
        down_grad,
        bias_grad,
    )


def solution(mesh):
    spread = ("dp", "vocab")
    placed = (
        P(spread),
        P(spread),
        P("vocab", None),
        P(),
        P(),
        P(),
        P(),
        P(),
        P(),
        P(),
        P(),
        P(),
        P(spread, None),
    )
    return jax.shard_map(
        body,
        mesh=mesh,
        in_specs=placed,
        out_specs=(
            P(spread, None),
            P(spread, None),
            P("vocab", None),
            P(),
            P("dp", "vocab"),
            P("dp", "vocab"),
            P("dp", "vocab"),
            P("dp", "vocab"),
            P(),
            P("dp", "vocab"),
            P("dp", "vocab"),
            P(),
        ),
        check_vma=False,
    )
```

```python
from functools import partial

import jax
import jax.numpy as jnp
import numpy as np
from jax import lax
from jax.experimental import pallas as pl
from jax.experimental.pallas import tpu as pltpu
from jax.sharding import PartitionSpec as P

EPS = 1e-06
PRECISE = lax.Precision.HIGHEST
MASKED = -1e30
THRESHOLDS = (12, 16, 23, 32, 46, 64, 91)
LANES = 128
NOWHERE = 1 << 30
BUCKETS = 32
PER_STEP = 2
PER_FETCH = 2
BF = jnp.bfloat16
F32 = jnp.float32
NN = (((1,), (0,)), ((), ()))
NT = (((1,), (1,)), ((), ()))
TN = (((0,), (0,)), ((), ()))


def mm(left, right, dims=NN):
    return lax.dot_general(left, right, dims, preferred_element_type=F32)


def params(mib=56):
    return pltpu.CompilerParams(vmem_limit_bytes=mib << 20)


def cost(macs, moved):
    return pl.CostEstimate(flops=2 * macs, bytes_accessed=moved, transcendentals=0)


def whole(shape):
    return pl.BlockSpec(shape, lambda *_: (0,) * len(shape), pipeline_mode=pl.Buffered(1))


def bucket_of(offset):
    distance = np.abs(offset)
    far = 8 + sum((distance >= t).astype(np.int32) for t in THRESHOLDS)
    return np.where(offset > 0, 16, 0) + np.where(distance < 8, distance, far)


def band_offsets():
    lane = np.arange(4 * LANES)
    return np.where(lane < 3 * LANES, lane, lane - 4 * LANES) - LANES


def band_onehot(buckets):
    return (bucket_of(band_offsets())[:, None] == np.arange(buckets)[None, :]).astype(np.float32)


def route_kernel(me_ref, ids_row_ref, ids_col_ref, slot_row_ref, slot_col_ref, ask_ref, *, seq_len, opening, shard, owners, cap, width):
    me = me_ref[0]
    tokens = ids_row_ref.shape[1]
    ids_row, ids_col = ids_row_ref[...], ids_col_ref[...]
    owner_row, owner_col = jnp.zeros_like(ids_row), jnp.zeros_like(ids_col)
    for o in range(1, owners):
        owner_row += (ids_row >= o * shard).astype(jnp.int32)
        owner_col += (ids_col >= o * shard).astype(jnp.int32)

    def places(shape, axis):
        t = lax.broadcasted_iota(jnp.int32, shape, axis)
        within = lax.rem(t, seq_len)
        repeated = (within < opening) & (t >= seq_len)
        return jnp.where(within < opening, within, t), jnp.logical_not(repeated)

    at_row, first_row = places((1, tokens), 1)
    at_col, first_col = places((tokens, 1), 0)
    key_row, key_col = ids_row * tokens + at_row, ids_col * tokens + at_col
    low_row, low_col = owner_row * (shard * tokens), owner_col * (shard * tokens)
    given_row = jnp.where(first_row, key_row, -1)
    given_col = jnp.where(first_col, key_col, -1)
    rank_col = jnp.sum(((given_row >= low_col) & (given_row < key_col)).astype(jnp.int32), axis=1, keepdims=True)
    rank_row = jnp.sum(((given_col >= low_row) & (given_col < key_row)).astype(jnp.int32), axis=0, keepdims=True)
    slot_row_ref[...] = jnp.where(rank_row < cap, (owner_row ^ me) * cap + rank_row, NOWHERE)
    slot_col_ref[...] = jnp.where(rank_col < cap, (owner_col ^ me) * cap + rank_col, NOWHERE)
    over = (jnp.max(rank_row) >= cap).astype(jnp.int32)
    place_col = jnp.where(first_col & (rank_col < cap), owner_col * width + rank_col, -1)
    step = 4 * LANES
    for start in range(0, owners * width, step):
        lane = lax.broadcasted_iota(jnp.int32, (1, step), 1) + start
        asked = jnp.sum(jnp.where(place_col == lane, ids_col + 1, 0), axis=0, keepdims=True) - 1
        ask_ref[:, start : start + step] = jnp.where(lax.rem(lane, width) == width - 1, over, asked)


def route(token_ids, me, seq_len, opening, shard, owners, cap, width):
    tokens = token_ids.shape[0]
    body = partial(route_kernel, seq_len=seq_len, opening=opening, shard=shard, owners=owners, cap=cap, width=width)
    return pl.pallas_call(
        body,
        in_specs=[pl.BlockSpec(memory_space=pltpu.SMEM), pl.BlockSpec(memory_space=pltpu.VMEM), pl.BlockSpec(memory_space=pltpu.VMEM)],
        out_shape=[
            jax.ShapeDtypeStruct((1, tokens), jnp.int32),
            jax.ShapeDtypeStruct((tokens, 1), jnp.int32),
            jax.ShapeDtypeStruct((1, owners * width), jnp.int32),
        ],
        compiler_params=params(),
        name="route",
    )(me, token_ids.reshape(1, -1), token_ids.reshape(-1, 1))


def windows(lists, tile, shard, window):
    cap = lists.shape[1]
    edges = jnp.arange(pl.cdiv(shard, tile) + 1, dtype=jnp.int32) * tile
    known = jnp.where(lists < 0, NOWHERE, lists)
    below = jnp.sum((known[:, None, :] < edges[None, :, None]).astype(jnp.int32), axis=2)
    starts = jnp.minimum(below[:, :-1] // 16 * 16, cap - window)
    counts = (below[:, 1:] - starts + window - 1) // window
    return starts.T, counts.T, jnp.max(counts, axis=0)


def in_window(start, step, window, cap):
    wanted = start + step * window
    begin = pl.multiple_of(jnp.minimum(wanted, cap - window), 16)
    return begin, begin + lax.broadcasted_iota(jnp.int32, (window, 1), 0) >= wanted


def fetch_kernel(starts_ref, counts_ref, more_ref, list_ref, table_ref, out_refs, total_ref, *, tile, window, shard):
    step_rows, width = table_ref.shape
    blocks = len(out_refs)
    cap = out_refs[0].shape[0]

    @pl.when(pl.program_id(0) == 0)
    def _():
        total_ref[...] = jnp.zeros_like(total_ref)

    for sub in range(step_rows // tile):
        at = pl.program_id(0) * (step_rows // tile) + sub
        row = lax.broadcasted_iota(jnp.int32, (tile, 1), 0) + at * tile
        lane = lax.broadcasted_iota(jnp.int32, (1, tile), 1) + at * tile
        table = table_ref[sub * tile : (sub + 1) * tile, :]
        table = jnp.where(row < shard, table, jnp.zeros((), BF))
        begins = [pl.multiple_of(starts_ref[at, n], 16) for n in range(blocks)]
        wanted = [list_ref[pl.ds(n * cap + begins[n], window), :] for n in range(blocks)]
        found = mm((jnp.concatenate(wanted, axis=0) == lane).astype(F32).astype(BF), table)
        for n in range(blocks):
            total_ref[pl.ds(n * cap + begins[n], window), :] += found[n * window : (n + 1) * window]

        @pl.when(more_ref[at] > 1)
        def _():
            for n in range(blocks):
                def extra(step, carry):
                    begin, fresh = in_window(starts_ref[at, n], step, window, cap)
                    place = pl.ds(n * cap + begin, window)
                    mark = (list_ref[place, :] == lane) & fresh
                    total_ref[place, :] += mm(mark.astype(F32).astype(BF), table)
                    return carry

                lax.fori_loop(1, counts_ref[at, n], extra, 0)

    @pl.when(pl.program_id(0) == pl.num_programs(0) - 1)
    def _():
        for n in range(blocks):
            out_refs[n][...] = total_ref[n * cap : (n + 1) * cap, :].astype(BF)


def fetch_rows(table, lists):
    shard, width = table.shape
    blocks, cap = lists.shape
    tile, window = min(512, shard), min(48, cap)
    starts, counts, more = windows(lists, tile, shard, window)
    tiles = starts.shape[0]
    per_step = PER_FETCH if tiles % PER_FETCH == 0 else 1
    return pl.pallas_call(
        partial(fetch_kernel, tile=tile, window=window, shard=shard),
        grid_spec=pltpu.PrefetchScalarGridSpec(
            num_scalar_prefetch=3,
            grid=(tiles // per_step,),
            in_specs=[whole((blocks * cap, 1)), pl.BlockSpec((per_step * tile, width), lambda t, *_: (t, 0))],
            out_specs=[[whole((cap, width))] * blocks],
            scratch_shapes=[pltpu.VMEM((blocks * cap, width), F32)],
        ),
        out_shape=[[jax.ShapeDtypeStruct((cap, width), BF)] * blocks],
        compiler_params=params(),
        cost_estimate=cost(shard * width * blocks * window, 2 * (shard + blocks * cap) * width),
        name="fetch_rows",
    )(starts, counts, more, lists.reshape(-1, 1), table)[0]


def project_kernel(slot_ref, more_ref, rows_refs, gain_ref, wq_ref, wk_ref, wv_ref, x_ref, hidden_ref, q_ref, k_ref, v_ref):
    slot = slot_ref[...]
    rows = jnp.concatenate([r[...] for r in rows_refs], axis=0)
    lane = lax.broadcasted_iota(jnp.int32, (slot.shape[0], rows.shape[0]), 1)
    x = mm((lane == slot).astype(F32).astype(BF), rows)
    if more_ref is not None:
        x = x + more_ref[...].astype(F32)
    x_ref[...] = x.astype(BF)
    scale = lax.rsqrt(jnp.mean(x * x, axis=1, keepdims=True) + EPS)
    hidden = (x * scale * gain_ref[...]).astype(BF)
    hidden_ref[...] = hidden
    q_ref[...] = mm(hidden, wq_ref[...]).astype(BF)
    k_ref[...] = mm(hidden, wk_ref[...]).astype(BF)
    v_ref[...] = mm(hidden, wv_ref[...]).astype(BF)


def project(slot_col, more, rows, gain, w_query, w_key, w_value):
    tokens, width = slot_col.shape[0], gain.shape[1]
    tile = min(256, tokens)
    out = pl.BlockSpec((tile, width), lambda t: (t, 0))
    count = sum(r.shape[0] for r in rows)
    return pl.pallas_call(
        project_kernel,
        grid=(tokens // tile,),
        in_specs=[pl.BlockSpec((tile, 1), lambda t: (t, 0)), None if more is None else out, [whole(r.shape) for r in rows], whole(gain.shape)]
        + [whole(w_query.shape)] * 3,
        out_specs=[out] * 5,
        out_shape=[jax.ShapeDtypeStruct((tokens, width), BF)] * 5,
        compiler_params=params(),
        cost_estimate=cost(tokens * width * (3 * width + count), 14 * tokens * width),
        name="project",
    )(slot_col, more, rows, gain, w_query, w_key, w_value)


def band_kernel(line_ref, band_ref):
    line = jnp.broadcast_to(line_ref[0], (LANES, line_ref.shape[2]))
    band_ref[0] = pltpu.roll(line, 0, 1, stride=1, stride_axis=0)[:, : 3 * LANES]


def make_band(rel_bias):
    heads = rel_bias.shape[1]
    line = jnp.dot(band_onehot(rel_bias.shape[0]), rel_bias, precision=PRECISE).T.reshape(heads, 1, -1)
    return pl.pallas_call(
        band_kernel,
        grid=(heads,),
        in_specs=[pl.BlockSpec((1,) + line.shape[1:], lambda h: (h, 0, 0))],
        out_specs=pl.BlockSpec((1, LANES, 3 * LANES), lambda h: (h, 0, 0)),
        out_shape=jax.ShapeDtypeStruct((heads, LANES, 3 * LANES), F32),
        compiler_params=params(30),
        name="band",
    )(line)


def attend_kernel(len_ref, far_ref, q_ref, k_ref, v_ref, band_ref, ctx_ref, p_ref):
    pair = pl.program_id(1)
    q, k, v = q_ref[...], k_ref[...], v_ref[...]
    seq_len = q.shape[0]
    blocks = seq_len // LANES
    last = far_ref.shape[0] // 2 - 1
    half = lax.broadcasted_iota(jnp.int32, (1, LANES), 1) // (LANES // 2)
    key_at = lax.broadcasted_iota(jnp.int32, (1, seq_len), 1)
    mask = jnp.where(key_at < len_ref[pl.program_id(0)], 0.0, MASKED)
    none = jnp.zeros((), BF)
    ctx = jnp.zeros((seq_len, LANES), F32)
    for h in range(2):
        k_own, v_own = jnp.where(half == h, k, none), jnp.where(half == h, v, none)
        left, right = far_ref[last, 2 * pair + h], far_ref[2 * last + 1, 2 * pair + h]
        for i in range(blocks):
            raw = mm(q[i * LANES : (i + 1) * LANES], k_own, NT)
            tiles = []
            for j in range(blocks):
                cols = slice(j * LANES, (j + 1) * LANES)
                d = j - i
                if abs(d) <= 1:
                    tiles.append(raw[:, cols] + band_ref[h, :, (d + 1) * LANES : (d + 2) * LANES] + mask[:, cols])
                else:
                    tiles.append(raw[:, cols] + (mask[:, cols] + (left if d < 0 else right)))
            scores = jnp.concatenate(tiles, axis=1)
            grown = jnp.exp(scores - jnp.max(scores, axis=1, keepdims=True))
            total = jnp.sum(grown, axis=1, keepdims=True)
            p_ref[0, h, i * LANES : (i + 1) * LANES, :] = (grown * (1.0 / total)).astype(BF)
        ctx = ctx + mm(p_ref[0, h], v_own)
    ctx_ref[...] = ctx.astype(BF)


def attend(q, k, v, lengths, rel_bias, band):
    seqs, heads = lengths.shape[0], rel_bias.shape[1]
    tokens, width = q.shape
    seq_len = tokens // seqs
    block = pl.BlockSpec((seq_len, LANES), lambda s, p, *_: (s, p))
    return pl.pallas_call(
        attend_kernel,
        grid_spec=pltpu.PrefetchScalarGridSpec(
            num_scalar_prefetch=2,
            grid=(seqs, heads // 2),
            in_specs=[block] * 3 + [pl.BlockSpec((2,) + band.shape[1:], lambda s, p, *_: (p, 0, 0))],
            out_specs=[block, pl.BlockSpec((1, 2, seq_len, seq_len), lambda s, p, *_: (s, p, 0, 0))],
        ),
        out_shape=[
            jax.ShapeDtypeStruct((tokens, width), BF),
            jax.ShapeDtypeStruct((seqs, heads, seq_len, seq_len), BF),
        ],
        compiler_params=params(),
        cost_estimate=cost(tokens * seq_len * width * 8, 2 * tokens * seq_len * heads),
        name="attend",
    )(lengths, rel_bias, q, k, v, band)


def attend_back_kernel(q_ref, k_ref, v_ref, do_ref, p_ref, dq_ref, dk_ref, dv_ref, line_ref, ds_ref, band_ref, far_ref):
    seq_at = pl.program_id(1)
    q, k, v, do = q_ref[...], k_ref[...], v_ref[...], do_ref[...]
    seq_len = q.shape[0]
    blocks = seq_len // LANES
    half = lax.broadcasted_iota(jnp.int32, (1, LANES), 1) // (LANES // 2)
    none = jnp.zeros((), BF)

    @pl.when(seq_at == 0)
    def _():
        band_ref[...] = jnp.zeros_like(band_ref)
        far_ref[...] = jnp.zeros_like(far_ref)

    dq = dk = dv = jnp.zeros((seq_len, LANES), F32)
    for h in range(2):
        k_own, v_own = jnp.where(half == h, k, none), jnp.where(half == h, v, none)
        q_own, do_own = jnp.where(half == h, q, none), jnp.where(half == h, do, none)
        near = [jnp.zeros((LANES, LANES), F32) for _ in range(3)]
        far = [jnp.zeros((8, LANES), F32) for _ in range(2)]
        for i in range(blocks):
            rows = slice(i * LANES, (i + 1) * LANES)
            probs = p_ref[0, h, rows, :].astype(F32)
            weighed = probs * mm(do[rows], v_own, NT)
            ds = weighed - probs * jnp.sum(weighed, axis=1, keepdims=True)
            for j in range(blocks):
                d = j - i
                tile = ds[:, j * LANES : (j + 1) * LANES]
                if abs(d) <= 1:
                    near[d + 1] = near[d + 1] + tile
                else:
                    side = 0 if d < 0 else 1
                    far[side] = far[side] + jnp.sum(tile.reshape(LANES // 8, 8, LANES), axis=0)
            ds_ref[rows, :] = ds.astype(BF)
        for d in range(3):
            band_ref[h, :, d * LANES : (d + 1) * LANES] += near[d]
        for side in range(2):
            far_ref[h, :, side * LANES : (side + 1) * LANES] += far[side]
        d_low = ds_ref[...]
        dk = dk + mm(d_low, q_own, TN)
        dv = dv + mm(p_ref[0, h], do_own, TN)
        dq = dq + mm(d_low, k_own)
    dq_ref[...], dk_ref[...], dv_ref[...] = dq.astype(BF), dk.astype(BF), dv.astype(BF)

    @pl.when(seq_at == pl.num_programs(1) - 1)
    def _():
        row = lax.broadcasted_iota(jnp.int32, (8, 1), 0)
        for h in range(2):
            padded = jnp.concatenate([band_ref[h], jnp.zeros((LANES, LANES), F32)], axis=1)
            turned = padded[:8]
            for start in range(8, LANES, 8):
                turned = turned + pltpu.roll(padded[start : start + 8], 4 * LANES - start, 1)
            for bit in (1, 2, 4):
                turned = jnp.where(row & bit > 0, pltpu.roll(turned, 4 * LANES - bit, 1), turned)
            line_ref[0, h : h + 1, :] = jnp.sum(turned, axis=0, keepdims=True)
            line_ref[0, 2 + h : 3 + h, : 2 * LANES] = jnp.sum(far_ref[h], axis=0, keepdims=True)


def attend_back(q, k, v, d_context, probs):
    seqs, heads, seq_len, _ = probs.shape
    tokens, width = q.shape
    pairs = heads // 2
    block = pl.BlockSpec((seq_len, LANES), lambda p, s: (s, p))
    return pl.pallas_call(
        attend_back_kernel,
        grid=(pairs, seqs),
        in_specs=[block] * 4 + [pl.BlockSpec((1, 2, seq_len, seq_len), lambda p, s: (s, p, 0, 0))],
        out_specs=[block] * 3 + [pl.BlockSpec((1, 8, 4 * LANES), lambda p, s: (p, 0, 0))],
        out_shape=[jax.ShapeDtypeStruct((tokens, width), BF)] * 3
        + [jax.ShapeDtypeStruct((heads // 2, 8, 4 * LANES), F32)],
        scratch_shapes=[
            pltpu.VMEM((seq_len, seq_len), BF),
            pltpu.VMEM((2, LANES, 3 * LANES), F32),
            pltpu.VMEM((2, 8, 2 * LANES), F32),
        ],
        compiler_params=params(),
        cost_estimate=cost(tokens * seq_len * width * 12, 2 * tokens * seq_len * heads),
        name="attend_back",
    )(q, k, v, d_context, probs)


def read_lines(lines):
    heads = 2 * lines.shape[0]
    near = lines[:, 0:2, :].reshape(heads, -1)
    far = jnp.sum(lines[:, 2:4, : 2 * LANES].reshape(heads, 2, LANES), axis=2)
    return near, far


def middle_kernel(x_ref, ctx_ref, cot_ref, gain_ref, w_out_ref, w_in_ref, w_down_ref, mixed_ref, act_ref, d_pre_ref, hidden_t_ref, d_mid_ref, d_att_ref, d_ctx_ref, gain_grad_ref, *, chunk):
    mid = x_ref[...].astype(F32) + mm(ctx_ref[...], w_out_ref[...])
    gain = gain_ref[...]
    scale = lax.rsqrt(jnp.mean(mid * mid, axis=1, keepdims=True) + EPS)
    hidden_full = mid * scale * gain
    hidden = hidden_full.astype(BF)
    hidden_t_ref[...] = hidden_full.T.astype(BF)
    cot = cot_ref[...]
    mixed, d_hidden = mid, jnp.zeros_like(mid)
    slope = float(np.sqrt(2 / np.pi))
    for start in range(0, w_in_ref.shape[1], chunk):
        cols = slice(start, start + chunk)
        pre = mm(hidden, w_in_ref[:, cols])
        d_act = mm(cot, w_down_ref[cols, :], NT)
        square = pre * pre
        bent = jnp.tanh(slope * pre * (1.0 + 0.044715 * square))
        open_half = 0.5 + 0.5 * bent
        act = (pre * open_half).astype(BF)
        curve = (0.5 * slope) * pre * (1.0 - bent * bent) * (1.0 + (3 * 0.044715) * square)
        d_pre = (d_act * (open_half + curve)).astype(BF)
        act_ref[:, cols] = act
        d_pre_ref[:, cols] = d_pre
        mixed = mixed + mm(act, w_down_ref[cols, :])
        d_hidden = d_hidden + mm(d_pre, w_in_ref[:, cols], NT)
    mixed_ref[...] = mixed.astype(BF)
    u = d_hidden * gain
    swing = jnp.mean(u * mid, axis=1, keepdims=True)
    d_mid = cot.astype(F32) + scale * u - mid * (scale * scale * scale * swing)
    d_mid_ref[...] = d_mid
    d_att = d_mid.astype(BF)
    d_att_ref[...] = d_att
    d_ctx_ref[...] = mm(d_att, w_out_ref[...], NT).astype(BF)

    @pl.when(pl.program_id(0) == 0)
    def _():
        gain_grad_ref[...] = jnp.zeros_like(gain_grad_ref)

    gain_grad_ref[...] += jnp.sum((d_hidden * mid * scale).reshape(-1, 8, mid.shape[1]), axis=0)


def middle_part(x, ctx, cot, gain, w_out, w_in, w_down):
    tokens, width = x.shape
    wide = w_in.shape[1]
    tile = min(256, tokens)
    rows = pl.BlockSpec((tile, width), lambda t: (t, 0))
    wide_rows = pl.BlockSpec((tile, wide), lambda t: (t, 0))
    return pl.pallas_call(
        partial(middle_kernel, chunk=min(768, wide)),
        grid=(tokens // tile,),
        in_specs=[rows] * 3 + [whole(a.shape) for a in (gain, w_out, w_in, w_down)],
        out_specs=[rows, wide_rows, wide_rows, pl.BlockSpec((width, tile), lambda t: (0, t)), rows, rows, rows]
        + [pl.BlockSpec((8, width), lambda t: (0, 0))],
        out_shape=[
            jax.ShapeDtypeStruct((tokens, width), BF),
            jax.ShapeDtypeStruct((tokens, wide), BF),
            jax.ShapeDtypeStruct((tokens, wide), BF),
            jax.ShapeDtypeStruct((width, tokens), BF),
            jax.ShapeDtypeStruct((tokens, width), F32),
            jax.ShapeDtypeStruct((tokens, width), BF),
            jax.ShapeDtypeStruct((tokens, width), BF),
            jax.ShapeDtypeStruct((8, width), F32),
        ],
        compiler_params=params(),
        cost_estimate=cost(tokens * width * (4 * wide + 2 * width), 4 * width * wide + 8 * tokens * (wide + width)),
        name="middle",
    )(x, ctx, cot, gain, w_out, w_in, w_down)


def in_grads_kernel(core_ref, hidden_t_ref, d_pre_ref, keep_ref, send_ref):
    part = mm(hidden_t_ref[...], d_pre_ref[...]).astype(BF).reshape(keep_ref.shape)
    own = lax.rem(pl.program_id(0), 2) == core_ref[0]

    @pl.when(own)
    def _():
        keep_ref[...] = part

    @pl.when(jnp.logical_not(own))
    def _():
        send_ref[...] = part


def in_grads(core, hidden_t, d_pre, groups, owners):
    width, tokens = hidden_t.shape
    wide = d_pre.shape[1]
    lanes = wide // owners
    out = pl.BlockSpec((groups, 1, width // groups, lanes), lambda v, *_: (0, v // 2, 0, 0))
    return pl.pallas_call(
        in_grads_kernel,
        grid_spec=pltpu.PrefetchScalarGridSpec(
            num_scalar_prefetch=1,
            grid=(owners,),
            in_specs=[whole(hidden_t.shape), pl.BlockSpec((tokens, lanes), lambda v, *_: (0, v))],
            out_specs=[out, out],
        ),
        out_shape=[jax.ShapeDtypeStruct((groups, owners // 2, width // groups, lanes), BF)] * 2,
        compiler_params=params(),
        cost_estimate=cost(tokens * width * wide, 2 * wide * (tokens + width)),
        name="in_grads",
    )(core, hidden_t, d_pre)


def down_grads_kernel(core_ref, cot_t_ref, act_ref, keep_ref, send_ref, parts_ref):
    core = core_ref[0]
    parts_ref[...] = mm(cot_t_ref[...], act_ref[...]).astype(BF).reshape(parts_ref.shape)
    for z in range(parts_ref.shape[0] // 2):
        keep_ref[0, z, 0] = parts_ref[2 * z + core]
        send_ref[0, z, 0] = parts_ref[2 * z + 1 - core]


def down_grads(core, cot_t, act, groups, owners):
    width, tokens = cot_t.shape
    wide = act.shape[1]
    lanes, zs = wide // owners, owners // 2
    halves = owners // groups
    out = pl.BlockSpec((1, zs, 1, width // owners, lanes), lambda v, *_: (v // halves, 0, v % halves, 0, 0))
    return pl.pallas_call(
        down_grads_kernel,
        grid_spec=pltpu.PrefetchScalarGridSpec(
            num_scalar_prefetch=1,
            grid=(owners,),
            in_specs=[whole(cot_t.shape), pl.BlockSpec((tokens, lanes), lambda v, *_: (0, v))],
            out_specs=[out, out],
            scratch_shapes=[pltpu.VMEM((owners, width // owners, lanes), BF)],
        ),
        out_shape=[jax.ShapeDtypeStruct((groups, zs, halves, width // owners, lanes), BF)] * 2,
        compiler_params=params(),
        cost_estimate=cost(tokens * width * wide, 2 * wide * (tokens + width)),
        name="down_grads",
    )(core, cot_t, act)


def square_kernel(left_ref, right_ref, out_ref):
    out_ref[...] = mm(left_ref[...], right_ref[...], TN).astype(BF).reshape(out_ref.shape)


def square_part(left, right, owners):
    tokens, width = left.shape
    return pl.pallas_call(
        square_kernel,
        out_shape=jax.ShapeDtypeStruct((owners, width // owners, right.shape[1]), BF),
        compiler_params=params(30),
        cost_estimate=cost(tokens * width * width, 6 * tokens * width),
        name="square_part",
    )(left, right)


def square_grads_kernel(core_ref, left_refs, right_refs, ready_ref, keep_ref, send_ref, parts_ref, *, groups, owners):
    core = core_ref[0]
    for n, (left_ref, right_ref) in enumerate(zip(left_refs, right_refs)):
        parts_ref[n] = mm(left_ref[...], right_ref[...], TN).astype(BF).reshape(parts_ref.shape[1:])
    lanes = right_refs[0].shape[1] // groups
    for z in range(owners // 2):
        for target_ref, v in ((keep_ref, 2 * z + core), (send_ref, 2 * z + 1 - core)):
            first, second = parts_ref[0, v], parts_ref[1, v] if ready_ref is None else ready_ref[v]
            for d in range(groups):
                cols = slice(d * lanes, (d + 1) * lanes)
                target_ref[d, z] = jnp.concatenate([first[:, cols], second[:, cols]], axis=1)


def square_grads(core, lefts, rights, ready, groups, owners):
    tokens, width = rights[0].shape
    shape = (groups, owners // 2, width // owners, 2 * width // groups)
    vmem = pl.BlockSpec(memory_space=pltpu.VMEM)
    return pl.pallas_call(
        partial(square_grads_kernel, groups=groups, owners=owners),
        in_specs=[pl.BlockSpec(memory_space=pltpu.SMEM), [vmem] * len(lefts), [vmem] * len(lefts)]
        + [None if ready is None else vmem],
        out_shape=[jax.ShapeDtypeStruct(shape, BF)] * 2,
        scratch_shapes=[pltpu.VMEM((len(lefts), owners, width // owners, width), BF)],
        compiler_params=params(30),
        cost_estimate=cost(len(lefts) * tokens * width * width, 12 * tokens * width),
        name="square_grads",
    )(core, lefts, rights, ready)


SMALL = 16


def low_parts(value):
    high = value.astype(BF)
    return jnp.concatenate([high, (value - high.astype(F32)).astype(BF)], axis=0)


def whole_value(parts):
    return parts[:SMALL].astype(F32) + parts[SMALL:].astype(F32)


def small_rows(lines_ref, onehot_ref, gain_one_part, gain_two_part, width):
    pairs = lines_ref.shape[0]
    last = onehot_ref.shape[1]
    near = jnp.concatenate([lines_ref[p, 0:2, :] for p in range(pairs)], axis=0)
    far = jnp.concatenate([lines_ref[p, 2:4, : 2 * LANES] for p in range(pairs)], axis=0)
    bias = lax.dot_general(near, onehot_ref[...], NN, precision=PRECISE, preferred_element_type=F32)
    lane = lax.broadcasted_iota(jnp.int32, (1, last), 1)
    left = jnp.sum(far[:, :LANES], axis=1, keepdims=True)
    right = jnp.sum(far[:, LANES:], axis=1, keepdims=True)
    bias = bias + jnp.where(lane == BUCKETS // 2 - 1, left, 0.0) + jnp.where(lane == BUCKETS - 1, right, 0.0)
    bias = jnp.concatenate([bias, jnp.zeros((2 * pairs, width - last), F32)], axis=1)
    gains = [jnp.sum(g, axis=0, keepdims=True) for g in (gain_one_part, gain_two_part)]
    spare = jnp.zeros((SMALL - 2 - 2 * pairs, width), F32)
    return jnp.concatenate(gains + [bias, spare], axis=0)


def rows_kernel(slot_ref, x_ref, d_mid_ref, dq_ref, dk_ref, dv_ref, gain_ref, wq_ref, wk_ref, wv_ref, lines_ref, onehot_ref, gain_two_ref, row_ref, even_refs, odd_ref, held_ref, gain_grad_ref):
    d_hidden = mm(dq_ref[...], wq_ref[...], NT) + mm(dk_ref[...], wk_ref[...], NT) + mm(dv_ref[...], wv_ref[...], NT)
    x = x_ref[...].astype(F32)
    scale = lax.rsqrt(jnp.mean(x * x, axis=1, keepdims=True) + EPS)
    u = d_hidden * gain_ref[...]
    swing = jnp.mean(u * x, axis=1, keepdims=True)
    row = d_mid_ref[...] + scale * u - x * (scale * scale * scale * swing)
    row_ref[...] = row
    at = pl.program_id(0)

    @pl.when(at == 0)
    def _():
        gain_grad_ref[...] = jnp.zeros_like(gain_grad_ref)

    gain_grad_ref[...] += jnp.sum((d_hidden * x * scale).reshape(-1, 8, x.shape[1]), axis=0)
    tile = row.shape[0]
    held_ref[pl.ds(pl.multiple_of(at * tile, tile), tile), :] = row.astype(BF)

    @pl.when(at == pl.num_programs(0) - 1)
    def _():
        slot, held = slot_ref[...], held_ref[...]
        cap, evens = even_refs[0].shape[0], len(even_refs)
        order = [2 * n for n in range(evens)] + [2 * n + 1 for n in range(evens)]
        line = lax.broadcasted_iota(jnp.int32, (cap, slot.shape[1]), 0)
        together = min(len(order), 8)
        for low in range(0, len(order), together):
            places = jnp.concatenate([line + k * cap for k in order[low : low + together]], axis=0)
            sent = mm((places == slot).astype(F32).astype(BF), held).astype(BF)
            for n in range(together):
                part, at_n = sent[n * cap : (n + 1) * cap], low + n
                if at_n < evens:
                    even_refs[at_n][...] = part
                else:
                    odd_ref[(at_n - evens) * cap : (at_n - evens + 1) * cap, :] = part
        small = small_rows(lines_ref, onehot_ref, gain_grad_ref[...], gain_two_ref[...], row.shape[1])
        odd_ref[evens * cap :, :] = low_parts(small)


def rows_back(slot_row, x, d_mid, dq, dk, dv, gain, w_query, w_key, w_value, lines, gain_two_part, owners, cap):
    tokens, width = x.shape
    onehot = jnp.asarray(band_onehot(LANES))
    half = owners // 2
    tile = min(256, tokens)
    rows = pl.BlockSpec((tile, width), lambda t: (t, 0))
    return pl.pallas_call(
        rows_kernel,
        grid=(tokens // tile,),
        in_specs=[whole(slot_row.shape)] + [rows] * 5 + [whole(gain.shape)] + [whole(w_query.shape)] * 3
        + [whole(a.shape) for a in (lines, onehot, gain_two_part)],
        out_specs=[rows, [whole((cap, width))] * half, whole((half * cap + 2 * SMALL, width))],
        out_shape=[
            jax.ShapeDtypeStruct((tokens, width), F32),
            [jax.ShapeDtypeStruct((cap, width), BF)] * half,
            jax.ShapeDtypeStruct((half * cap + 2 * SMALL, width), BF),
        ],
        scratch_shapes=[pltpu.VMEM((tokens, width), BF), pltpu.VMEM((8, width), F32)],
        compiler_params=params(),
        cost_estimate=cost(tokens * width * (3 * width + owners * cap), 20 * tokens * width),
        name="rows_back",
    )(slot_row, x, d_mid, dq, dk, dv, gain, w_query, w_key, w_value, lines, onehot, gain_two_part)


def plan_kernel(starts_ref, list_ref, plan_ref, *, blocks, window):
    at = pl.program_id(0)
    cap = list_ref.shape[0] // blocks
    wanted = [list_ref[pl.ds(n * cap + pl.multiple_of(starts_ref[at, n], 16), window), :] for n in range(blocks)]
    wanted = jnp.concatenate(wanted, axis=0)
    for low in range(0, wanted.shape[0], LANES):
        part = jnp.broadcast_to(wanted[low : low + LANES], (min(LANES, wanted.shape[0] - low), LANES))
        plan_ref[0, :, low : low + LANES] = part.T[:1]


def place_plan(lists, shard):
    blocks, cap = lists.shape
    tile, window = min(256, shard), min(32, cap)
    starts, counts, more = windows(lists, tile, shard, window)
    tiles = pl.cdiv(shard, tile)
    column = lists.reshape(-1, 1)
    plan = pl.pallas_call(
        partial(plan_kernel, blocks=blocks, window=window),
        grid_spec=pltpu.PrefetchScalarGridSpec(
            num_scalar_prefetch=1,
            grid=(tiles,),
            in_specs=[whole(column.shape)],
            out_specs=pl.BlockSpec((1, 1, blocks * window), lambda t, *_: (t, 0, 0)),
        ),
        out_shape=jax.ShapeDtypeStruct((tiles, 1, blocks * window), jnp.int32),
        compiler_params=params(30),
        name="place_plan",
    )(starts, column)
    return starts, counts, more, plan, column


def place_kernel(starts_ref, counts_ref, more_ref, plan_ref, list_ref, rows_refs, out_ref, list_held, list_sem, *, tile, window, cap):
    per_step = plan_ref.shape[0]
    places = [(ref, low) for ref in rows_refs for low in range(0, ref.shape[0] // cap * cap, cap)]
    for sub in range(per_step):
        at = pl.program_id(0) * per_step + sub
        out_rows = slice(sub * tile, (sub + 1) * tile)
        row = lax.broadcasted_iota(jnp.int32, (tile, 1), 0) + at * tile
        held = []
        for n, (rows_ref, low) in enumerate(places):
            held.append(rows_ref[pl.ds(low + pl.multiple_of(starts_ref[at, n], 16), window), :])
        out_ref[out_rows, :] = mm((row == plan_ref[sub]).astype(F32).astype(BF), jnp.concatenate(held, axis=0))

    for sub in range(per_step):
        at = pl.program_id(0) * per_step + sub
        out_rows = slice(sub * tile, (sub + 1) * tile)

        @pl.when(more_ref[at] > 1)
        def _():
            copy = pltpu.make_async_copy(list_ref, list_held, list_sem)
            copy.start()
            copy.wait()
            lane = lax.broadcasted_iota(jnp.int32, (1, tile), 1) + at * tile
            for n, (rows_ref, low) in enumerate(places):
                def extra(step, carry):
                    begin, fresh = in_window(starts_ref[at, n], step, window, cap)
                    own = (list_held[pl.ds(n * cap + begin, window), :] == lane) & fresh
                    rows = rows_ref[pl.ds(low + begin, window), :]
                    out_ref[out_rows, :] += mm(own.astype(F32).astype(BF), rows, TN)
                    return carry

                lax.fori_loop(1, counts_ref[at, n], extra, 0)


def place_rows(plan, rows, shard, cap):
    width = rows[0].shape[1]
    starts, counts, more, lanes, column = plan
    tile, window = min(256, shard), min(32, cap)
    per_step = PER_STEP if starts.shape[0] % PER_STEP == 0 else 1
    return pl.pallas_call(
        partial(place_kernel, tile=tile, window=window, cap=cap),
        grid_spec=pltpu.PrefetchScalarGridSpec(
            num_scalar_prefetch=3,
            grid=(starts.shape[0] // per_step,),
            in_specs=[
                pl.BlockSpec((per_step, 1, lanes.shape[2]), lambda t, *_: (t, 0, 0)),
                pl.BlockSpec(memory_space=pl.ANY),
                [whole(r.shape) for r in rows],
            ],
            out_specs=pl.BlockSpec((per_step * tile, width), lambda t, *_: (t, 0)),
            scratch_shapes=[pltpu.VMEM(column.shape, jnp.int32), pltpu.SemaphoreType.DMA],
        ),
        out_shape=jax.ShapeDtypeStruct((shard, width), F32),
        compiler_params=params(30),
        cost_estimate=cost(shard * width * lanes.shape[2], 4 * shard * width + 2 * column.shape[0] * width),
        name="place_rows",
    )(starts, counts, more, lanes, column, rows)


def pair_kernel(even_refs, own_ref, came_ref, out_refs, small_ref):
    cap = even_refs[0].shape[0]
    rows = len(even_refs) * cap
    small = whole_value(own_ref[rows:, :]) + whole_value(came_ref[rows:, :])
    small_ref[...] = small
    for n, out_ref in enumerate(out_refs):
        out_ref[:cap, :] = even_refs[n][...]
        out_ref[cap : 2 * cap, :] = came_ref[n * cap : (n + 1) * cap, :]
        if n > 0:
            out_ref[2 * cap :, :] = low_parts(small)


def pair_blocks(evens, own, came):
    cap, width = evens[0].shape
    shapes = [(2 * cap, width)] + [(2 * cap + 2 * SMALL, width)] * (len(evens) - 1)
    return pl.pallas_call(
        pair_kernel,
        out_shape=[[jax.ShapeDtypeStruct(shape, BF) for shape in shapes], jax.ShapeDtypeStruct((SMALL, width), F32)],
        compiler_params=params(),
        cost_estimate=cost(1, 1),
        name="pair_blocks",
    )(evens, own, came)


def swap(value, axis, bit):
    count = lax.axis_size(axis)
    return lax.ppermute(value, axis, [(i, i ^ bit) for i in range(count)])


def arrival_order(owners):
    if owners != 8:
        return [(n, 0, owners) for n in range(4)]
    order = [(n, low, high) for low, high in ((0, 2), (2, 6), (6, 8)) for n in range(3)]
    return order + [(3, 0, 1), (3, 2, 4), (3, 1, 2), (3, 4, 6), (3, 6, 7), (3, 7, 8)]


def add_low(first, second):
    return (first.astype(F32) + second.astype(F32)).astype(BF)


def pick(blocks, at):
    return lax.dynamic_index_in_dim(blocks, at, 0, keepdims=False)


def exchange(blocks):
    owners = lax.axis_size("vocab")
    if owners <= 8:
        return [blocks[0]] + [swap(blocks[k], "vocab", k) for k in range(1, owners)]
    order = lax.axis_index("vocab") ^ jnp.arange(owners)
    sent = jnp.take(jnp.stack(blocks), order, axis=0)
    came = lax.all_to_all(sent, "vocab", split_axis=0, concat_axis=0, tiled=True)
    return list(jnp.take(came, order, axis=0))


def around(block):
    return swap(block, "dp", 1), swap(block, "dp", 2)


def across(block, by_x, by_y):
    half = block.shape[0] // 2
    return [block, by_x, by_y, swap(by_x[:half], "dp", 2), swap(by_y[half:], "dp", 1)]


def halve(keep, came, at, axis=0):
    if axis == 1:
        keep, came = (jnp.moveaxis(a, 1, 0) for a in (keep, came))
    other = add_low(pick(keep, 1 - at), pick(came, 1 - at))
    return other, add_low(pick(keep, at), pick(came, at))


def with_small(rows, small):
    high = lax.reduce_precision(small, 8, 7)
    low = lax.reduce_precision(small - high, 8, 7)
    return jnp.concatenate([rows, high.astype(BF), low.astype(BF)], axis=0), high + low


def by_bits(shares):
    return shares.reshape((2, 2) + shares.shape[1:])


def after(value, *others):
    if isinstance(value, (list, tuple)):
        return list(lax.optimization_barrier(tuple(value) + others)[: len(value)])
    return lax.optimization_barrier((value,) + others)[0]


def finish_kernel(keep_ref, came_ref, in_ref, down_ref, q_ref, k_ref, v_ref, o_ref):
    total = keep_ref[...].astype(F32) + came_ref[...].astype(F32)
    in_ref[...] = total[: in_ref.shape[0]]
    rows, lanes, low = down_ref.shape[1], total.shape[1], in_ref.shape[0]
    for n in range(down_ref.shape[0] // lanes):
        down_ref[n * lanes : (n + 1) * lanes, :] = total[low : low + rows].T
        low += rows
    for first_ref, second_ref in ((q_ref, k_ref), (v_ref, o_ref)):
        turned = total[low : low + rows].T
        first_ref[...] = turned[: q_ref.shape[0]]
        second_ref[...] = turned[q_ref.shape[0] :]
        low += rows


def finish(keep, came, in_rows, rows):
    lanes = keep.shape[1]
    square = jax.ShapeDtypeStruct((lanes // 2, rows), F32)
    wide = (keep.shape[0] - in_rows) // rows - 2
    return pl.pallas_call(
        finish_kernel,
        out_shape=[jax.ShapeDtypeStruct((in_rows, lanes), F32), jax.ShapeDtypeStruct((wide * lanes, rows), F32)]
        + [square] * 4,
        compiler_params=params(24),
        name="finish",
    )(keep, came)


def spare_slots(token_ids, seq_len, opening, shard, owners, cap, spare):
    tokens = token_ids.shape[0]
    t = jnp.arange(tokens, dtype=jnp.int32)
    within = t % seq_len
    at = jnp.where(within < opening, within, t)
    first = (within >= opening) | (t < seq_len)
    owner = token_ids // shard
    key = token_ids * tokens + at
    same = (owner[:, None] == owner[None, :]) & first[None, :] & (key[None, :] < key[:, None])
    rank = jnp.sum(same.astype(jnp.int32), axis=1) - cap
    slot = jnp.where(rank >= 0, owner * spare + rank, owners * spare)
    request = jnp.full((owners * spare + 1,), -1, jnp.int32).at[slot].set(token_ids)[:-1]
    asked = lax.all_to_all(request.reshape(owners, spare), "vocab", split_axis=0, concat_axis=0, tiled=True)
    return slot, asked


def body(
    token_ids,
    seq_lengths,
    table,
    gain_one,
    w_query,
    w_key,
    w_value,
    w_out,
    gain_two,
    w_in,
    w_down,
    rel_bias,
    cotangent,
):
    owners, groups = lax.axis_size("vocab"), lax.axis_size("dp")
    me = lax.axis_index("vocab").astype(jnp.int32)
    core = (me % 2).reshape(1)
    shard, width = table.shape
    tokens, seqs = token_ids.shape[0], seq_lengths.shape[0]
    seq_len = tokens // seqs
    heads = rel_bias.shape[1]
    most = 2 * tokens // owners
    opening = most // seqs
    cap = min(most, -(-(9 * most // 16) // 16) * 16)
    spare = most - cap
    lanes = -(-(cap + 1) // LANES) * LANES
    gain_one_row, gain_two_row = gain_one.reshape(1, -1), gain_two.reshape(1, -1)

    slot_row, slot_col, ask = route(token_ids, me.reshape(1), seq_len, opening, shard, owners, cap, lanes)
    asked = lax.all_to_all(ask.reshape(owners, lanes), "vocab", split_axis=0, concat_axis=0, tiled=True)
    asked = jnp.take(asked, me ^ jnp.arange(owners), axis=0)
    by_x = swap(asked, "dp", 1)
    by_y = swap(jnp.stack([asked, by_x]), "dp", 2)
    asked_all = jnp.stack([asked, by_x, by_y[0], by_y[1]])
    overflow = jnp.max(asked_all[:, :, lanes - 1]) > 0 if spare else None
    base = me * shard
    targets = jnp.where(asked_all[:, :, :cap] >= 0, asked_all[:, :, :cap] - base, -1)
    local = jnp.clip(asked[:, :cap] - base, 0, shard - 1)
    picked = fetch_rows(table, jnp.where(asked[:, :cap] >= 0, asked[:, :cap] - base, -1))
    rows = exchange(picked)

    rel_bias, cotangent, targets = after([rel_bias, cotangent, targets], rows[1])
    band = make_band(rel_bias)
    cot_t = cotangent.T
    lists = [targets[n, low:high] for n, low, high in arrival_order(owners)]
    lists = jnp.concatenate(lists, axis=0)
    plan = place_plan(lists, shard)

    def spare_rows(step, _):
        slot, asked_more = spare_slots(token_ids + step, seq_len, opening, shard, owners, cap, spare)
        found = jnp.take(table, jnp.clip(asked_more - base, 0, shard - 1), axis=0)
        came = lax.all_to_all(found, "vocab", split_axis=0, concat_axis=0, tiled=True).reshape(-1, width)
        more = jnp.take(came, jnp.clip(slot, 0, owners * spare - 1), axis=0)
        return jnp.where((slot < owners * spare)[:, None], more, jnp.zeros((), BF))

    more = None
    if spare:
        more = lax.fori_loop(0, overflow.astype(jnp.int32), spare_rows, jnp.zeros((tokens, width), BF))
    held = after([rows[0], band, cot_t, *plan])
    rows[0], band, cot_t, plan = held[0], held[1], held[2], held[3:]

    x, hidden, q, k, v = project(slot_col, more, rows, gain_one_row, w_query, w_key, w_value)

    ctx, probs = attend(q, k, v, seq_lengths, rel_bias, band)
    mixed_out, act, d_pre, hidden_t, d_mid, d_att, d_ctx, gain_two_part = middle_part(
        x, ctx, cotangent, gain_two_row, w_out, w_in, w_down
    )
    packed = owners == 8 and groups == 4 and (width // groups) % 64 == 0 and (w_in.shape[1] // owners) % LANES == 0
    place_dp = lax.axis_index("dp")
    x_bit, y_bit, z_high, z_low = place_dp % 2, place_dp // 2, me // 4, (me // 2) % 2
    if packed:
        in_keep, in_send = in_grads(core, hidden_t, d_pre, groups, owners)
        down_keep, down_send = down_grads(core, cot_t, after(act, in_send), groups, owners)
        in_came = swap(in_send, "vocab", 1)
        down_send = after(down_send, in_came)
        down_came = swap(down_send, "vocab", 1)
        out_part = square_part(after(d_att, down_send), ctx, owners)
        down_came = after(down_came, out_part)
        in_sent, in_keep = halve(by_bits(in_keep), by_bits(in_came), x_bit, 1)
        down_sent, down_keep = halve(by_bits(down_keep), by_bits(down_came), y_bit)
        d_ctx = after(d_ctx, in_sent, down_sent, out_part)
        in_came, down_came = swap(in_sent, "dp", 1), swap(down_sent, "dp", 2)
    dq, dk, dv, lines = attend_back(q, k, v, d_ctx, probs)
    if packed:
        in_came, down_came = after([in_came, down_came], dq)
        in_sent, in_keep = halve(in_keep, in_came, y_bit)
        down_sent, down_keep = halve(down_keep, down_came, x_bit)
        qk_keep, qk_send = square_grads(core, [dq, dk], [hidden, hidden], None, groups, owners)
        vo_keep, vo_send = square_grads(core, [dv], [hidden], out_part, groups, owners)
        qk_came, vo_came = swap(qk_send, "vocab", 1), swap(vo_send, "vocab", 1)
        d_mid = after(d_mid, in_sent, down_sent, qk_send, vo_send)
        in_came, down_came = swap(in_sent, "dp", 2), swap(down_sent, "dp", 1)
    row_grad, evens, odds = rows_back(
        slot_row, x, d_mid, dq, dk, dv, gain_one_row, w_query, w_key, w_value, lines, gain_two_part, owners, cap
    )

    if packed:
        odds, *evens = after([odds, *evens], in_came, down_came)
        along, small = pair_blocks(evens, odds, swap(odds, "vocab", 1))
        pair = 2 * cap

        by_one, by_two = swap(along[1], "vocab", 2), swap(along[2], "vocab", 4)
        own_x, own_y = around(along[0])
        qk_came, vo_came = after([qk_came, vo_came], row_grad)
        qk_sent, qk_keep = halve(by_bits(qk_keep), by_bits(qk_came), x_bit, 1)
        vo_sent, vo_keep = halve(by_bits(vo_keep), by_bits(vo_came), y_bit)
        qk_came, vo_came = swap(qk_sent, "dp", 1), swap(vo_sent, "dp", 2)
        held = lax.optimization_barrier((by_one, by_two, own_x, own_y, along[3], qk_came, vo_came))
        by_one, by_two, own_x, own_y, by_three, qk_came, vo_came = held

        by_three = swap(by_three, "vocab", 6)
        mid_rows = jnp.concatenate([by_one[:pair], by_two[:pair]], axis=0)
        mid_x, mid_y = around(mid_rows)
        qk_sent, qk_keep = halve(qk_keep, qk_came, y_bit)
        vo_sent, vo_keep = halve(vo_keep, vo_came, x_bit)
        qk_came, vo_came = swap(qk_sent, "dp", 2), swap(vo_sent, "dp", 1)
        keep = [in_keep, down_keep.reshape(in_keep.shape)]
        came = [in_came, down_came.reshape(in_keep.shape)]
        held = lax.optimization_barrier((by_three, mid_x, mid_y, qk_came, vo_came, own_x, own_y, *came))
        by_three, mid_x, mid_y, qk_came, vo_came, own_x, own_y, *came = held

        small = (small + whole_value(by_one[pair:])) + (whole_value(by_two[pair:]) + whole_value(by_three[pair:]))
        last_sent, small = with_small(by_three[:pair], small)
        last_x, last_y = swap(last_sent, "dp", 1), swap(by_three, "dp", 2)
        keep, came = jnp.concatenate(keep, axis=1), jnp.concatenate(came, axis=1)
        sent, wide_keep = halve(by_bits(keep), by_bits(came), z_high)
        wide_came = swap(sent, "vocab", 4)
        far_low = swap(jnp.concatenate([own_x[:cap], mid_x[:pair]], axis=0), "dp", 2)
        far_high = swap(jnp.concatenate([own_y[cap:], mid_y[pair:]], axis=0), "dp", 1)
        held = lax.optimization_barrier((last_x, last_y, far_low, far_high, wide_came, qk_came, vo_came))
        last_x, last_y, far_low, far_high, wide_came, qk_came, vo_came = held

        low_sent, small = with_small(last_x[:cap], small + whole_value(last_x[pair:]))
        last_low, last_high = swap(low_sent, "dp", 2), swap(last_y[cap:pair], "dp", 1)
        keep = jnp.concatenate([qk_keep, vo_keep], axis=1)
        came = jnp.concatenate([qk_came, vo_came], axis=1)
        sent, keep = halve(by_bits(keep), by_bits(came), z_high)
        came = swap(sent, "vocab", 4)
        sent, wide_keep = halve(wide_keep, wide_came, z_low)
        wide_came = swap(sent, "vocab", 2)
        small = small + whole_value(last_low[cap:])

        placed = [along[0], own_x, own_y, mid_rows, mid_x, mid_y, by_three, last_x, last_y]
        placed += [far_low, far_high, last_low, last_high]
        table_grad = place_rows(plan, placed, shard, cap)
        sent, keep = halve(keep, came, z_low)
        came = swap(sent, "vocab", 2)
        keep = jnp.concatenate([wide_keep, keep], axis=0)
        came = jnp.concatenate([wide_came, came], axis=0)
    else:
        body_rows = owners // 2 * cap
        blocks = [b for both in zip(evens, jnp.split(odds[:body_rows], owners // 2, axis=0)) for b in both]
        arrived = jnp.concatenate(exchange(blocks), axis=0)
        placed = across(arrived, *around(arrived))
        small = whole_value(odds[body_rows:])
        for axis in ("vocab", "dp"):
            bit = 1
            while bit < lax.axis_size(axis):
                small = small + swap(small, axis, bit)
                bit *= 2
        table_grad = place_rows(plan, placed, shard, cap)

    def add_spare(step, total):
        slot, asked_more = spare_slots(token_ids + step, seq_len, opening, shard, owners, cap, spare)
        sent = jnp.zeros((owners * spare + 1, width), F32).at[slot].add(row_grad)[:-1]
        sent = sent.astype(BF).reshape(owners, spare, width)
        came = lax.all_to_all(sent, "vocab", split_axis=0, concat_axis=0, tiled=True)
        target = jnp.where(asked_more >= 0, asked_more - base, shard).reshape(-1)
        part = jnp.zeros((shard, width), F32).at[target].add(came.reshape(-1, width).astype(F32), mode="drop")
        for bit in (1, 2):
            part = part + swap(part, "dp", bit)
        return total + part

    if spare:
        table_grad = lax.fori_loop(0, overflow.astype(jnp.int32), add_spare, table_grad)

    if packed:
        in_grad, down_grad, query_grad, key_grad, value_grad, out_grad = finish(keep, came, width // groups, width // owners)
    else:
        def spread(left, right):
            full = jnp.einsum("td,te->de", left, right, preferred_element_type=F32)
            part = lax.psum_scatter(full, "vocab", scatter_dimension=1, tiled=True).astype(BF)
            return lax.psum_scatter(part, "dp", scatter_dimension=0, tiled=True).astype(F32)

        query_grad, key_grad, value_grad = spread(hidden, dq), spread(hidden, dk), spread(hidden, dv)
        out_grad = spread(ctx, d_att)
        in_grad = spread(hidden_t.T, d_pre)
        down_grad = spread(act, cotangent)

    gain_one_grad, gain_two_grad = small[0], small[1]
    bias_grad = small[2 : 2 + heads, : rel_bias.shape[0]].T
    return (
        mixed_out,
        row_grad,
        table_grad,
        gain_one_grad,
        query_grad,
        key_grad,
        value_grad,
        out_grad,
        gain_two_grad,
        in_grad,
        down_grad,
        bias_grad,
    )


def solution(mesh):
    spread = ("dp", "vocab")
    placed = (
        P(spread),
        P(spread),
        P("vocab", None),
        P(),
        P(),
        P(),
        P(),
        P(),
        P(),
        P(),
        P(),
        P(),
        P(spread, None),
    )
    return jax.shard_map(
        body,
        mesh=mesh,
        in_specs=placed,
        out_specs=(
            P(spread, None),
            P(spread, None),
            P("vocab", None),
            P(),
            P("dp", "vocab"),
            P("dp", "vocab"),
            P("dp", "vocab"),
            P("dp", "vocab"),
            P(),
            P("dp", "vocab"),
            P("dp", "vocab"),
            P(),
        ),
        check_vma=False,
    )
```

```python
from functools import partial

import jax
import jax.numpy as jnp
import numpy as np
from jax import lax
from jax.experimental import pallas as pl
from jax.experimental.pallas import tpu as pltpu
from jax.sharding import PartitionSpec as P

EPS = 1e-06
PRECISE = lax.Precision.HIGHEST
MASKED = -1e30
THRESHOLDS = (12, 16, 23, 32, 46, 64, 91)
LANES = 128
NOWHERE = 1 << 30
BUCKETS = 32
PER_STEP = 2
PER_FETCH = 2
BF = jnp.bfloat16
F32 = jnp.float32
NN = (((1,), (0,)), ((), ()))
NT = (((1,), (1,)), ((), ()))
TN = (((0,), (0,)), ((), ()))


def mm(left, right, dims=NN):
    return lax.dot_general(left, right, dims, preferred_element_type=F32)


def params(mib=56):
    return pltpu.CompilerParams(vmem_limit_bytes=mib << 20)


def cost(macs, moved):
    return pl.CostEstimate(flops=2 * macs, bytes_accessed=moved, transcendentals=0)


def whole(shape):
    return pl.BlockSpec(shape, lambda *_: (0,) * len(shape), pipeline_mode=pl.Buffered(1))


def bucket_of(offset):
    distance = np.abs(offset)
    far = 8 + sum((distance >= t).astype(np.int32) for t in THRESHOLDS)
    return np.where(offset > 0, 16, 0) + np.where(distance < 8, distance, far)


def band_offsets():
    lane = np.arange(4 * LANES)
    return np.where(lane < 3 * LANES, lane, lane - 4 * LANES) - LANES


def band_onehot(buckets):
    return (bucket_of(band_offsets())[:, None] == np.arange(buckets)[None, :]).astype(np.float32)


def route_kernel(me_ref, ids_row_ref, ids_col_ref, slot_row_ref, slot_col_ref, ask_ref, *, seq_len, opening, shard, owners, cap, width):
    me = me_ref[0]
    tokens = ids_row_ref.shape[1]
    ids_row, ids_col = ids_row_ref[...], ids_col_ref[...]
    owner_row, owner_col = jnp.zeros_like(ids_row), jnp.zeros_like(ids_col)
    for o in range(1, owners):
        owner_row += (ids_row >= o * shard).astype(jnp.int32)
        owner_col += (ids_col >= o * shard).astype(jnp.int32)

    def places(shape, axis):
        t = lax.broadcasted_iota(jnp.int32, shape, axis)
        within = lax.rem(t, seq_len)
        repeated = (within < opening) & (t >= seq_len)
        return jnp.where(within < opening, within, t), jnp.logical_not(repeated)

    at_row, first_row = places((1, tokens), 1)
    at_col, first_col = places((tokens, 1), 0)
    key_row, key_col = ids_row * tokens + at_row, ids_col * tokens + at_col
    low_row, low_col = owner_row * (shard * tokens), owner_col * (shard * tokens)
    given_row = jnp.where(first_row, key_row, -1)
    given_col = jnp.where(first_col, key_col, -1)
    rank_col = jnp.sum(((given_row >= low_col) & (given_row < key_col)).astype(jnp.int32), axis=1, keepdims=True)
    rank_row = jnp.sum(((given_col >= low_row) & (given_col < key_row)).astype(jnp.int32), axis=0, keepdims=True)
    slot_row_ref[...] = jnp.where(rank_row < cap, (owner_row ^ me) * cap + rank_row, NOWHERE)
    slot_col_ref[...] = jnp.where(rank_col < cap, (owner_col ^ me) * cap + rank_col, NOWHERE)
    over = (jnp.max(rank_row) >= cap).astype(jnp.int32)
    place_col = jnp.where(first_col & (rank_col < cap), owner_col * width + rank_col, -1)
    step = 4 * LANES
    for start in range(0, owners * width, step):
        lane = lax.broadcasted_iota(jnp.int32, (1, step), 1) + start
        asked = jnp.sum(jnp.where(place_col == lane, ids_col + 1, 0), axis=0, keepdims=True) - 1
        ask_ref[:, start : start + step] = jnp.where(lax.rem(lane, width) == width - 1, over, asked)


def route(token_ids, me, seq_len, opening, shard, owners, cap, width):
    tokens = token_ids.shape[0]
    body = partial(route_kernel, seq_len=seq_len, opening=opening, shard=shard, owners=owners, cap=cap, width=width)
    return pl.pallas_call(
        body,
        in_specs=[pl.BlockSpec(memory_space=pltpu.SMEM), pl.BlockSpec(memory_space=pltpu.VMEM), pl.BlockSpec(memory_space=pltpu.VMEM)],
        out_shape=[
            jax.ShapeDtypeStruct((1, tokens), jnp.int32),
            jax.ShapeDtypeStruct((tokens, 1), jnp.int32),
            jax.ShapeDtypeStruct((1, owners * width), jnp.int32),
        ],
        compiler_params=params(),
        name="route",
    )(me, token_ids.reshape(1, -1), token_ids.reshape(-1, 1))


def windows(lists, tile, shard, window):
    cap = lists.shape[1]
    edges = jnp.arange(pl.cdiv(shard, tile) + 1, dtype=jnp.int32) * tile
    known = jnp.where(lists < 0, NOWHERE, lists)
    below = jnp.sum((known[:, None, :] < edges[None, :, None]).astype(jnp.int32), axis=2)
    starts = jnp.minimum(below[:, :-1] // 16 * 16, cap - window)
    counts = (below[:, 1:] - starts + window - 1) // window
    return starts.T, counts.T, jnp.max(counts, axis=0)


def in_window(start, step, window, cap):
    wanted = start + step * window
    begin = pl.multiple_of(jnp.minimum(wanted, cap - window), 16)
    return begin, begin + lax.broadcasted_iota(jnp.int32, (window, 1), 0) >= wanted


def fetch_kernel(starts_ref, counts_ref, more_ref, list_ref, table_ref, out_refs, total_ref, *, tile, window, shard):
    step_rows, width = table_ref.shape
    blocks = len(out_refs)
    cap = out_refs[0].shape[0]

    @pl.when(pl.program_id(0) == 0)
    def _():
        total_ref[...] = jnp.zeros_like(total_ref)

    for sub in range(step_rows // tile):
        at = pl.program_id(0) * (step_rows // tile) + sub
        row = lax.broadcasted_iota(jnp.int32, (tile, 1), 0) + at * tile
        lane = lax.broadcasted_iota(jnp.int32, (1, tile), 1) + at * tile
        table = table_ref[sub * tile : (sub + 1) * tile, :]
        table = jnp.where(row < shard, table, jnp.zeros((), BF))
        begins = [pl.multiple_of(starts_ref[at, n], 16) for n in range(blocks)]
        wanted = [list_ref[pl.ds(n * cap + begins[n], window), :] for n in range(blocks)]
        found = mm((jnp.concatenate(wanted, axis=0) == lane).astype(F32).astype(BF), table)
        for n in range(blocks):
            total_ref[pl.ds(n * cap + begins[n], window), :] += found[n * window : (n + 1) * window]

        @pl.when(more_ref[at] > 1)
        def _():
            for n in range(blocks):
                def extra(step, carry):
                    begin, fresh = in_window(starts_ref[at, n], step, window, cap)
                    place = pl.ds(n * cap + begin, window)
                    mark = (list_ref[place, :] == lane) & fresh
                    total_ref[place, :] += mm(mark.astype(F32).astype(BF), table)
                    return carry

                lax.fori_loop(1, counts_ref[at, n], extra, 0)

    @pl.when(pl.program_id(0) == pl.num_programs(0) - 1)
    def _():
        for n in range(blocks):
            out_refs[n][...] = total_ref[n * cap : (n + 1) * cap, :].astype(BF)


def fetch_rows(table, lists):
    shard, width = table.shape
    blocks, cap = lists.shape
    tile, window = min(512, shard), min(48, cap)
    starts, counts, more = windows(lists, tile, shard, window)
    tiles = starts.shape[0]
    per_step = PER_FETCH if tiles % PER_FETCH == 0 else 1
    return pl.pallas_call(
        partial(fetch_kernel, tile=tile, window=window, shard=shard),
        grid_spec=pltpu.PrefetchScalarGridSpec(
            num_scalar_prefetch=3,
            grid=(tiles // per_step,),
            in_specs=[whole((blocks * cap, 1)), pl.BlockSpec((per_step * tile, width), lambda t, *_: (t, 0))],
            out_specs=[[whole((cap, width))] * blocks],
            scratch_shapes=[pltpu.VMEM((blocks * cap, width), F32)],
        ),
        out_shape=[[jax.ShapeDtypeStruct((cap, width), BF)] * blocks],
        compiler_params=params(),
        cost_estimate=cost(shard * width * blocks * window, 2 * (shard + blocks * cap) * width),
        name="fetch_rows",
    )(starts, counts, more, lists.reshape(-1, 1), table)[0]


def project_kernel(slot_ref, more_ref, rows_refs, gain_ref, wq_ref, wk_ref, wv_ref, x_ref, hidden_ref, q_ref, k_ref, v_ref):
    slot = slot_ref[...]
    rows = jnp.concatenate([r[...] for r in rows_refs], axis=0)
    lane = lax.broadcasted_iota(jnp.int32, (slot.shape[0], rows.shape[0]), 1)
    x = mm((lane == slot).astype(F32).astype(BF), rows)
    if more_ref is not None:
        x = x + more_ref[...].astype(F32)
    x_ref[...] = x.astype(BF)
    scale = lax.rsqrt(jnp.mean(x * x, axis=1, keepdims=True) + EPS)
    hidden = (x * scale * gain_ref[...]).astype(BF)
    hidden_ref[...] = hidden
    q_ref[...] = mm(hidden, wq_ref[...]).astype(BF)
    k_ref[...] = mm(hidden, wk_ref[...]).astype(BF)
    v_ref[...] = mm(hidden, wv_ref[...]).astype(BF)


def project(slot_col, more, rows, gain, w_query, w_key, w_value):
    tokens, width = slot_col.shape[0], gain.shape[1]
    tile = min(512, tokens)
    out = pl.BlockSpec((tile, width), lambda t: (t, 0))
    count = sum(r.shape[0] for r in rows)
    return pl.pallas_call(
        project_kernel,
        grid=(tokens // tile,),
        in_specs=[pl.BlockSpec((tile, 1), lambda t: (t, 0)), None if more is None else out, [whole(r.shape) for r in rows], whole(gain.shape)]
        + [whole(w_query.shape)] * 3,
        out_specs=[out] * 5,
        out_shape=[jax.ShapeDtypeStruct((tokens, width), BF)] * 5,
        compiler_params=params(),
        cost_estimate=cost(tokens * width * (3 * width + count), 14 * tokens * width),
        name="project",
    )(slot_col, more, rows, gain, w_query, w_key, w_value)


def band_kernel(line_ref, band_ref):
    line = jnp.broadcast_to(line_ref[0], (LANES, line_ref.shape[2]))
    band_ref[0] = pltpu.roll(line, 0, 1, stride=1, stride_axis=0)[:, : 3 * LANES]


def make_band(rel_bias):
    heads = rel_bias.shape[1]
    line = jnp.dot(band_onehot(rel_bias.shape[0]), rel_bias, precision=PRECISE).T.reshape(heads, 1, -1)
    return pl.pallas_call(
        band_kernel,
        grid=(heads,),
        in_specs=[pl.BlockSpec((1,) + line.shape[1:], lambda h: (h, 0, 0))],
        out_specs=pl.BlockSpec((1, LANES, 3 * LANES), lambda h: (h, 0, 0)),
        out_shape=jax.ShapeDtypeStruct((heads, LANES, 3 * LANES), F32),
        compiler_params=params(30),
        name="band",
    )(line)


def attend_kernel(len_ref, far_ref, q_ref, k_ref, v_ref, band_ref, ctx_ref, p_ref):
    pair = pl.program_id(1)
    q, k, v = q_ref[...], k_ref[...], v_ref[...]
    seq_len = q.shape[0]
    blocks = seq_len // LANES
    last = far_ref.shape[0] // 2 - 1
    half = lax.broadcasted_iota(jnp.int32, (1, LANES), 1) // (LANES // 2)
    key_at = lax.broadcasted_iota(jnp.int32, (1, seq_len), 1)
    mask = jnp.where(key_at < len_ref[pl.program_id(0)], 0.0, MASKED)
    none = jnp.zeros((), BF)
    ctx = jnp.zeros((seq_len, LANES), F32)
    for h in range(2):
        k_own, v_own = jnp.where(half == h, k, none), jnp.where(half == h, v, none)
        left, right = far_ref[last, 2 * pair + h], far_ref[2 * last + 1, 2 * pair + h]
        for i in range(blocks):
            raw = mm(q[i * LANES : (i + 1) * LANES], k_own, NT)
            tiles = []
            for j in range(blocks):
                cols = slice(j * LANES, (j + 1) * LANES)
                d = j - i
                if abs(d) <= 1:
                    tiles.append(raw[:, cols] + band_ref[h, :, (d + 1) * LANES : (d + 2) * LANES] + mask[:, cols])
                else:
                    tiles.append(raw[:, cols] + (mask[:, cols] + (left if d < 0 else right)))
            scores = jnp.concatenate(tiles, axis=1)
            grown = jnp.exp(scores - jnp.max(scores, axis=1, keepdims=True))
            total = jnp.sum(grown, axis=1, keepdims=True)
            p_ref[0, h, i * LANES : (i + 1) * LANES, :] = (grown * (1.0 / total)).astype(BF)
        ctx = ctx + mm(p_ref[0, h], v_own)
    ctx_ref[...] = ctx.astype(BF)


def attend(q, k, v, lengths, rel_bias, band):
    seqs, heads = lengths.shape[0], rel_bias.shape[1]
    tokens, width = q.shape
    seq_len = tokens // seqs
    block = pl.BlockSpec((seq_len, LANES), lambda s, p, *_: (s, p))
    return pl.pallas_call(
        attend_kernel,
        grid_spec=pltpu.PrefetchScalarGridSpec(
            num_scalar_prefetch=2,
            grid=(seqs, heads // 2),
            in_specs=[block] * 3 + [pl.BlockSpec((2,) + band.shape[1:], lambda s, p, *_: (p, 0, 0))],
            out_specs=[block, pl.BlockSpec((1, 2, seq_len, seq_len), lambda s, p, *_: (s, p, 0, 0))],
        ),
        out_shape=[
            jax.ShapeDtypeStruct((tokens, width), BF),
            jax.ShapeDtypeStruct((seqs, heads, seq_len, seq_len), BF),
        ],
        compiler_params=params(),
        cost_estimate=cost(tokens * seq_len * width * 8, 2 * tokens * seq_len * heads),
        name="attend",
    )(lengths, rel_bias, q, k, v, band)


def attend_back_kernel(q_ref, k_ref, v_ref, ctx_ref, do_ref, p_ref, dq_ref, dk_ref, dv_ref, line_ref, ds_ref, band_ref, far_ref):
    seq_at = pl.program_id(1)
    q, k, v, do = q_ref[...], k_ref[...], v_ref[...], do_ref[...]
    seq_len = q.shape[0]
    blocks = seq_len // LANES
    half = lax.broadcasted_iota(jnp.int32, (1, LANES), 1) // (LANES // 2)
    none = jnp.zeros((), BF)

    @pl.when(seq_at == 0)
    def _():
        band_ref[...] = jnp.zeros_like(band_ref)
        far_ref[...] = jnp.zeros_like(far_ref)

    swing = ctx_ref[...].astype(F32) * do.astype(F32)
    row_half = lax.broadcasted_iota(jnp.int32, (LANES, 1), 0) // (LANES // 2)
    q_t, do_t = (a.astype(F32).T.astype(BF) for a in (q, do))
    dq = jnp.zeros((seq_len, LANES), F32)
    dk_t = dv_t = jnp.zeros((LANES, seq_len), F32)
    for h in range(2):
        k_own, v_own = jnp.where(half == h, k, none), jnp.where(half == h, v, none)
        near = [jnp.zeros((LANES, LANES), F32) for _ in range(3)]
        far = [jnp.zeros((8, LANES), F32) for _ in range(2)]
        for i in range(blocks):
            rows = slice(i * LANES, (i + 1) * LANES)
            probs = p_ref[0, h, rows, :].astype(F32)
            swing_own = jnp.sum(jnp.where(half == h, swing[rows], 0.0), axis=1, keepdims=True)
            ds = probs * (mm(do[rows], v_own, NT) - swing_own)
            for j in range(blocks):
                d = j - i
                tile = ds[:, j * LANES : (j + 1) * LANES]
                if abs(d) <= 1:
                    near[d + 1] = near[d + 1] + tile
                else:
                    side = 0 if d < 0 else 1
                    far[side] = far[side] + jnp.sum(tile.reshape(LANES // 8, 8, LANES), axis=0)
            ds_ref[rows, :] = ds.astype(BF)
        for d in range(3):
            band_ref[h, :, d * LANES : (d + 1) * LANES] += near[d]
        for side in range(2):
            far_ref[h, :, side * LANES : (side + 1) * LANES] += far[side]
        d_low = ds_ref[...]
        dk_t = dk_t + mm(jnp.where(row_half == h, q_t, none), d_low)
        dv_t = dv_t + mm(jnp.where(row_half == h, do_t, none), p_ref[0, h])
        dq = dq + mm(d_low, k_own)
    dq_ref[...], dk_ref[...], dv_ref[...] = dq.astype(BF), dk_t.T.astype(BF), dv_t.T.astype(BF)

    @pl.when(seq_at == pl.num_programs(1) - 1)
    def _():
        row = lax.broadcasted_iota(jnp.int32, (8, 1), 0)
        for h in range(2):
            padded = jnp.concatenate([band_ref[h], jnp.zeros((LANES, LANES), F32)], axis=1)
            turned = padded[:8]
            for start in range(8, LANES, 8):
                turned = turned + pltpu.roll(padded[start : start + 8], 4 * LANES - start, 1)
            for bit in (1, 2, 4):
                turned = jnp.where(row & bit > 0, pltpu.roll(turned, 4 * LANES - bit, 1), turned)
            line_ref[0, h : h + 1, :] = jnp.sum(turned, axis=0, keepdims=True)
            line_ref[0, 2 + h : 3 + h, : 2 * LANES] = jnp.sum(far_ref[h], axis=0, keepdims=True)


def attend_back(q, k, v, ctx, d_context, probs):
    seqs, heads, seq_len, _ = probs.shape
    tokens, width = q.shape
    pairs = heads // 2
    block = pl.BlockSpec((seq_len, LANES), lambda p, s: (s, p))
    return pl.pallas_call(
        attend_back_kernel,
        grid=(pairs, seqs),
        in_specs=[block] * 5 + [pl.BlockSpec((1, 2, seq_len, seq_len), lambda p, s: (s, p, 0, 0))],
        out_specs=[block] * 3 + [pl.BlockSpec((1, 8, 4 * LANES), lambda p, s: (p, 0, 0))],
        out_shape=[jax.ShapeDtypeStruct((tokens, width), BF)] * 3
        + [jax.ShapeDtypeStruct((heads // 2, 8, 4 * LANES), F32)],
        scratch_shapes=[
            pltpu.VMEM((seq_len, seq_len), BF),
            pltpu.VMEM((2, LANES, 3 * LANES), F32),
            pltpu.VMEM((2, 8, 2 * LANES), F32),
        ],
        compiler_params=params(),
        cost_estimate=cost(tokens * seq_len * width * 12, 2 * tokens * seq_len * heads),
        name="attend_back",
    )(q, k, v, ctx, d_context, probs)


def middle_kernel(x_ref, ctx_ref, cot_ref, gain_ref, w_out_ref, w_in_ref, w_down_ref, mid_ref, act_ref, d_pre_ref, hidden_t_ref, d_mid_ref, d_att_ref, d_ctx_ref, gain_grad_ref, *, chunk):
    mid = x_ref[...].astype(F32) + mm(ctx_ref[...], w_out_ref[...])
    gain = gain_ref[...]
    scale = lax.rsqrt(jnp.mean(mid * mid, axis=1, keepdims=True) + EPS)
    hidden_full = mid * scale * gain
    hidden = hidden_full.astype(BF)
    hidden_t_ref[...] = hidden_full.T.astype(BF)
    cot = cot_ref[...]
    mid_ref[...] = mid
    d_hidden = jnp.zeros_like(mid)
    slope = float(np.sqrt(2 / np.pi))
    for start in range(0, w_in_ref.shape[1], chunk):
        cols = slice(start, start + chunk)
        pre = mm(hidden, w_in_ref[:, cols])
        d_act = mm(cot, w_down_ref[cols, :], NT)
        square = pre * pre
        bent = jnp.tanh(slope * pre * (1.0 + 0.044715 * square))
        open_half = 0.5 + 0.5 * bent
        act = (pre * open_half).astype(BF)
        curve = (0.5 * slope) * pre * (1.0 - bent * bent) * (1.0 + (3 * 0.044715) * square)
        d_pre = (d_act * (open_half + curve)).astype(BF)
        act_ref[:, cols] = act
        d_pre_ref[:, cols] = d_pre
        d_hidden = d_hidden + mm(d_pre, w_in_ref[:, cols], NT)
    u = d_hidden * gain
    swing = jnp.mean(u * mid, axis=1, keepdims=True)
    d_mid = cot.astype(F32) + scale * u - mid * (scale * scale * scale * swing)
    d_mid_ref[...] = d_mid
    d_att = d_mid.astype(BF)
    d_att_ref[...] = d_att
    d_ctx_ref[...] = mm(d_att, w_out_ref[...], NT).astype(BF)

    @pl.when(pl.program_id(0) == 0)
    def _():
        gain_grad_ref[...] = jnp.zeros_like(gain_grad_ref)

    gain_grad_ref[...] += jnp.sum((d_hidden * mid * scale).reshape(-1, 8, mid.shape[1]), axis=0)


def middle_part(x, ctx, cot, gain, w_out, w_in, w_down):
    tokens, width = x.shape
    wide = w_in.shape[1]
    tile = min(256, tokens)
    rows = pl.BlockSpec((tile, width), lambda t: (t, 0))
    wide_rows = pl.BlockSpec((tile, wide), lambda t: (t, 0))
    return pl.pallas_call(
        partial(middle_kernel, chunk=min(768, wide)),
        grid=(tokens // tile,),
        in_specs=[rows] * 3 + [whole(a.shape) for a in (gain, w_out, w_in, w_down)],
        out_specs=[rows, wide_rows, wide_rows, pl.BlockSpec((width, tile), lambda t: (0, t)), rows, rows, rows]
        + [pl.BlockSpec((8, width), lambda t: (0, 0))],
        out_shape=[
            jax.ShapeDtypeStruct((tokens, width), F32),
            jax.ShapeDtypeStruct((tokens, wide), BF),
            jax.ShapeDtypeStruct((tokens, wide), BF),
            jax.ShapeDtypeStruct((width, tokens), BF),
            jax.ShapeDtypeStruct((tokens, width), F32),
            jax.ShapeDtypeStruct((tokens, width), BF),
            jax.ShapeDtypeStruct((tokens, width), BF),
            jax.ShapeDtypeStruct((8, width), F32),
        ],
        compiler_params=params(),
        cost_estimate=cost(tokens * width * (4 * wide + 2 * width), 4 * width * wide + 8 * tokens * (wide + width)),
        name="middle",
    )(x, ctx, cot, gain, w_out, w_in, w_down)


def mix_kernel(mid_ref, act_ref, w_down_ref, mixed_ref):
    mixed_ref[...] = (mid_ref[...] + mm(act_ref[...], w_down_ref[...])).astype(BF)


def mix(mid, act, w_down):
    tokens, width = mid.shape
    wide = act.shape[1]
    tile = min(256, tokens)
    rows = pl.BlockSpec((tile, width), lambda t: (t, 0))
    return pl.pallas_call(
        mix_kernel,
        grid=(tokens // tile,),
        in_specs=[rows, pl.BlockSpec((tile, wide), lambda t: (t, 0)), whole(w_down.shape)],
        out_specs=rows,
        out_shape=jax.ShapeDtypeStruct((tokens, width), BF),
        compiler_params=params(),
        cost_estimate=cost(tokens * width * wide, 2 * wide * (tokens + width)),
        name="mix",
    )(mid, act, w_down)


def in_grads_kernel(core_ref, hidden_t_ref, d_pre_ref, keep_ref, send_ref, part_ref):
    core = core_ref[0]
    groups, lanes = keep_ref.shape[0], keep_ref.shape[3]
    part = mm(hidden_t_ref[...], d_pre_ref[...]).astype(BF)
    for c in range(2):
        part_ref[c] = part[:, c * lanes : (c + 1) * lanes].reshape(groups, -1, lanes)
    for d in range(groups):
        keep_ref[d, 0] = part_ref[core, d]
        send_ref[d, 0] = part_ref[1 - core, d]


def in_grads(core, hidden_t, d_pre, groups, owners):
    width, tokens = hidden_t.shape
    wide = d_pre.shape[1]
    lanes, zs = wide // owners, owners // 2
    out = pl.BlockSpec((groups, 1, width // groups, lanes), lambda z, *_: (0, z, 0, 0))
    return pl.pallas_call(
        in_grads_kernel,
        grid_spec=pltpu.PrefetchScalarGridSpec(
            num_scalar_prefetch=1,
            grid=(zs,),
            in_specs=[whole(hidden_t.shape), pl.BlockSpec((tokens, 2 * lanes), lambda z, *_: (0, z))],
            out_specs=[out, out],
            scratch_shapes=[pltpu.VMEM((2, groups, width // groups, lanes), BF)],
        ),
        out_shape=[jax.ShapeDtypeStruct((groups, zs, width // groups, lanes), BF)] * 2,
        compiler_params=params(),
        cost_estimate=cost(tokens * width * wide, 2 * wide * (tokens + width)),
        name="in_grads",
    )(core, hidden_t, d_pre)


def down_grads_kernel(core_ref, cot_t_ref, act_ref, keep_ref, send_ref, parts_ref):
    core = core_ref[0]
    halves, lanes = keep_ref.shape[2], keep_ref.shape[4]
    part = mm(cot_t_ref[...], act_ref[...]).astype(BF)
    for h in range(halves):
        parts_ref[h] = part[:, h * lanes : (h + 1) * lanes].reshape(parts_ref.shape[1:])
        for z in range(keep_ref.shape[1]):
            keep_ref[0, z, h] = parts_ref[h, 2 * z + core]
            send_ref[0, z, h] = parts_ref[h, 2 * z + 1 - core]


def down_grads(core, cot_t, act, groups, owners):
    width, tokens = cot_t.shape
    wide = act.shape[1]
    lanes, zs = wide // owners, owners // 2
    halves = owners // groups
    out = pl.BlockSpec((1, zs, halves, width // owners, lanes), lambda d, *_: (d, 0, 0, 0, 0))
    return pl.pallas_call(
        down_grads_kernel,
        grid_spec=pltpu.PrefetchScalarGridSpec(
            num_scalar_prefetch=1,
            grid=(groups,),
            in_specs=[whole(cot_t.shape), pl.BlockSpec((tokens, wide // groups), lambda d, *_: (0, d))],
            out_specs=[out, out],
            scratch_shapes=[pltpu.VMEM((halves, owners, width // owners, lanes), BF)],
        ),
        out_shape=[jax.ShapeDtypeStruct((groups, zs, halves, width // owners, lanes), BF)] * 2,
        compiler_params=params(),
        cost_estimate=cost(tokens * width * wide, 2 * wide * (tokens + width)),
        name="down_grads",
    )(core, cot_t, act)


def square_kernel(left_ref, right_ref, out_ref):
    out_ref[...] = mm(left_ref[...], right_ref[...], TN).astype(BF).reshape(out_ref.shape)


def square_part(left, right, owners):
    tokens, width = left.shape
    return pl.pallas_call(
        square_kernel,
        out_shape=jax.ShapeDtypeStruct((owners, width // owners, right.shape[1]), BF),
        compiler_params=params(30),
        cost_estimate=cost(tokens * width * width, 6 * tokens * width),
        name="square_part",
    )(left, right)


def square_grads_kernel(core_ref, left_refs, right_refs, ready_ref, keep_ref, send_ref, parts_ref, *, groups, owners):
    core = core_ref[0]
    for n, (left_ref, right_ref) in enumerate(zip(left_refs, right_refs)):
        parts_ref[n] = mm(left_ref[...], right_ref[...], TN).astype(BF).reshape(parts_ref.shape[1:])
    lanes = right_refs[0].shape[1] // groups
    for z in range(owners // 2):
        for target_ref, v in ((keep_ref, 2 * z + core), (send_ref, 2 * z + 1 - core)):
            first, second = parts_ref[0, v], parts_ref[1, v] if ready_ref is None else ready_ref[v]
            for d in range(groups):
                cols = slice(d * lanes, (d + 1) * lanes)
                target_ref[d, z] = jnp.concatenate([first[:, cols], second[:, cols]], axis=1)


def square_grads(core, lefts, rights, ready, groups, owners):
    tokens, width = rights[0].shape
    shape = (groups, owners // 2, width // owners, 2 * width // groups)
    vmem = pl.BlockSpec(memory_space=pltpu.VMEM)
    return pl.pallas_call(
        partial(square_grads_kernel, groups=groups, owners=owners),
        in_specs=[pl.BlockSpec(memory_space=pltpu.SMEM), [vmem] * len(lefts), [vmem] * len(lefts)]
        + [None if ready is None else vmem],
        out_shape=[jax.ShapeDtypeStruct(shape, BF)] * 2,
        scratch_shapes=[pltpu.VMEM((len(lefts), owners, width // owners, width), BF)],
        compiler_params=params(30),
        cost_estimate=cost(len(lefts) * tokens * width * width, 12 * tokens * width),
        name="square_grads",
    )(core, lefts, rights, ready)


SMALL = 16


def low_parts(value, high_of):
    gains, bias = value
    gains_high, bias_high = high_of(gains), high_of(bias)
    bias = jnp.concatenate([bias_high, bias - bias_high], axis=1)
    bias = jnp.concatenate([bias, jnp.zeros((SMALL - 4, gains.shape[1] - bias.shape[1]), F32)], axis=1)
    return jnp.concatenate([gains_high, gains - gains_high, bias], axis=0).astype(BF)


def whole_value(parts):
    parts = parts.astype(F32)
    return parts[0:2] + parts[2:4], parts[4:SMALL, :LANES] + parts[4:SMALL, LANES : 2 * LANES]


def sum_of(first, second):
    return tuple(a + b for a, b in zip(first, second))


def round_low(value):
    return value.astype(BF).astype(F32)


def small_value(lines_ref, onehot_ref, gain_one_part, gain_two_part):
    pairs = lines_ref.shape[0]
    near = jnp.concatenate([lines_ref[p, 0:2, :] for p in range(pairs)], axis=0)
    far = jnp.concatenate([lines_ref[p, 2:4, : 2 * LANES] for p in range(pairs)], axis=0)
    bias = lax.dot_general(near, onehot_ref[...], NN, precision=PRECISE, preferred_element_type=F32)
    lane = lax.broadcasted_iota(jnp.int32, (1, LANES), 1)
    left = jnp.sum(far[:, :LANES], axis=1, keepdims=True)
    right = jnp.sum(far[:, LANES:], axis=1, keepdims=True)
    bias = bias + jnp.where(lane == BUCKETS // 2 - 1, left, 0.0) + jnp.where(lane == BUCKETS - 1, right, 0.0)
    gains = [jnp.sum(g, axis=0, keepdims=True) for g in (gain_one_part, gain_two_part)]
    return jnp.concatenate(gains, axis=0), bias


def rows_kernel(slot_ref, x_ref, d_mid_ref, dq_ref, dk_ref, dv_ref, gain_ref, wq_ref, wk_ref, wv_ref, lines_ref, onehot_ref, gain_two_ref, row_ref, even_refs, odd_ref, held_ref, gain_grad_ref):
    d_hidden = mm(dq_ref[...], wq_ref[...], NT) + mm(dk_ref[...], wk_ref[...], NT) + mm(dv_ref[...], wv_ref[...], NT)
    x = x_ref[...].astype(F32)
    scale = lax.rsqrt(jnp.mean(x * x, axis=1, keepdims=True) + EPS)
    u = d_hidden * gain_ref[...]
    swing = jnp.mean(u * x, axis=1, keepdims=True)
    row = d_mid_ref[...] + scale * u - x * (scale * scale * scale * swing)
    row_ref[...] = row
    at = pl.program_id(0)

    @pl.when(at == 0)
    def _():
        gain_grad_ref[...] = jnp.zeros_like(gain_grad_ref)

    gain_grad_ref[...] += jnp.sum((d_hidden * x * scale).reshape(-1, 8, x.shape[1]), axis=0)
    tile = row.shape[0]
    held_ref[pl.ds(pl.multiple_of(at * tile, tile), tile), :] = row.astype(BF)

    @pl.when(at == pl.num_programs(0) - 1)
    def _():
        slot, held = slot_ref[...], held_ref[...]
        cap, evens = even_refs[0].shape[0], len(even_refs)
        order = [2 * n for n in range(evens)] + [2 * n + 1 for n in range(evens)]
        line = lax.broadcasted_iota(jnp.int32, (cap, slot.shape[1]), 0)
        together = min(len(order), 8)
        for low in range(0, len(order), together):
            places = jnp.concatenate([line + k * cap for k in order[low : low + together]], axis=0)
            sent = mm((places == slot).astype(F32).astype(BF), held).astype(BF)
            for n in range(together):
                part, at_n = sent[n * cap : (n + 1) * cap], low + n
                if at_n < evens:
                    even_refs[at_n][...] = part
                else:
                    odd_ref[(at_n - evens) * cap : (at_n - evens + 1) * cap, :] = part
        small = small_value(lines_ref, onehot_ref, gain_grad_ref[...], gain_two_ref[...])
        odd_ref[evens * cap :, :] = low_parts(small, round_low)


def rows_back(slot_row, x, d_mid, dq, dk, dv, gain, w_query, w_key, w_value, lines, gain_two_part, owners, cap):
    tokens, width = x.shape
    onehot = jnp.asarray(band_onehot(LANES))
    half = owners // 2
    tile = min(256, tokens)
    rows = pl.BlockSpec((tile, width), lambda t: (t, 0))
    return pl.pallas_call(
        rows_kernel,
        grid=(tokens // tile,),
        in_specs=[whole(slot_row.shape)] + [rows] * 5 + [whole(gain.shape)] + [whole(w_query.shape)] * 3
        + [whole(a.shape) for a in (lines, onehot, gain_two_part)],
        out_specs=[rows, [whole((cap, width))] * half, whole((half * cap + SMALL, width))],
        out_shape=[
            jax.ShapeDtypeStruct((tokens, width), F32),
            [jax.ShapeDtypeStruct((cap, width), BF)] * half,
            jax.ShapeDtypeStruct((half * cap + SMALL, width), BF),
        ],
        scratch_shapes=[pltpu.VMEM((tokens, width), BF), pltpu.VMEM((8, width), F32)],
        compiler_params=params(),
        cost_estimate=cost(tokens * width * (3 * width + owners * cap), 20 * tokens * width),
        name="rows_back",
    )(slot_row, x, d_mid, dq, dk, dv, gain, w_query, w_key, w_value, lines, onehot, gain_two_part)


def plan_kernel(starts_ref, list_ref, plan_ref, *, blocks, window):
    at = pl.program_id(0)
    cap = list_ref.shape[0] // blocks
    wanted = [list_ref[pl.ds(n * cap + pl.multiple_of(starts_ref[at, n], 16), window), :] for n in range(blocks)]
    wanted = jnp.concatenate(wanted, axis=0)
    for low in range(0, wanted.shape[0], LANES):
        part = jnp.broadcast_to(wanted[low : low + LANES], (min(LANES, wanted.shape[0] - low), LANES))
        plan_ref[0, :, low : low + LANES] = part.T[:1]


def place_plan(lists, shard):
    blocks, cap = lists.shape
    tile, window = min(256, shard), min(32, cap)
    starts, counts, more = windows(lists, tile, shard, window)
    tiles = pl.cdiv(shard, tile)
    column = lists.reshape(-1, 1)
    plan = pl.pallas_call(
        partial(plan_kernel, blocks=blocks, window=window),
        grid_spec=pltpu.PrefetchScalarGridSpec(
            num_scalar_prefetch=1,
            grid=(tiles,),
            in_specs=[whole(column.shape)],
            out_specs=pl.BlockSpec((1, 1, blocks * window), lambda t, *_: (t, 0, 0)),
        ),
        out_shape=jax.ShapeDtypeStruct((tiles, 1, blocks * window), jnp.int32),
        compiler_params=params(30),
        name="place_plan",
    )(starts, column)
    return starts, counts, more, plan, column


def place_kernel(starts_ref, counts_ref, more_ref, plan_ref, list_ref, rows_refs, out_ref, list_held, list_sem, *, tile, window, cap):
    per_step = plan_ref.shape[0]
    places = [(ref, low) for ref in rows_refs for low in range(0, ref.shape[0] // cap * cap, cap)]
    for sub in range(per_step):
        at = pl.program_id(0) * per_step + sub
        out_rows = slice(sub * tile, (sub + 1) * tile)
        row = lax.broadcasted_iota(jnp.int32, (tile, 1), 0) + at * tile
        held = []
        for n, (rows_ref, low) in enumerate(places):
            held.append(rows_ref[pl.ds(low + pl.multiple_of(starts_ref[at, n], 16), window), :])
        out_ref[out_rows, :] = mm((row == plan_ref[sub]).astype(F32).astype(BF), jnp.concatenate(held, axis=0))

    for sub in range(per_step):
        at = pl.program_id(0) * per_step + sub
        out_rows = slice(sub * tile, (sub + 1) * tile)

        @pl.when(more_ref[at] > 1)
        def _():
            copy = pltpu.make_async_copy(list_ref, list_held, list_sem)
            copy.start()
            copy.wait()
            lane = lax.broadcasted_iota(jnp.int32, (1, tile), 1) + at * tile
            for n, (rows_ref, low) in enumerate(places):
                def extra(step, carry):
                    begin, fresh = in_window(starts_ref[at, n], step, window, cap)
                    own = (list_held[pl.ds(n * cap + begin, window), :] == lane) & fresh
                    rows = rows_ref[pl.ds(low + begin, window), :]
                    out_ref[out_rows, :] += mm(own.astype(F32).astype(BF), rows, TN)
                    return carry

                lax.fori_loop(1, counts_ref[at, n], extra, 0)


def place_rows(plan, rows, shard, cap):
    width = rows[0].shape[1]
    starts, counts, more, lanes, column = plan
    tile, window = min(256, shard), min(32, cap)
    per_step = PER_STEP if starts.shape[0] % PER_STEP == 0 else 1
    return pl.pallas_call(
        partial(place_kernel, tile=tile, window=window, cap=cap),
        grid_spec=pltpu.PrefetchScalarGridSpec(
            num_scalar_prefetch=3,
            grid=(starts.shape[0] // per_step,),
            in_specs=[
                pl.BlockSpec((per_step, 1, lanes.shape[2]), lambda t, *_: (t, 0, 0)),
                pl.BlockSpec(memory_space=pl.ANY),
                [whole(r.shape) for r in rows],
            ],
            out_specs=pl.BlockSpec((per_step * tile, width), lambda t, *_: (t, 0)),
            scratch_shapes=[pltpu.VMEM(column.shape, jnp.int32), pltpu.SemaphoreType.DMA],
        ),
        out_shape=jax.ShapeDtypeStruct((shard, width), F32),
        compiler_params=params(30),
        cost_estimate=cost(shard * width * lanes.shape[2], 4 * shard * width + 2 * column.shape[0] * width),
        name="place_rows",
    )(starts, counts, more, lanes, column, rows)


def pair_kernel(even_refs, own_ref, came_ref, out_refs):
    cap = even_refs[0].shape[0]
    rows = len(even_refs) * cap
    small = sum_of(whole_value(own_ref[rows:, :]), whole_value(came_ref[rows:, :]))
    parts = low_parts(small, round_low)
    for n, out_ref in enumerate(out_refs):
        out_ref[:cap, :] = even_refs[n][...]
        out_ref[cap : 2 * cap, :] = came_ref[n * cap : (n + 1) * cap, :]
        if n > 0:
            out_ref[2 * cap :, :] = parts


def pair_blocks(evens, own, came):
    cap, width = evens[0].shape
    shapes = [(2 * cap, width)] + [(2 * cap + SMALL, width)] * (len(evens) - 1)
    return pl.pallas_call(
        pair_kernel,
        out_shape=[[jax.ShapeDtypeStruct(shape, BF) for shape in shapes]],
        compiler_params=params(),
        cost_estimate=cost(1, 1),
        name="pair_blocks",
    )(evens, own, came)[0]


def swap(value, axis, bit):
    count = lax.axis_size(axis)
    return lax.ppermute(value, axis, [(i, i ^ bit) for i in range(count)])


def arrival_order(owners):
    if owners != 8:
        return [(n, 0, owners) for n in range(4)]
    order = [(n, low, high) for low, high in ((0, 2), (2, 6), (6, 8)) for n in range(3)]
    return order + [(3, 0, 1), (3, 2, 4), (3, 1, 2), (3, 4, 6), (3, 6, 7), (3, 7, 8)]


def exchange(blocks):
    owners = lax.axis_size("vocab")
    if owners <= 8:
        return [blocks[0]] + [swap(blocks[k], "vocab", k) for k in range(1, owners)]
    order = lax.axis_index("vocab") ^ jnp.arange(owners)
    sent = jnp.take(jnp.stack(blocks), order, axis=0)
    came = lax.all_to_all(sent, "vocab", split_axis=0, concat_axis=0, tiled=True)
    return list(jnp.take(came, order, axis=0))


def around(block):
    return swap(block, "dp", 1), swap(block, "dp", 2)


def across(block, by_x, by_y):
    half = block.shape[0] // 2
    return [block, by_x, by_y, swap(by_x[:half], "dp", 2), swap(by_y[half:], "dp", 1)]


class Shares:
    def __init__(self, *terms):
        self.terms = [t.reshape((2, 2, 2, 2, -1, t.shape[-1])) for t in terms]
        self.bits = {}

    def half(self, term, bits):
        starts = [bits.get(axis, 0) if size == 2 and axis < 4 else 0 for axis, size in enumerate(term.shape)]
        sizes = [1 if axis in bits else size for axis, size in enumerate(term.shape)]
        return lax.dynamic_slice(term, starts, sizes).astype(F32)

    def send(self, axis, at):
        sent = sum(self.half(t, {**self.bits, axis: 1 - at}) for t in self.terms).astype(BF)
        self.bits[axis] = at
        return sent

    def add(self, came):
        self.terms.append(came)

    def part(self, bits):
        total = sum(self.half(t, {**self.bits, **bits}) for t in self.terms).astype(BF)
        return total.reshape(total.shape[-2:])


def with_small(rows, small):
    parts = low_parts(small, lambda value: lax.reduce_precision(value, 8, 7))
    return jnp.concatenate([rows, parts], axis=0), whole_value(parts)


def after(value, *others):
    if isinstance(value, (list, tuple)):
        return list(lax.optimization_barrier(tuple(value) + others)[: len(value)])
    return lax.optimization_barrier((value,) + others)[0]


def finish_kernel(wide_refs, square_refs, in_ref, down_ref, q_ref, k_ref, v_ref, o_ref):
    wide, square = (sum(ref[...].astype(F32) for ref in refs) for refs in (wide_refs, square_refs))
    rows, lanes, low = down_ref.shape[1], wide.shape[1], in_ref.shape[0]
    in_ref[...] = wide[:low]
    for n in range(down_ref.shape[0] // lanes):
        down_ref[n * lanes : (n + 1) * lanes, :] = wide[low : low + rows].T
        low += rows
    for n, (first_ref, second_ref) in enumerate(((q_ref, k_ref), (v_ref, o_ref))):
        turned = square[n * rows : (n + 1) * rows].T
        first_ref[...] = turned[: q_ref.shape[0]]
        second_ref[...] = turned[q_ref.shape[0] :]


def finish(wide, square, in_rows, rows):
    lanes = wide[0].shape[1]
    down = (wide[0].shape[0] - in_rows) // rows * lanes
    return pl.pallas_call(
        finish_kernel,
        out_shape=[jax.ShapeDtypeStruct((in_rows, lanes), F32), jax.ShapeDtypeStruct((down, rows), F32)]
        + [jax.ShapeDtypeStruct((lanes // 2, rows), F32)] * 4,
        compiler_params=params(24),
        cost_estimate=cost(1, 1),
        name="finish",
    )(wide, square)


def spare_slots(token_ids, seq_len, opening, shard, owners, cap, spare):
    tokens = token_ids.shape[0]
    t = jnp.arange(tokens, dtype=jnp.int32)
    within = t % seq_len
    at = jnp.where(within < opening, within, t)
    first = (within >= opening) | (t < seq_len)
    owner = token_ids // shard
    key = token_ids * tokens + at
    same = (owner[:, None] == owner[None, :]) & first[None, :] & (key[None, :] < key[:, None])
    rank = jnp.sum(same.astype(jnp.int32), axis=1) - cap
    slot = jnp.where(rank >= 0, owner * spare + rank, owners * spare)
    request = jnp.full((owners * spare + 1,), -1, jnp.int32).at[slot].set(token_ids)[:-1]
    asked = lax.all_to_all(request.reshape(owners, spare), "vocab", split_axis=0, concat_axis=0, tiled=True)
    return slot, asked


def body(
    token_ids,
    seq_lengths,
    table,
    gain_one,
    w_query,
    w_key,
    w_value,
    w_out,
    gain_two,
    w_in,
    w_down,
    rel_bias,
    cotangent,
):
    owners, groups = lax.axis_size("vocab"), lax.axis_size("dp")
    me = lax.axis_index("vocab").astype(jnp.int32)
    core = (me % 2).reshape(1)
    shard, width = table.shape
    tokens, seqs = token_ids.shape[0], seq_lengths.shape[0]
    seq_len = tokens // seqs
    heads = rel_bias.shape[1]
    most = 2 * tokens // owners
    opening = most // seqs
    cap = min(most, -(-(9 * most // 16) // 16) * 16)
    spare = most - cap
    lanes = -(-(cap + 1) // LANES) * LANES
    gain_one_row, gain_two_row = gain_one.reshape(1, -1), gain_two.reshape(1, -1)

    slot_row, slot_col, ask = route(token_ids, me.reshape(1), seq_len, opening, shard, owners, cap, lanes)
    asked = lax.all_to_all(ask.reshape(owners, lanes), "vocab", split_axis=0, concat_axis=0, tiled=True)
    asked = jnp.take(asked, me ^ jnp.arange(owners), axis=0)
    base = me * shard
    by_x = swap(asked, "dp", 1)
    by_y = swap(jnp.stack([asked, by_x]), "dp", 2)
    asked_all = jnp.stack([asked, by_x, by_y[0], by_y[1]])
    overflow = jnp.max(asked_all[:, :, lanes - 1]) > 0 if spare else None
    targets = jnp.where(asked_all[:, :, :cap] >= 0, asked_all[:, :, :cap] - base, -1)
    picked = fetch_rows(table, jnp.where(asked[:, :cap] >= 0, asked[:, :cap] - base, -1))
    rows = exchange(picked)
    rel_bias, cotangent, targets = after([rel_bias, cotangent, targets], rows[1])
    band = make_band(rel_bias)
    cot_t = cotangent.T
    lists = [targets[n, low:high] for n, low, high in arrival_order(owners)]
    lists = jnp.concatenate(lists, axis=0)
    plan = place_plan(lists, shard)

    def spare_rows(step, _):
        slot, asked_more = spare_slots(token_ids + step, seq_len, opening, shard, owners, cap, spare)
        found = jnp.take(table, jnp.clip(asked_more - base, 0, shard - 1), axis=0)
        came = lax.all_to_all(found, "vocab", split_axis=0, concat_axis=0, tiled=True).reshape(-1, width)
        more = jnp.take(came, jnp.clip(slot, 0, owners * spare - 1), axis=0)
        return jnp.where((slot < owners * spare)[:, None], more, jnp.zeros((), BF))

    more = None
    if spare:
        more = lax.fori_loop(0, overflow.astype(jnp.int32), spare_rows, jnp.zeros((tokens, width), BF))
    held = after([rows[0], band, cot_t, *plan])
    rows[0], band, cot_t, plan = held[0], held[1], held[2], held[3:]

    x, hidden, q, k, v = project(slot_col, more, rows, gain_one_row, w_query, w_key, w_value)

    ctx, probs = attend(q, k, v, seq_lengths, rel_bias, band)
    mid, act, d_pre, hidden_t, d_mid, d_att, d_ctx, gain_two_part = middle_part(
        x, ctx, cotangent, gain_two_row, w_out, w_in, w_down
    )
    packed = owners == 8 and groups == 4 and (width // groups) % 64 == 0 and (w_in.shape[1] // owners) % LANES == 0
    place_dp = lax.axis_index("dp")
    x_bit, y_bit, z_high, z_low = place_dp % 2, place_dp // 2, me // 4, (me // 2) % 2
    if packed:
        in_keep, in_send = in_grads(core, hidden_t, d_pre, groups, owners)
        down_keep, down_send = down_grads(core, cot_t, after(act, in_send), groups, owners)
        in_came = swap(in_send, "vocab", 1)
        down_send = after(down_send, in_came)
        down_came = swap(down_send, "vocab", 1)
        out_part = square_part(after(d_att, down_send), ctx, owners)
        down_came = after(down_came, out_part)
        in_shares, down_shares = Shares(in_keep, in_came), Shares(down_keep, down_came)
        in_sent, down_sent = in_shares.send(1, x_bit), down_shares.send(0, y_bit)
        d_ctx = after(d_ctx, in_sent, down_sent, out_part)
        in_came, down_came = swap(in_sent, "dp", 1), swap(down_sent, "dp", 2)
    dq, dk, dv, lines = attend_back(q, k, v, ctx, d_ctx, probs)
    if packed:
        in_came, down_came = after([in_came, down_came], dq)
        in_shares.add(in_came)
        down_shares.add(down_came)
        in_sent, down_sent = in_shares.send(0, y_bit), down_shares.send(1, x_bit)
        qk_keep, qk_send = square_grads(core, [dq, dk], [hidden, hidden], None, groups, owners)
        vo_keep, vo_send = square_grads(core, [dv], [hidden], out_part, groups, owners)
        qk_came, vo_came = swap(qk_send, "vocab", 1), swap(vo_send, "vocab", 1)
        d_mid = after(d_mid, in_sent, down_sent, qk_send, vo_send)
        in_came, down_came = swap(in_sent, "dp", 2), swap(down_sent, "dp", 1)
    row_grad, evens, odds = rows_back(
        slot_row, x, d_mid, dq, dk, dv, gain_one_row, w_query, w_key, w_value, lines, gain_two_part, owners, cap
    )

    if packed:
        odds, *evens = after([odds, *evens], in_came, down_came)
        along = pair_blocks(evens, odds, swap(odds, "vocab", 1))
        pair = 2 * cap

        by_one, by_two = swap(along[1], "vocab", 2), swap(along[2], "vocab", 4)
        own_x, own_y = around(along[0])
        qk_came, vo_came = after([qk_came, vo_came], row_grad)
        qk_shares, vo_shares = Shares(qk_keep, qk_came), Shares(vo_keep, vo_came)
        qk_came, vo_came = swap(qk_shares.send(1, x_bit), "dp", 1), swap(vo_shares.send(0, y_bit), "dp", 2)
        in_shares.add(in_came)
        down_shares.add(down_came)
        wide_sent = jnp.concatenate([in_shares.send(2, z_high), down_shares.send(2, z_high)], axis=4)
        in_rows = in_keep.shape[2]
        qk_came, vo_came = after([qk_came, vo_came], own_x, own_y)
        qk_shares.add(qk_came)
        vo_shares.add(vo_came)
        qk_came, vo_came = swap(qk_shares.send(0, y_bit), "dp", 2), swap(vo_shares.send(1, x_bit), "dp", 1)
        by_three = swap(after(along[3], by_two), "vocab", 6)
        held = (by_one, by_two, own_x, own_y, qk_came, vo_came, wide_sent)
        by_one, by_two, own_x, own_y, qk_came, vo_came, wide_sent = lax.optimization_barrier(held)

        mid_rows = jnp.concatenate([by_one[:pair], by_two[:pair]], axis=0)
        mid_x, mid_y = around(mid_rows)
        qk_shares.add(qk_came)
        vo_shares.add(vo_came)
        mixed_out = mix(after(mid, by_one), act, w_down)
        held = (by_three, mid_x, mid_y, own_x, own_y, wide_sent, mixed_out)
        by_three, mid_x, mid_y, own_x, own_y, wide_sent, mixed_out = lax.optimization_barrier(held)

        far_low = swap(jnp.concatenate([own_x[:cap], mid_x[:pair]], axis=0), "dp", 2)
        far_high = swap(jnp.concatenate([own_y[cap:], mid_y[pair:]], axis=0), "dp", 1)
        small = whole_value(along[1][pair:])
        small = sum_of(
            sum_of(small, whole_value(by_one[pair:])), sum_of(whole_value(by_two[pair:]), whole_value(by_three[pair:]))
        )
        last_sent, small = with_small(by_three[:pair], small)
        last_x, last_y = swap(last_sent, "dp", 1), swap(by_three, "dp", 2)
        wide_came = swap(wide_sent, "vocab", 4)
        low_sent, small = with_small(last_x[:cap], sum_of(small, whole_value(last_x[pair:])))
        last_low, last_high = swap(low_sent, "dp", 2), swap(last_y[cap:pair], "dp", 1)
        wide_came = after(wide_came, last_low, last_high)
        qk_shares.terms[-1] = after(qk_shares.terms[-1], last_x, last_y)
        vo_shares.terms[-1] = after(vo_shares.terms[-1], last_x, last_y)
        square_sent = [
            jnp.concatenate([a.part({2: z_high ^ (k // 2), 3: z_low ^ (k % 2)}) for a in (qk_shares, vo_shares)], axis=0)
            for k in range(1, 4)
        ]
        square_sent = after(square_sent, last_low, last_high)
        square_came = [swap(block, "vocab", 2 * k) for k, block in enumerate(square_sent, 1)]
        in_shares.add(wide_came[..., :in_rows, :])
        down_shares.add(wide_came[..., in_rows:, :])
        wide_sent = jnp.concatenate([in_shares.send(3, z_low), down_shares.send(3, z_low)], axis=4)
        wide_came = swap(wide_sent, "vocab", 2)
        small = sum_of(small, whole_value(last_low[cap:]))

        placed = [along[0], own_x, own_y, mid_rows, mid_x, mid_y, by_three, last_x, last_y]
        placed += [far_low, far_high, last_low, last_high]
        table_grad = place_rows(plan, placed, shard, cap)
        own_z = {2: z_high, 3: z_low}
        wide = [jnp.concatenate([in_shares.part(own_z), down_shares.part(own_z)], axis=0), wide_came]
        wide = [a.reshape(-1, a.shape[-1]) for a in wide]
        square = [jnp.concatenate([qk_shares.part(own_z), vo_shares.part(own_z)], axis=0)] + square_came
    else:
        mixed_out = mix(mid, act, w_down)
        body_rows = owners // 2 * cap
        blocks = [b for both in zip(evens, jnp.split(odds[:body_rows], owners // 2, axis=0)) for b in both]
        arrived = jnp.concatenate(exchange(blocks), axis=0)
        placed = across(arrived, *around(arrived))
        small = whole_value(odds[body_rows:])
        for axis in ("vocab", "dp"):
            bit = 1
            while bit < lax.axis_size(axis):
                small = sum_of(small, [swap(a, axis, bit) for a in small])
                bit *= 2
        table_grad = place_rows(plan, placed, shard, cap)

    def add_spare(step, total):
        slot, asked_more = spare_slots(token_ids + step, seq_len, opening, shard, owners, cap, spare)
        sent = jnp.zeros((owners * spare + 1, width), F32).at[slot].add(row_grad)[:-1]
        sent = sent.astype(BF).reshape(owners, spare, width)
        came = lax.all_to_all(sent, "vocab", split_axis=0, concat_axis=0, tiled=True)
        target = jnp.where(asked_more >= 0, asked_more - base, shard).reshape(-1)
        part = jnp.zeros((shard, width), F32).at[target].add(came.reshape(-1, width).astype(F32), mode="drop")
        for bit in (1, 2):
            part = part + swap(part, "dp", bit)
        return total + part

    if spare:
        table_grad = lax.fori_loop(0, overflow.astype(jnp.int32), add_spare, table_grad)

    if packed:
        in_grad, down_grad, query_grad, key_grad, value_grad, out_grad = finish(wide, square, width // groups, width // owners)
    else:
        def spread(left, right):
            full = jnp.einsum("td,te->de", left, right, preferred_element_type=F32)
            part = lax.psum_scatter(full, "vocab", scatter_dimension=1, tiled=True).astype(BF)
            return lax.psum_scatter(part, "dp", scatter_dimension=0, tiled=True).astype(F32)

        query_grad, key_grad, value_grad = spread(hidden, dq), spread(hidden, dk), spread(hidden, dv)
        out_grad = spread(ctx, d_att)
        in_grad = spread(hidden_t.T, d_pre)
        down_grad = spread(act, cotangent)

    gains, bias = small
    gain_one_grad, gain_two_grad = gains[0], gains[1]
    bias_grad = bias[:, : rel_bias.shape[0]].T
    return (
        mixed_out,
        row_grad,
        table_grad,
        gain_one_grad,
        query_grad,
        key_grad,
        value_grad,
        out_grad,
        gain_two_grad,
        in_grad,
        down_grad,
        bias_grad,
    )


def solution(mesh):
    spread = ("dp", "vocab")
    placed = (
        P(spread),
        P(spread),
        P("vocab", None),
        P(),
        P(),
        P(),
        P(),
        P(),
        P(),
        P(),
        P(),
        P(),
        P(spread, None),
    )
    return jax.shard_map(
        body,
        mesh=mesh,
        in_specs=placed,
        out_specs=(
            P(spread, None),
            P(spread, None),
            P("vocab", None),
            P(),
            P("dp", "vocab"),
            P("dp", "vocab"),
            P("dp", "vocab"),
            P("dp", "vocab"),
            P(),
            P("dp", "vocab"),
            P("dp", "vocab"),
            P(),
        ),
        check_vma=False,
    )
```

```python
from functools import partial

import jax
import jax.numpy as jnp
import numpy as np
from jax import lax
from jax.experimental import pallas as pl
from jax.experimental.pallas import tpu as pltpu
from jax.sharding import PartitionSpec as P

EPS = 1e-06
PRECISE = lax.Precision.HIGHEST
MASKED = -1e30
THRESHOLDS = (12, 16, 23, 32, 46, 64, 91)
LANES = 128
NOWHERE = 1 << 30
BUCKETS = 32
PER_STEP = 2
PER_FETCH = 2
BF = jnp.bfloat16
F32 = jnp.float32
NN = (((1,), (0,)), ((), ()))
NT = (((1,), (1,)), ((), ()))
TN = (((0,), (0,)), ((), ()))


def mm(left, right, dims=NN):
    return lax.dot_general(left, right, dims, preferred_element_type=F32)


def params(mib=56):
    return pltpu.CompilerParams(vmem_limit_bytes=mib << 20)


def cost(macs, moved):
    return pl.CostEstimate(flops=2 * macs, bytes_accessed=moved, transcendentals=0)


def whole(shape):
    return pl.BlockSpec(shape, lambda *_: (0,) * len(shape), pipeline_mode=pl.Buffered(1))


def bucket_of(offset):
    distance = np.abs(offset)
    far = 8 + sum((distance >= t).astype(np.int32) for t in THRESHOLDS)
    return np.where(offset > 0, 16, 0) + np.where(distance < 8, distance, far)


def band_offsets():
    lane = np.arange(4 * LANES)
    return np.where(lane < 3 * LANES, lane, lane - 4 * LANES) - LANES


def band_onehot(buckets):
    return (bucket_of(band_offsets())[:, None] == np.arange(buckets)[None, :]).astype(np.float32)


def route_kernel(me_ref, ids_row_ref, slot_row_ref, slot_col_ref, ask_ref, *, seq_len, opening, shard, owners, cap, width):
    me = me_ref[0]
    tokens = ids_row_ref.shape[1]
    ids_row = ids_row_ref[...]
    parts = [jnp.broadcast_to(ids_row[:, low : low + LANES], (LANES, LANES)) for low in range(0, tokens, LANES)]
    ids_col = jnp.concatenate([part.T[:, :1] for part in parts], axis=0)
    owner_row, owner_col = jnp.zeros_like(ids_row), jnp.zeros_like(ids_col)
    for o in range(1, owners):
        owner_row += (ids_row >= o * shard).astype(jnp.int32)
        owner_col += (ids_col >= o * shard).astype(jnp.int32)

    def places(shape, axis):
        t = lax.broadcasted_iota(jnp.int32, shape, axis)
        within = lax.rem(t, seq_len)
        repeated = (within < opening) & (t >= seq_len)
        return jnp.where(within < opening, within, t), jnp.logical_not(repeated)

    at_row, first_row = places((1, tokens), 1)
    at_col, first_col = places((tokens, 1), 0)
    key_row, key_col = ids_row * tokens + at_row, ids_col * tokens + at_col
    low_row, low_col = owner_row * (shard * tokens), owner_col * (shard * tokens)
    given_row = jnp.where(first_row, key_row, -1)
    given_col = jnp.where(first_col, key_col, -1)
    rank_col = jnp.sum(((given_row >= low_col) & (given_row < key_col)).astype(jnp.int32), axis=1, keepdims=True)
    rank_row = jnp.sum(((given_col >= low_row) & (given_col < key_row)).astype(jnp.int32), axis=0, keepdims=True)
    slot_row_ref[...] = jnp.where(rank_row < cap, (owner_row ^ me) * cap + rank_row, NOWHERE)
    slot_col_ref[...] = jnp.where(rank_col < cap, (owner_col ^ me) * cap + rank_col, NOWHERE)
    over = (jnp.max(rank_row) >= cap).astype(jnp.int32)
    place_col = jnp.where(first_col & (rank_col < cap), owner_col * width + rank_col, -1)
    step = 4 * LANES
    for start in range(0, owners * width, step):
        lane = lax.broadcasted_iota(jnp.int32, (1, step), 1) + start
        asked = jnp.sum(jnp.where(place_col == lane, ids_col + 1, 0), axis=0, keepdims=True) - 1
        ask_ref[:, start : start + step] = jnp.where(lax.rem(lane, width) == width - 1, over, asked)


def route(token_ids, me, seq_len, opening, shard, owners, cap, width):
    tokens = token_ids.shape[0]
    body = partial(route_kernel, seq_len=seq_len, opening=opening, shard=shard, owners=owners, cap=cap, width=width)
    return pl.pallas_call(
        body,
        in_specs=[pl.BlockSpec(memory_space=pltpu.SMEM), pl.BlockSpec(memory_space=pltpu.VMEM)],
        out_shape=[
            jax.ShapeDtypeStruct((1, tokens), jnp.int32),
            jax.ShapeDtypeStruct((tokens, 1), jnp.int32),
            jax.ShapeDtypeStruct((1, owners * width), jnp.int32),
        ],
        compiler_params=params(),
        name="route",
    )(me, token_ids.reshape(1, -1))


def windows(lists, tile, shard, window):
    cap = lists.shape[1]
    edges = jnp.arange(pl.cdiv(shard, tile) + 1, dtype=jnp.int32) * tile
    known = jnp.where(lists < 0, NOWHERE, lists)
    below = jnp.sum((known[:, None, :] < edges[None, :, None]).astype(jnp.int32), axis=2)
    starts = jnp.minimum(below[:, :-1] // 16 * 16, cap - window)
    counts = (below[:, 1:] - starts + window - 1) // window
    return starts.T, counts.T, jnp.max(counts, axis=0)


def in_window(start, step, window, cap):
    wanted = start + step * window
    begin = pl.multiple_of(jnp.minimum(wanted, cap - window), 16)
    return begin, begin + lax.broadcasted_iota(jnp.int32, (window, 1), 0) >= wanted


def fetch_kernel(starts_ref, counts_ref, more_ref, list_ref, table_ref, out_refs, total_ref, *, tile, window, shard):
    step_rows, width = table_ref.shape
    blocks = len(out_refs)
    cap = out_refs[0].shape[0]

    @pl.when(pl.program_id(0) == 0)
    def _():
        total_ref[...] = jnp.zeros_like(total_ref)

    for sub in range(step_rows // tile):
        at = pl.program_id(0) * (step_rows // tile) + sub
        row = lax.broadcasted_iota(jnp.int32, (tile, 1), 0) + at * tile
        lane = lax.broadcasted_iota(jnp.int32, (1, tile), 1) + at * tile
        table = table_ref[sub * tile : (sub + 1) * tile, :]
        table = jnp.where(row < shard, table, jnp.zeros((), BF))
        begins = [pl.multiple_of(starts_ref[at, n], 16) for n in range(blocks)]
        wanted = [list_ref[pl.ds(n * cap + begins[n], window), :] for n in range(blocks)]
        found = mm((jnp.concatenate(wanted, axis=0) == lane).astype(F32).astype(BF), table)
        for n in range(blocks):
            total_ref[pl.ds(n * cap + begins[n], window), :] += found[n * window : (n + 1) * window]

        @pl.when(more_ref[at] > 1)
        def _():
            for n in range(blocks):
                def extra(step, carry):
                    begin, fresh = in_window(starts_ref[at, n], step, window, cap)
                    place = pl.ds(n * cap + begin, window)
                    mark = (list_ref[place, :] == lane) & fresh
                    total_ref[place, :] += mm(mark.astype(F32).astype(BF), table)
                    return carry

                lax.fori_loop(1, counts_ref[at, n], extra, 0)

    @pl.when(pl.program_id(0) == pl.num_programs(0) - 1)
    def _():
        for n in range(blocks):
            out_refs[n][...] = total_ref[n * cap : (n + 1) * cap, :].astype(BF)


def fetch_rows(table, lists):
    shard, width = table.shape
    blocks, cap = lists.shape
    tile, window = min(512, shard), min(48, cap)
    starts, counts, more = windows(lists, tile, shard, window)
    tiles = starts.shape[0]
    per_step = PER_FETCH if tiles % PER_FETCH == 0 else 1
    return pl.pallas_call(
        partial(fetch_kernel, tile=tile, window=window, shard=shard),
        grid_spec=pltpu.PrefetchScalarGridSpec(
            num_scalar_prefetch=3,
            grid=(tiles // per_step,),
            in_specs=[whole((blocks * cap, 1)), pl.BlockSpec((per_step * tile, width), lambda t, *_: (t, 0))],
            out_specs=[[whole((cap, width))] * blocks],
            scratch_shapes=[pltpu.VMEM((blocks * cap, width), F32)],
        ),
        out_shape=[[jax.ShapeDtypeStruct((cap, width), BF)] * blocks],
        compiler_params=params(),
        cost_estimate=cost(shard * width * blocks * window, 2 * (shard + blocks * cap) * width),
        name="fetch_rows",
    )(starts, counts, more, lists.reshape(-1, 1), table)[0]


def project_kernel(slot_ref, more_ref, rows_refs, gain_ref, wq_ref, wk_ref, wv_ref, x_ref, hidden_ref, q_ref, k_ref, v_ref):
    slot = slot_ref[...]
    rows = jnp.concatenate([r[...] for r in rows_refs], axis=0)
    lane = lax.broadcasted_iota(jnp.int32, (slot.shape[0], rows.shape[0]), 1)
    x = mm((lane == slot).astype(F32).astype(BF), rows)
    if more_ref is not None:
        x = x + more_ref[...].astype(F32)
    x_ref[...] = x.astype(BF)
    scale = lax.rsqrt(jnp.mean(x * x, axis=1, keepdims=True) + EPS)
    hidden = (x * scale * gain_ref[...]).astype(BF)
    hidden_ref[...] = hidden
    q_ref[...] = mm(hidden, wq_ref[...]).astype(BF)
    k_ref[...] = mm(hidden, wk_ref[...]).astype(BF)
    v_ref[...] = mm(hidden, wv_ref[...]).astype(BF)


def project(slot_col, more, rows, gain, w_query, w_key, w_value):
    tokens, width = slot_col.shape[0], gain.shape[1]
    tile = min(512, tokens)
    out = pl.BlockSpec((tile, width), lambda t: (t, 0))
    count = sum(r.shape[0] for r in rows)
    return pl.pallas_call(
        project_kernel,
        grid=(tokens // tile,),
        in_specs=[pl.BlockSpec((tile, 1), lambda t: (t, 0)), None if more is None else out, [whole(r.shape) for r in rows], whole(gain.shape)]
        + [whole(w_query.shape)] * 3,
        out_specs=[out] * 5,
        out_shape=[jax.ShapeDtypeStruct((tokens, width), BF)] * 5,
        compiler_params=params(),
        cost_estimate=cost(tokens * width * (3 * width + count), 14 * tokens * width),
        name="project",
    )(slot_col, more, rows, gain, w_query, w_key, w_value)


def band_kernel(line_ref, band_ref):
    line = jnp.broadcast_to(line_ref[0], (LANES, line_ref.shape[2]))
    band_ref[0] = pltpu.roll(line, 0, 1, stride=1, stride_axis=0)[:, : 3 * LANES]


def make_band(rel_bias):
    heads = rel_bias.shape[1]
    line = jnp.dot(band_onehot(rel_bias.shape[0]), rel_bias, precision=PRECISE).T.reshape(heads, 1, -1)
    return pl.pallas_call(
        band_kernel,
        grid=(heads,),
        in_specs=[pl.BlockSpec((1,) + line.shape[1:], lambda h: (h, 0, 0))],
        out_specs=pl.BlockSpec((1, LANES, 3 * LANES), lambda h: (h, 0, 0)),
        out_shape=jax.ShapeDtypeStruct((heads, LANES, 3 * LANES), F32),
        compiler_params=params(30),
        name="band",
    )(line)


def attend_kernel(len_ref, far_ref, q_ref, k_ref, v_ref, band_ref, ctx_ref, p_ref):
    pair = pl.program_id(1)
    q, k, v = q_ref[...], k_ref[...], v_ref[...]
    seq_len = q.shape[0]
    blocks = seq_len // LANES
    last = far_ref.shape[0] // 2 - 1
    half = lax.broadcasted_iota(jnp.int32, (1, LANES), 1) // (LANES // 2)
    key_at = lax.broadcasted_iota(jnp.int32, (1, seq_len), 1)
    mask = jnp.where(key_at < len_ref[pl.program_id(0)], 0.0, MASKED)
    none = jnp.zeros((), BF)
    ctx = jnp.zeros((seq_len, LANES), F32)
    for h in range(2):
        k_own, v_own = jnp.where(half == h, k, none), jnp.where(half == h, v, none)
        left, right = far_ref[last, 2 * pair + h], far_ref[2 * last + 1, 2 * pair + h]
        for i in range(blocks):
            raw = mm(q[i * LANES : (i + 1) * LANES], k_own, NT)
            tiles = []
            for j in range(blocks):
                cols = slice(j * LANES, (j + 1) * LANES)
                d = j - i
                if abs(d) <= 1:
                    tiles.append(raw[:, cols] + band_ref[h, :, (d + 1) * LANES : (d + 2) * LANES] + mask[:, cols])
                else:
                    tiles.append(raw[:, cols] + (mask[:, cols] + (left if d < 0 else right)))
            scores = jnp.concatenate(tiles, axis=1)
            grown = jnp.exp(scores - jnp.max(scores, axis=1, keepdims=True))
            total = jnp.sum(grown, axis=1, keepdims=True)
            p_ref[0, h, i * LANES : (i + 1) * LANES, :] = (grown * (1.0 / total)).astype(BF)
        ctx = ctx + mm(p_ref[0, h], v_own)
    ctx_ref[...] = ctx.astype(BF)


def attend(q, k, v, lengths, rel_bias, band):
    seqs, heads = lengths.shape[0], rel_bias.shape[1]
    tokens, width = q.shape
    seq_len = tokens // seqs
    block = pl.BlockSpec((seq_len, LANES), lambda s, p, *_: (s, p))
    return pl.pallas_call(
        attend_kernel,
        grid_spec=pltpu.PrefetchScalarGridSpec(
            num_scalar_prefetch=2,
            grid=(seqs, heads // 2),
            in_specs=[block] * 3 + [pl.BlockSpec((2,) + band.shape[1:], lambda s, p, *_: (p, 0, 0))],
            out_specs=[block, pl.BlockSpec((1, 2, seq_len, seq_len), lambda s, p, *_: (s, p, 0, 0))],
        ),
        out_shape=[
            jax.ShapeDtypeStruct((tokens, width), BF),
            jax.ShapeDtypeStruct((seqs, heads, seq_len, seq_len), BF),
        ],
        compiler_params=params(),
        cost_estimate=cost(tokens * seq_len * width * 8, 2 * tokens * seq_len * heads),
        name="attend",
    )(lengths, rel_bias, q, k, v, band)


def attend_back_kernel(q_ref, k_ref, v_ref, ctx_ref, do_ref, p_ref, dq_ref, dk_ref, dv_ref, line_ref, ds_ref, band_ref, far_ref):
    seq_at = pl.program_id(1)
    q, k, v, do = q_ref[...], k_ref[...], v_ref[...], do_ref[...]
    seq_len = q.shape[0]
    blocks = seq_len // LANES
    half = lax.broadcasted_iota(jnp.int32, (1, LANES), 1) // (LANES // 2)
    none = jnp.zeros((), BF)

    @pl.when(seq_at == 0)
    def _():
        band_ref[...] = jnp.zeros_like(band_ref)
        far_ref[...] = jnp.zeros_like(far_ref)

    swing = ctx_ref[...].astype(F32) * do.astype(F32)
    row_half = lax.broadcasted_iota(jnp.int32, (LANES, 1), 0) // (LANES // 2)
    q_t, do_t = (a.astype(F32).T.astype(BF) for a in (q, do))
    dq = jnp.zeros((seq_len, LANES), F32)
    dk_t = dv_t = jnp.zeros((LANES, seq_len), F32)
    for h in range(2):
        k_own, v_own = jnp.where(half == h, k, none), jnp.where(half == h, v, none)
        near = [jnp.zeros((LANES, LANES), F32) for _ in range(3)]
        far = [jnp.zeros((8, LANES), F32) for _ in range(2)]
        for i in range(blocks):
            rows = slice(i * LANES, (i + 1) * LANES)
            probs = p_ref[0, h, rows, :].astype(F32)
            swing_own = jnp.sum(jnp.where(half == h, swing[rows], 0.0), axis=1, keepdims=True)
            ds = probs * (mm(do[rows], v_own, NT) - swing_own)
            for j in range(blocks):
                d = j - i
                tile = ds[:, j * LANES : (j + 1) * LANES]
                if abs(d) <= 1:
                    near[d + 1] = near[d + 1] + tile
                else:
                    side = 0 if d < 0 else 1
                    far[side] = far[side] + jnp.sum(tile.reshape(LANES // 8, 8, LANES), axis=0)
            ds_ref[rows, :] = ds.astype(BF)
        for d in range(3):
            band_ref[h, :, d * LANES : (d + 1) * LANES] += near[d]
        for side in range(2):
            far_ref[h, :, side * LANES : (side + 1) * LANES] += far[side]
        d_low = ds_ref[...]
        dk_t = dk_t + mm(jnp.where(row_half == h, q_t, none), d_low)
        dv_t = dv_t + mm(jnp.where(row_half == h, do_t, none), p_ref[0, h])
        dq = dq + mm(d_low, k_own)
    dq_ref[...], dk_ref[...], dv_ref[...] = dq.astype(BF), dk_t.T.astype(BF), dv_t.T.astype(BF)

    @pl.when(seq_at == pl.num_programs(1) - 1)
    def _():
        row = lax.broadcasted_iota(jnp.int32, (8, 1), 0)
        for h in range(2):
            padded = jnp.concatenate([band_ref[h], jnp.zeros((LANES, LANES), F32)], axis=1)
            turned = padded[:8]
            for start in range(8, LANES, 8):
                turned = turned + pltpu.roll(padded[start : start + 8], 4 * LANES - start, 1)
            for bit in (1, 2, 4):
                turned = jnp.where(row & bit > 0, pltpu.roll(turned, 4 * LANES - bit, 1), turned)
            line_ref[0, h : h + 1, :] = jnp.sum(turned, axis=0, keepdims=True)
            line_ref[0, 2 + h : 3 + h, : 2 * LANES] = jnp.sum(far_ref[h], axis=0, keepdims=True)


def attend_back(q, k, v, ctx, d_context, probs):
    seqs, heads, seq_len, _ = probs.shape
    tokens, width = q.shape
    pairs = heads // 2
    block = pl.BlockSpec((seq_len, LANES), lambda p, s: (s, p))
    return pl.pallas_call(
        attend_back_kernel,
        grid=(pairs, seqs),
        in_specs=[block] * 5 + [pl.BlockSpec((1, 2, seq_len, seq_len), lambda p, s: (s, p, 0, 0))],
        out_specs=[block] * 3 + [pl.BlockSpec((1, 8, 4 * LANES), lambda p, s: (p, 0, 0))],
        out_shape=[jax.ShapeDtypeStruct((tokens, width), BF)] * 3
        + [jax.ShapeDtypeStruct((heads // 2, 8, 4 * LANES), F32)],
        scratch_shapes=[
            pltpu.VMEM((seq_len, seq_len), BF),
            pltpu.VMEM((2, LANES, 3 * LANES), F32),
            pltpu.VMEM((2, 8, 2 * LANES), F32),
        ],
        compiler_params=params(),
        cost_estimate=cost(tokens * seq_len * width * 12, 2 * tokens * seq_len * heads),
        name="attend_back",
    )(q, k, v, ctx, d_context, probs)


def middle_kernel(x_ref, ctx_ref, cot_ref, gain_ref, w_out_ref, w_in_ref, w_down_ref, mid_ref, act_ref, d_pre_ref, hidden_t_ref, d_mid_ref, d_att_ref, d_ctx_ref, gain_grad_ref, *, chunk):
    mid = x_ref[...].astype(F32) + mm(ctx_ref[...], w_out_ref[...])
    gain = gain_ref[...]
    scale = lax.rsqrt(jnp.mean(mid * mid, axis=1, keepdims=True) + EPS)
    hidden_full = mid * scale * gain
    hidden = hidden_full.astype(BF)
    hidden_t_ref[...] = hidden_full.T.astype(BF)
    cot = cot_ref[...]
    mid_ref[...] = mid
    d_hidden = jnp.zeros_like(mid)
    slope = float(np.sqrt(2 / np.pi))
    for start in range(0, w_in_ref.shape[1], chunk):
        cols = slice(start, start + chunk)
        pre = mm(hidden, w_in_ref[:, cols])
        d_act = mm(cot, w_down_ref[cols, :], NT)
        square = pre * pre
        bent = jnp.tanh(slope * pre * (1.0 + 0.044715 * square))
        open_half = 0.5 + 0.5 * bent
        act = (pre * open_half).astype(BF)
        curve = (0.5 * slope) * pre * (1.0 - bent * bent) * (1.0 + (3 * 0.044715) * square)
        d_pre = (d_act * (open_half + curve)).astype(BF)
        act_ref[:, cols] = act
        d_pre_ref[:, cols] = d_pre
        d_hidden = d_hidden + mm(d_pre, w_in_ref[:, cols], NT)
    u = d_hidden * gain
    swing = jnp.mean(u * mid, axis=1, keepdims=True)
    d_mid = cot.astype(F32) + scale * u - mid * (scale * scale * scale * swing)
    d_mid_ref[...] = d_mid
    d_att = d_mid.astype(BF)
    d_att_ref[...] = d_att
    d_ctx_ref[...] = mm(d_att, w_out_ref[...], NT).astype(BF)

    @pl.when(pl.program_id(0) == 0)
    def _():
        gain_grad_ref[...] = jnp.zeros_like(gain_grad_ref)

    gain_grad_ref[...] += jnp.sum((d_hidden * mid * scale).reshape(-1, 8, mid.shape[1]), axis=0)


def middle_part(x, ctx, cot, gain, w_out, w_in, w_down):
    tokens, width = x.shape
    wide = w_in.shape[1]
    tile = min(256, tokens)
    rows = pl.BlockSpec((tile, width), lambda t: (t, 0))
    wide_rows = pl.BlockSpec((tile, wide), lambda t: (t, 0))
    return pl.pallas_call(
        partial(middle_kernel, chunk=min(768, wide)),
        grid=(tokens // tile,),
        in_specs=[rows] * 3 + [whole(a.shape) for a in (gain, w_out, w_in, w_down)],
        out_specs=[rows, wide_rows, wide_rows, pl.BlockSpec((width, tile), lambda t: (0, t)), rows, rows, rows]
        + [pl.BlockSpec((8, width), lambda t: (0, 0))],
        out_shape=[
            jax.ShapeDtypeStruct((tokens, width), F32),
            jax.ShapeDtypeStruct((tokens, wide), BF),
            jax.ShapeDtypeStruct((tokens, wide), BF),
            jax.ShapeDtypeStruct((width, tokens), BF),
            jax.ShapeDtypeStruct((tokens, width), F32),
            jax.ShapeDtypeStruct((tokens, width), BF),
            jax.ShapeDtypeStruct((tokens, width), BF),
            jax.ShapeDtypeStruct((8, width), F32),
        ],
        compiler_params=params(),
        cost_estimate=cost(tokens * width * (4 * wide + 2 * width), 4 * width * wide + 8 * tokens * (wide + width)),
        name="middle",
    )(x, ctx, cot, gain, w_out, w_in, w_down)


def mix_kernel(mid_ref, act_ref, w_down_ref, mixed_ref):
    mixed_ref[...] = (mid_ref[...] + mm(act_ref[...], w_down_ref[...])).astype(BF)


def mix(mid, act, w_down):
    tokens, width = mid.shape
    wide = act.shape[1]
    tile = min(256, tokens)
    rows = pl.BlockSpec((tile, width), lambda t: (t, 0))
    return pl.pallas_call(
        mix_kernel,
        grid=(tokens // tile,),
        in_specs=[rows, pl.BlockSpec((tile, wide), lambda t: (t, 0)), whole(w_down.shape)],
        out_specs=rows,
        out_shape=jax.ShapeDtypeStruct((tokens, width), BF),
        compiler_params=params(),
        cost_estimate=cost(tokens * width * wide, 2 * wide * (tokens + width)),
        name="mix",
    )(mid, act, w_down)


def in_grads_kernel(core_ref, hidden_t_ref, d_pre_ref, keep_ref, send_ref, part_ref):
    core = core_ref[0]
    groups, lanes = keep_ref.shape[0], keep_ref.shape[3]
    part = mm(hidden_t_ref[...], d_pre_ref[...]).astype(BF)
    for c in range(2):
        part_ref[c] = part[:, c * lanes : (c + 1) * lanes].reshape(groups, -1, lanes)
    for d in range(groups):
        keep_ref[d, 0] = part_ref[core, d]
        send_ref[d, 0] = part_ref[1 - core, d]


def in_grads(core, hidden_t, d_pre, groups, owners):
    width, tokens = hidden_t.shape
    wide = d_pre.shape[1]
    lanes, zs = wide // owners, owners // 2
    out = pl.BlockSpec((groups, 1, width // groups, lanes), lambda z, *_: (0, z, 0, 0))
    return pl.pallas_call(
        in_grads_kernel,
        grid_spec=pltpu.PrefetchScalarGridSpec(
            num_scalar_prefetch=1,
            grid=(zs,),
            in_specs=[whole(hidden_t.shape), pl.BlockSpec((tokens, 2 * lanes), lambda z, *_: (0, z))],
            out_specs=[out, out],
            scratch_shapes=[pltpu.VMEM((2, groups, width // groups, lanes), BF)],
        ),
        out_shape=[jax.ShapeDtypeStruct((groups, zs, width // groups, lanes), BF)] * 2,
        compiler_params=params(),
        cost_estimate=cost(tokens * width * wide, 2 * wide * (tokens + width)),
        name="in_grads",
    )(core, hidden_t, d_pre)


def down_grads_kernel(core_ref, cot_t_ref, act_ref, keep_ref, send_ref, parts_ref):
    core = core_ref[0]
    halves, lanes = keep_ref.shape[2], keep_ref.shape[4]
    part = mm(cot_t_ref[...], act_ref[...]).astype(BF)
    for h in range(halves):
        parts_ref[h] = part[:, h * lanes : (h + 1) * lanes].reshape(parts_ref.shape[1:])
        for z in range(keep_ref.shape[1]):
            keep_ref[0, z, h] = parts_ref[h, 2 * z + core]
            send_ref[0, z, h] = parts_ref[h, 2 * z + 1 - core]


def down_grads(core, cot_t, act, groups, owners):
    width, tokens = cot_t.shape
    wide = act.shape[1]
    lanes, zs = wide // owners, owners // 2
    halves = owners // groups
    out = pl.BlockSpec((1, zs, halves, width // owners, lanes), lambda d, *_: (d, 0, 0, 0, 0))
    return pl.pallas_call(
        down_grads_kernel,
        grid_spec=pltpu.PrefetchScalarGridSpec(
            num_scalar_prefetch=1,
            grid=(groups,),
            in_specs=[whole(cot_t.shape), pl.BlockSpec((tokens, wide // groups), lambda d, *_: (0, d))],
            out_specs=[out, out],
            scratch_shapes=[pltpu.VMEM((halves, owners, width // owners, lanes), BF)],
        ),
        out_shape=[jax.ShapeDtypeStruct((groups, zs, halves, width // owners, lanes), BF)] * 2,
        compiler_params=params(),
        cost_estimate=cost(tokens * width * wide, 2 * wide * (tokens + width)),
        name="down_grads",
    )(core, cot_t, act)


def square_kernel(left_ref, right_ref, out_ref):
    out_ref[...] = mm(left_ref[...], right_ref[...], TN).astype(BF).reshape(out_ref.shape)


def square_part(left, right, owners):
    tokens, width = left.shape
    return pl.pallas_call(
        square_kernel,
        out_shape=jax.ShapeDtypeStruct((owners, width // owners, right.shape[1]), BF),
        compiler_params=params(30),
        cost_estimate=cost(tokens * width * width, 6 * tokens * width),
        name="square_part",
    )(left, right)


def square_grads_kernel(core_ref, left_refs, right_refs, ready_ref, keep_ref, send_ref, parts_ref, *, groups, owners):
    core = core_ref[0]
    for n, (left_ref, right_ref) in enumerate(zip(left_refs, right_refs)):
        parts_ref[n] = mm(left_ref[...], right_ref[...], TN).astype(BF).reshape(parts_ref.shape[1:])
    lanes = right_refs[0].shape[1] // groups
    for z in range(owners // 2):
        for target_ref, v in ((keep_ref, 2 * z + core), (send_ref, 2 * z + 1 - core)):
            first, second = parts_ref[0, v], parts_ref[1, v] if ready_ref is None else ready_ref[v]
            for d in range(groups):
                cols = slice(d * lanes, (d + 1) * lanes)
                target_ref[d, z] = jnp.concatenate([first[:, cols], second[:, cols]], axis=1)


def square_grads(core, lefts, rights, ready, groups, owners):
    tokens, width = rights[0].shape
    shape = (groups, owners // 2, width // owners, 2 * width // groups)
    vmem = pl.BlockSpec(memory_space=pltpu.VMEM)
    return pl.pallas_call(
        partial(square_grads_kernel, groups=groups, owners=owners),
        in_specs=[pl.BlockSpec(memory_space=pltpu.SMEM), [vmem] * len(lefts), [vmem] * len(lefts)]
        + [None if ready is None else vmem],
        out_shape=[jax.ShapeDtypeStruct(shape, BF)] * 2,
        scratch_shapes=[pltpu.VMEM((len(lefts), owners, width // owners, width), BF)],
        compiler_params=params(30),
        cost_estimate=cost(len(lefts) * tokens * width * width, 12 * tokens * width),
        name="square_grads",
    )(core, lefts, rights, ready)


SMALL = 16


def low_parts(value, high_of):
    gains, bias = value
    gains_high, bias_high = high_of(gains), high_of(bias)
    bias = jnp.concatenate([bias_high, bias - bias_high], axis=1)
    bias = jnp.concatenate([bias, jnp.zeros((SMALL - 4, gains.shape[1] - bias.shape[1]), F32)], axis=1)
    return jnp.concatenate([gains_high, gains - gains_high, bias], axis=0).astype(BF)


def whole_value(parts):
    parts = parts.astype(F32)
    return parts[0:2] + parts[2:4], parts[4:SMALL, :LANES] + parts[4:SMALL, LANES : 2 * LANES]


def sum_of(first, second):
    return tuple(a + b for a, b in zip(first, second))


def round_low(value):
    return value.astype(BF).astype(F32)


def small_value(lines_ref, onehot_ref, gain_one_part, gain_two_part):
    pairs = lines_ref.shape[0]
    near = jnp.concatenate([lines_ref[p, 0:2, :] for p in range(pairs)], axis=0)
    far = jnp.concatenate([lines_ref[p, 2:4, : 2 * LANES] for p in range(pairs)], axis=0)
    bias = lax.dot_general(near, onehot_ref[...], NN, precision=PRECISE, preferred_element_type=F32)
    lane = lax.broadcasted_iota(jnp.int32, (1, LANES), 1)
    left = jnp.sum(far[:, :LANES], axis=1, keepdims=True)
    right = jnp.sum(far[:, LANES:], axis=1, keepdims=True)
    bias = bias + jnp.where(lane == BUCKETS // 2 - 1, left, 0.0) + jnp.where(lane == BUCKETS - 1, right, 0.0)
    gains = [jnp.sum(g, axis=0, keepdims=True) for g in (gain_one_part, gain_two_part)]
    return jnp.concatenate(gains, axis=0), bias


def rows_kernel(slot_ref, x_ref, d_mid_ref, dq_ref, dk_ref, dv_ref, gain_ref, wq_ref, wk_ref, wv_ref, lines_ref, onehot_ref, gain_two_ref, row_ref, even_refs, odd_ref, held_ref, gain_grad_ref):
    d_hidden = mm(dq_ref[...], wq_ref[...], NT) + mm(dk_ref[...], wk_ref[...], NT) + mm(dv_ref[...], wv_ref[...], NT)
    x = x_ref[...].astype(F32)
    scale = lax.rsqrt(jnp.mean(x * x, axis=1, keepdims=True) + EPS)
    u = d_hidden * gain_ref[...]
    swing = jnp.mean(u * x, axis=1, keepdims=True)
    row = d_mid_ref[...] + scale * u - x * (scale * scale * scale * swing)
    row_ref[...] = row
    at = pl.program_id(0)

    @pl.when(at == 0)
    def _():
        gain_grad_ref[...] = jnp.zeros_like(gain_grad_ref)

    gain_grad_ref[...] += jnp.sum((d_hidden * x * scale).reshape(-1, 8, x.shape[1]), axis=0)
    tile = row.shape[0]
    held_ref[pl.ds(pl.multiple_of(at * tile, tile), tile), :] = row.astype(BF)

    @pl.when(at == pl.num_programs(0) - 1)
    def _():
        slot, held = slot_ref[...], held_ref[...]
        cap, evens = even_refs[0].shape[0], len(even_refs)
        order = [2 * n for n in range(evens)] + [2 * n + 1 for n in range(evens)]
        line = lax.broadcasted_iota(jnp.int32, (cap, slot.shape[1]), 0)
        together = min(len(order), 8)
        for low in range(0, len(order), together):
            places = jnp.concatenate([line + k * cap for k in order[low : low + together]], axis=0)
            sent = mm((places == slot).astype(F32).astype(BF), held).astype(BF)
            for n in range(together):
                part, at_n = sent[n * cap : (n + 1) * cap], low + n
                if at_n < evens:
                    even_refs[at_n][...] = part
                else:
                    odd_ref[(at_n - evens) * cap : (at_n - evens + 1) * cap, :] = part
        small = small_value(lines_ref, onehot_ref, gain_grad_ref[...], gain_two_ref[...])
        odd_ref[evens * cap :, :] = low_parts(small, round_low)


def rows_back(slot_row, x, d_mid, dq, dk, dv, gain, w_query, w_key, w_value, lines, gain_two_part, owners, cap):
    tokens, width = x.shape
    onehot = jnp.asarray(band_onehot(LANES))
    half = owners // 2
    tile = min(256, tokens)
    rows = pl.BlockSpec((tile, width), lambda t: (t, 0))
    return pl.pallas_call(
        rows_kernel,
        grid=(tokens // tile,),
        in_specs=[whole(slot_row.shape)] + [rows] * 5 + [whole(gain.shape)] + [whole(w_query.shape)] * 3
        + [whole(a.shape) for a in (lines, onehot, gain_two_part)],
        out_specs=[rows, [whole((cap, width))] * half, whole((half * cap + SMALL, width))],
        out_shape=[
            jax.ShapeDtypeStruct((tokens, width), F32),
            [jax.ShapeDtypeStruct((cap, width), BF)] * half,
            jax.ShapeDtypeStruct((half * cap + SMALL, width), BF),
        ],
        scratch_shapes=[pltpu.VMEM((tokens, width), BF), pltpu.VMEM((8, width), F32)],
        compiler_params=params(),
        cost_estimate=cost(tokens * width * (3 * width + owners * cap), 20 * tokens * width),
        name="rows_back",
    )(slot_row, x, d_mid, dq, dk, dv, gain, w_query, w_key, w_value, lines, onehot, gain_two_part)


def plan_kernel(starts_ref, list_ref, plan_ref, *, blocks, window):
    at = pl.program_id(0)
    cap = list_ref.shape[0] // blocks
    wanted = [list_ref[pl.ds(n * cap + pl.multiple_of(starts_ref[at, n], 16), window), :] for n in range(blocks)]
    wanted = jnp.concatenate(wanted, axis=0)
    for low in range(0, wanted.shape[0], LANES):
        part = jnp.broadcast_to(wanted[low : low + LANES], (min(LANES, wanted.shape[0] - low), LANES))
        plan_ref[0, :, low : low + LANES] = part.T[:1]


def place_plan(lists, shard):
    blocks, cap = lists.shape
    tile, window = min(256, shard), min(32, cap)
    starts, counts, more = windows(lists, tile, shard, window)
    tiles = pl.cdiv(shard, tile)
    column = lists.reshape(-1, 1)
    plan = pl.pallas_call(
        partial(plan_kernel, blocks=blocks, window=window),
        grid_spec=pltpu.PrefetchScalarGridSpec(
            num_scalar_prefetch=1,
            grid=(tiles,),
            in_specs=[whole(column.shape)],
            out_specs=pl.BlockSpec((1, 1, blocks * window), lambda t, *_: (t, 0, 0)),
        ),
        out_shape=jax.ShapeDtypeStruct((tiles, 1, blocks * window), jnp.int32),
        compiler_params=params(30),
        name="place_plan",
    )(starts, column)
    return starts, counts, more, plan, column


def place_kernel(starts_ref, counts_ref, more_ref, plan_ref, list_ref, rows_refs, out_ref, list_held, list_sem, *, tile, window, cap):
    per_step = plan_ref.shape[0]
    places = [(ref, low) for ref in rows_refs for low in range(0, ref.shape[0] // cap * cap, cap)]
    for sub in range(per_step):
        at = pl.program_id(0) * per_step + sub
        out_rows = slice(sub * tile, (sub + 1) * tile)
        row = lax.broadcasted_iota(jnp.int32, (tile, 1), 0) + at * tile
        held = []
        for n, (rows_ref, low) in enumerate(places):
            held.append(rows_ref[pl.ds(low + pl.multiple_of(starts_ref[at, n], 16), window), :])
        out_ref[out_rows, :] = mm((row == plan_ref[sub]).astype(F32).astype(BF), jnp.concatenate(held, axis=0))

    for sub in range(per_step):
        at = pl.program_id(0) * per_step + sub
        out_rows = slice(sub * tile, (sub + 1) * tile)

        @pl.when(more_ref[at] > 1)
        def _():
            copy = pltpu.make_async_copy(list_ref, list_held, list_sem)
            copy.start()
            copy.wait()
            lane = lax.broadcasted_iota(jnp.int32, (1, tile), 1) + at * tile
            for n, (rows_ref, low) in enumerate(places):
                def extra(step, carry):
                    begin, fresh = in_window(starts_ref[at, n], step, window, cap)
                    own = (list_held[pl.ds(n * cap + begin, window), :] == lane) & fresh
                    rows = rows_ref[pl.ds(low + begin, window), :]
                    out_ref[out_rows, :] += mm(own.astype(F32).astype(BF), rows, TN)
                    return carry

                lax.fori_loop(1, counts_ref[at, n], extra, 0)


def place_rows(plan, rows, shard, cap):
    width = rows[0].shape[1]
    starts, counts, more, lanes, column = plan
    tile, window = min(256, shard), min(32, cap)
    per_step = PER_STEP if starts.shape[0] % PER_STEP == 0 else 1
    return pl.pallas_call(
        partial(place_kernel, tile=tile, window=window, cap=cap),
        grid_spec=pltpu.PrefetchScalarGridSpec(
            num_scalar_prefetch=3,
            grid=(starts.shape[0] // per_step,),
            in_specs=[
                pl.BlockSpec((per_step, 1, lanes.shape[2]), lambda t, *_: (t, 0, 0)),
                pl.BlockSpec(memory_space=pl.ANY),
                [whole(r.shape) for r in rows],
            ],
            out_specs=pl.BlockSpec((per_step * tile, width), lambda t, *_: (t, 0)),
            scratch_shapes=[pltpu.VMEM(column.shape, jnp.int32), pltpu.SemaphoreType.DMA],
        ),
        out_shape=jax.ShapeDtypeStruct((shard, width), F32),
        compiler_params=params(30),
        cost_estimate=cost(shard * width * lanes.shape[2], 4 * shard * width + 2 * column.shape[0] * width),
        name="place_rows",
    )(starts, counts, more, lanes, column, rows)


def pair_kernel(even_refs, own_ref, came_ref, out_refs):
    cap = even_refs[0].shape[0]
    rows = len(even_refs) * cap
    small = sum_of(whole_value(own_ref[rows:, :]), whole_value(came_ref[rows:, :]))
    parts = low_parts(small, round_low)
    for n, out_ref in enumerate(out_refs):
        out_ref[:cap, :] = even_refs[n][...]
        out_ref[cap : 2 * cap, :] = came_ref[n * cap : (n + 1) * cap, :]
        if n > 0:
            out_ref[2 * cap :, :] = parts


def pair_blocks(evens, own, came):
    cap, width = evens[0].shape
    shapes = [(2 * cap, width)] + [(2 * cap + SMALL, width)] * (len(evens) - 1)
    return pl.pallas_call(
        pair_kernel,
        out_shape=[[jax.ShapeDtypeStruct(shape, BF) for shape in shapes]],
        compiler_params=params(),
        cost_estimate=cost(1, 1),
        name="pair_blocks",
    )(evens, own, came)[0]


def swap(value, axis, bit):
    count = lax.axis_size(axis)
    return lax.ppermute(value, axis, [(i, i ^ bit) for i in range(count)])


def arrival_order(owners):
    if owners != 8:
        return [(n, 0, owners) for n in range(4)]
    order = [(n, low, high) for low, high in ((0, 2), (2, 6), (6, 8)) for n in range(3)]
    return order + [(3, 0, 1), (3, 2, 4), (3, 1, 2), (3, 4, 6), (3, 6, 7), (3, 7, 8)]


def exchange(blocks):
    owners = lax.axis_size("vocab")
    if owners <= 8:
        return [blocks[0]] + [swap(blocks[k], "vocab", k) for k in range(1, owners)]
    order = lax.axis_index("vocab") ^ jnp.arange(owners)
    sent = jnp.take(jnp.stack(blocks), order, axis=0)
    came = lax.all_to_all(sent, "vocab", split_axis=0, concat_axis=0, tiled=True)
    return list(jnp.take(came, order, axis=0))


def around(block):
    return swap(block, "dp", 1), swap(block, "dp", 2)


def across(block, by_x, by_y):
    half = block.shape[0] // 2
    return [block, by_x, by_y, swap(by_x[:half], "dp", 2), swap(by_y[half:], "dp", 1)]


class Shares:
    def __init__(self, *terms):
        self.terms = [t.reshape((2, 2, 2, 2, -1, t.shape[-1])) for t in terms]
        self.bits = {}

    def half(self, term, bits):
        starts = [bits.get(axis, 0) if size == 2 and axis < 4 else 0 for axis, size in enumerate(term.shape)]
        sizes = [1 if axis in bits else size for axis, size in enumerate(term.shape)]
        return lax.dynamic_slice(term, starts, sizes).astype(F32)

    def send(self, axis, at):
        sent = sum(self.half(t, {**self.bits, axis: 1 - at}) for t in self.terms).astype(BF)
        self.bits[axis] = at
        return sent

    def add(self, came):
        self.terms.append(came)

    def part(self, bits):
        total = sum(self.half(t, {**self.bits, **bits}) for t in self.terms).astype(BF)
        return total.reshape(total.shape[-2:])


def with_small(rows, small):
    parts = low_parts(small, lambda value: lax.reduce_precision(value, 8, 7))
    return jnp.concatenate([rows, parts], axis=0), whole_value(parts)


def after(value, *others):
    if isinstance(value, (list, tuple)):
        return list(lax.optimization_barrier(tuple(value) + others)[: len(value)])
    return lax.optimization_barrier((value,) + others)[0]


def finish_kernel(wide_refs, square_refs, in_ref, down_ref, q_ref, k_ref, v_ref, o_ref):
    wide, square = (sum(ref[...].astype(F32) for ref in refs) for refs in (wide_refs, square_refs))
    rows, lanes, low = down_ref.shape[1], wide.shape[1], in_ref.shape[0]
    in_ref[...] = wide[:low]
    for n in range(down_ref.shape[0] // lanes):
        down_ref[n * lanes : (n + 1) * lanes, :] = wide[low : low + rows].T
        low += rows
    for n, (first_ref, second_ref) in enumerate(((q_ref, k_ref), (v_ref, o_ref))):
        turned = square[n * rows : (n + 1) * rows].T
        first_ref[...] = turned[: q_ref.shape[0]]
        second_ref[...] = turned[q_ref.shape[0] :]


def finish(wide, square, in_rows, rows):
    lanes = wide[0].shape[1]
    down = (wide[0].shape[0] - in_rows) // rows * lanes
    return pl.pallas_call(
        finish_kernel,
        out_shape=[jax.ShapeDtypeStruct((in_rows, lanes), F32), jax.ShapeDtypeStruct((down, rows), F32)]
        + [jax.ShapeDtypeStruct((lanes // 2, rows), F32)] * 4,
        compiler_params=params(24),
        cost_estimate=cost(1, 1),
        name="finish",
    )(wide, square)


def spare_slots(token_ids, seq_len, opening, shard, owners, cap, spare):
    tokens = token_ids.shape[0]
    t = jnp.arange(tokens, dtype=jnp.int32)
    within = t % seq_len
    at = jnp.where(within < opening, within, t)
    first = (within >= opening) | (t < seq_len)
    owner = token_ids // shard
    key = token_ids * tokens + at
    same = (owner[:, None] == owner[None, :]) & first[None, :] & (key[None, :] < key[:, None])
    rank = jnp.sum(same.astype(jnp.int32), axis=1) - cap
    slot = jnp.where(rank >= 0, owner * spare + rank, owners * spare)
    request = jnp.full((owners * spare + 1,), -1, jnp.int32).at[slot].set(token_ids)[:-1]
    asked = lax.all_to_all(request.reshape(owners, spare), "vocab", split_axis=0, concat_axis=0, tiled=True)
    return slot, asked


def body(
    token_ids,
    seq_lengths,
    table,
    gain_one,
    w_query,
    w_key,
    w_value,
    w_out,
    gain_two,
    w_in,
    w_down,
    rel_bias,
    cotangent,
):
    owners, groups = lax.axis_size("vocab"), lax.axis_size("dp")
    me = lax.axis_index("vocab").astype(jnp.int32)
    core = (me % 2).reshape(1)
    shard, width = table.shape
    tokens, seqs = token_ids.shape[0], seq_lengths.shape[0]
    seq_len = tokens // seqs
    heads = rel_bias.shape[1]
    most = 2 * tokens // owners
    opening = most // seqs
    cap = min(most, -(-(9 * most // 16) // 16) * 16)
    spare = most - cap
    lanes = -(-(cap + 1) // LANES) * LANES
    gain_one_row, gain_two_row = gain_one.reshape(1, -1), gain_two.reshape(1, -1)

    slot_row, slot_col, ask = route(token_ids, me.reshape(1), seq_len, opening, shard, owners, cap, lanes)
    asked = lax.all_to_all(ask.reshape(owners, lanes), "vocab", split_axis=0, concat_axis=0, tiled=True)
    asked = jnp.take(asked, me ^ jnp.arange(owners), axis=0)
    base = me * shard
    by_x = swap(asked, "dp", 1)
    by_y = swap(jnp.stack([asked, by_x]), "dp", 2)
    asked_all = jnp.stack([asked, by_x, by_y[0], by_y[1]])
    overflow = jnp.max(asked_all[:, :, lanes - 1]) > 0 if spare else None
    targets = jnp.where(asked_all[:, :, :cap] >= 0, asked_all[:, :, :cap] - base, -1)
    picked = fetch_rows(table, jnp.where(asked[:, :cap] >= 0, asked[:, :cap] - base, -1))
    rows = exchange(picked)
    rel_bias, cotangent, targets = after([rel_bias, cotangent, targets], rows[1])
    band = make_band(rel_bias)
    cot_t = cotangent.T
    lists = [targets[n, low:high] for n, low, high in arrival_order(owners)]
    lists = jnp.concatenate(lists, axis=0)
    plan = place_plan(lists, shard)

    def spare_rows(step, _):
        slot, asked_more = spare_slots(token_ids + step, seq_len, opening, shard, owners, cap, spare)
        found = jnp.take(table, jnp.clip(asked_more - base, 0, shard - 1), axis=0)
        came = lax.all_to_all(found, "vocab", split_axis=0, concat_axis=0, tiled=True).reshape(-1, width)
        more = jnp.take(came, jnp.clip(slot, 0, owners * spare - 1), axis=0)
        return jnp.where((slot < owners * spare)[:, None], more, jnp.zeros((), BF))

    more = None
    if spare:
        more = lax.fori_loop(0, overflow.astype(jnp.int32), spare_rows, jnp.zeros((tokens, width), BF))
    held = after([rows[0], band, cot_t, *plan])
    rows[0], band, cot_t, plan = held[0], held[1], held[2], held[3:]

    x, hidden, q, k, v = project(slot_col, more, rows, gain_one_row, w_query, w_key, w_value)

    ctx, probs = attend(q, k, v, seq_lengths, rel_bias, band)
    mid, act, d_pre, hidden_t, d_mid, d_att, d_ctx, gain_two_part = middle_part(
        x, ctx, cotangent, gain_two_row, w_out, w_in, w_down
    )
    packed = owners == 8 and groups == 4 and (width // groups) % 64 == 0 and (w_in.shape[1] // owners) % LANES == 0
    place_dp = lax.axis_index("dp")
    x_bit, y_bit, z_high, z_low = place_dp % 2, place_dp // 2, me // 4, (me // 2) % 2
    if packed:
        in_keep, in_send = in_grads(core, hidden_t, d_pre, groups, owners)
        down_keep, down_send = down_grads(core, cot_t, after(act, in_send), groups, owners)
        in_came = swap(in_send, "vocab", 1)
        down_send = after(down_send, in_came)
        down_came = swap(down_send, "vocab", 1)
        out_part = square_part(after(d_att, down_send), ctx, owners)
        down_came = after(down_came, out_part)
        in_shares, down_shares = Shares(in_keep, in_came), Shares(down_keep, down_came)
        in_sent, down_sent = in_shares.send(1, x_bit), down_shares.send(0, y_bit)
        d_ctx = after(d_ctx, in_sent, down_sent, out_part)
        in_came, down_came = swap(in_sent, "dp", 1), swap(down_sent, "dp", 2)
    dq, dk, dv, lines = attend_back(q, k, v, ctx, d_ctx, probs)
    if packed:
        in_came, down_came = after([in_came, down_came], dq)
        in_shares.add(in_came)
        down_shares.add(down_came)
        in_sent, down_sent = in_shares.send(0, y_bit), down_shares.send(1, x_bit)
        qk_keep, qk_send = square_grads(core, [dq, dk], [hidden, hidden], None, groups, owners)
        vo_keep, vo_send = square_grads(core, [dv], [hidden], out_part, groups, owners)
        qk_came, vo_came = swap(qk_send, "vocab", 1), swap(vo_send, "vocab", 1)
        d_mid = after(d_mid, in_sent, down_sent, qk_send, vo_send)
        in_came, down_came = swap(in_sent, "dp", 2), swap(down_sent, "dp", 1)
    row_grad, evens, odds = rows_back(
        slot_row, x, d_mid, dq, dk, dv, gain_one_row, w_query, w_key, w_value, lines, gain_two_part, owners, cap
    )

    if packed:
        odds, *evens = after([odds, *evens], in_came, down_came)
        along = pair_blocks(evens, odds, swap(odds, "vocab", 1))
        pair = 2 * cap

        by_one, by_two = swap(along[1], "vocab", 2), swap(along[2], "vocab", 4)
        own_x, own_y = around(along[0])
        qk_came, vo_came = after([qk_came, vo_came], row_grad)
        qk_shares, vo_shares = Shares(qk_keep, qk_came), Shares(vo_keep, vo_came)
        qk_came, vo_came = swap(qk_shares.send(1, x_bit), "dp", 1), swap(vo_shares.send(0, y_bit), "dp", 2)
        in_shares.add(in_came)
        down_shares.add(down_came)
        wide_sent = jnp.concatenate([in_shares.send(2, z_high), down_shares.send(2, z_high)], axis=4)
        in_rows = in_keep.shape[2]
        qk_came, vo_came = after([qk_came, vo_came], own_x, own_y)
        qk_shares.add(qk_came)
        vo_shares.add(vo_came)
        qk_came, vo_came = swap(qk_shares.send(0, y_bit), "dp", 2), swap(vo_shares.send(1, x_bit), "dp", 1)
        by_three = swap(after(along[3], by_two), "vocab", 6)
        held = (by_one, by_two, own_x, own_y, qk_came, vo_came, wide_sent)
        by_one, by_two, own_x, own_y, qk_came, vo_came, wide_sent = lax.optimization_barrier(held)

        mid_rows = jnp.concatenate([by_one[:pair], by_two[:pair]], axis=0)
        mid_x, mid_y = around(mid_rows)
        qk_shares.add(qk_came)
        vo_shares.add(vo_came)
        mixed_out = mix(after(mid, by_one), act, w_down)
        held = (by_three, mid_x, mid_y, own_x, own_y, wide_sent, mixed_out)
        by_three, mid_x, mid_y, own_x, own_y, wide_sent, mixed_out = lax.optimization_barrier(held)

        far_low = swap(jnp.concatenate([own_x[:cap], mid_x[:pair]], axis=0), "dp", 2)
        far_high = swap(jnp.concatenate([own_y[cap:], mid_y[pair:]], axis=0), "dp", 1)
        small = whole_value(along[1][pair:])
        small = sum_of(
            sum_of(small, whole_value(by_one[pair:])), sum_of(whole_value(by_two[pair:]), whole_value(by_three[pair:]))
        )
        last_sent, small = with_small(by_three[:pair], small)
        last_x, last_y = swap(last_sent, "dp", 1), swap(by_three, "dp", 2)
        wide_came = swap(wide_sent, "vocab", 4)
        low_sent, small = with_small(last_x[:cap], sum_of(small, whole_value(last_x[pair:])))
        last_low, last_high = swap(low_sent, "dp", 2), swap(last_y[cap:pair], "dp", 1)
        wide_came = after(wide_came, last_low, last_high)
        qk_shares.terms[-1] = after(qk_shares.terms[-1], last_x, last_y)
        vo_shares.terms[-1] = after(vo_shares.terms[-1], last_x, last_y)
        square_sent = [
            jnp.concatenate([a.part({2: z_high ^ (k // 2), 3: z_low ^ (k % 2)}) for a in (qk_shares, vo_shares)], axis=0)
            for k in range(1, 4)
        ]
        square_sent = after(square_sent, last_low, last_high)
        square_came = [swap(block, "vocab", 2 * k) for k, block in enumerate(square_sent, 1)]
        in_shares.add(wide_came[..., :in_rows, :])
        down_shares.add(wide_came[..., in_rows:, :])
        wide_sent = jnp.concatenate([in_shares.send(3, z_low), down_shares.send(3, z_low)], axis=4)
        wide_came = swap(wide_sent, "vocab", 2)
        small = sum_of(small, whole_value(last_low[cap:]))

        placed = [along[0], own_x, own_y, mid_rows, mid_x, mid_y, by_three, last_x, last_y]
        placed += [far_low, far_high, last_low, last_high]
        table_grad = place_rows(plan, placed, shard, cap)
        own_z = {2: z_high, 3: z_low}
        wide = [jnp.concatenate([in_shares.part(own_z), down_shares.part(own_z)], axis=0), wide_came]
        wide = [a.reshape(-1, a.shape[-1]) for a in wide]
        square = [jnp.concatenate([qk_shares.part(own_z), vo_shares.part(own_z)], axis=0)] + square_came
    else:
        mixed_out = mix(mid, act, w_down)
        body_rows = owners // 2 * cap
        blocks = [b for both in zip(evens, jnp.split(odds[:body_rows], owners // 2, axis=0)) for b in both]
        arrived = jnp.concatenate(exchange(blocks), axis=0)
        placed = across(arrived, *around(arrived))
        small = whole_value(odds[body_rows:])
        for axis in ("vocab", "dp"):
            bit = 1
            while bit < lax.axis_size(axis):
                small = sum_of(small, [swap(a, axis, bit) for a in small])
                bit *= 2
        table_grad = place_rows(plan, placed, shard, cap)

    def add_spare(step, total):
        slot, asked_more = spare_slots(token_ids + step, seq_len, opening, shard, owners, cap, spare)
        sent = jnp.zeros((owners * spare + 1, width), F32).at[slot].add(row_grad)[:-1]
        sent = sent.astype(BF).reshape(owners, spare, width)
        came = lax.all_to_all(sent, "vocab", split_axis=0, concat_axis=0, tiled=True)
        target = jnp.where(asked_more >= 0, asked_more - base, shard).reshape(-1)
        part = jnp.zeros((shard, width), F32).at[target].add(came.reshape(-1, width).astype(F32), mode="drop")
        for bit in (1, 2):
            part = part + swap(part, "dp", bit)
        return total + part

    if spare:
        table_grad = lax.fori_loop(0, overflow.astype(jnp.int32), add_spare, table_grad)

    if packed:
        in_grad, down_grad, query_grad, key_grad, value_grad, out_grad = finish(wide, square, width // groups, width // owners)
    else:
        def spread(left, right):
            full = jnp.einsum("td,te->de", left, right, preferred_element_type=F32)
            part = lax.psum_scatter(full, "vocab", scatter_dimension=1, tiled=True).astype(BF)
            return lax.psum_scatter(part, "dp", scatter_dimension=0, tiled=True).astype(F32)

        query_grad, key_grad, value_grad = spread(hidden, dq), spread(hidden, dk), spread(hidden, dv)
        out_grad = spread(ctx, d_att)
        in_grad = spread(hidden_t.T, d_pre)
        down_grad = spread(act, cotangent)

    gains, bias = small
    gain_one_grad, gain_two_grad = gains[0], gains[1]
    bias_grad = bias[:, : rel_bias.shape[0]].T
    return (
        mixed_out,
        row_grad,
        table_grad,
        gain_one_grad,
        query_grad,
        key_grad,
        value_grad,
        out_grad,
        gain_two_grad,
        in_grad,
        down_grad,
        bias_grad,
    )


def solution(mesh):
    spread = ("dp", "vocab")
    placed = (
        P(spread),
        P(spread),
        P("vocab", None),
        P(),
        P(),
        P(),
        P(),
        P(),
        P(),
        P(),
        P(),
        P(),
        P(spread, None),
    )
    return jax.shard_map(
        body,
        mesh=mesh,
        in_specs=placed,
        out_specs=(
            P(spread, None),
            P(spread, None),
            P("vocab", None),
            P(),
            P("dp", "vocab"),
            P("dp", "vocab"),
            P("dp", "vocab"),
            P("dp", "vocab"),
            P(),
            P("dp", "vocab"),
            P("dp", "vocab"),
            P(),
        ),
        check_vma=False,
    )
```

```python
from functools import partial

import jax
import jax.numpy as jnp
import numpy as np
from jax import lax
from jax.experimental import pallas as pl
from jax.experimental.pallas import tpu as pltpu
from jax.sharding import PartitionSpec as P

EPS = 1e-06
PRECISE = lax.Precision.HIGHEST
MASKED = -1e30
THRESHOLDS = (12, 16, 23, 32, 46, 64, 91)
LANES = 128
NOWHERE = 1 << 30
BUCKETS = 32
PER_STEP = 2
PER_FETCH = 2
BF = jnp.bfloat16
F32 = jnp.float32
NN = (((1,), (0,)), ((), ()))
NT = (((1,), (1,)), ((), ()))
TN = (((0,), (0,)), ((), ()))


def mm(left, right, dims=NN):
    return lax.dot_general(left, right, dims, preferred_element_type=F32)


def params(mib=56):
    return pltpu.CompilerParams(vmem_limit_bytes=mib << 20)


def cost(macs, moved):
    return pl.CostEstimate(flops=2 * macs, bytes_accessed=moved, transcendentals=0)


def whole(shape):
    return pl.BlockSpec(shape, lambda *_: (0,) * len(shape), pipeline_mode=pl.Buffered(1))


def bucket_of(offset):
    distance = np.abs(offset)
    far = 8 + sum((distance >= t).astype(np.int32) for t in THRESHOLDS)
    return np.where(offset > 0, 16, 0) + np.where(distance < 8, distance, far)


def band_offsets():
    lane = np.arange(4 * LANES)
    return np.where(lane < 3 * LANES, lane, lane - 4 * LANES) - LANES


def band_onehot(buckets):
    return (bucket_of(band_offsets())[:, None] == np.arange(buckets)[None, :]).astype(np.float32)


def route_kernel(me_ref, ids_row_ref, slot_row_ref, slot_col_ref, ask_ref, *, seq_len, opening, shard, owners, cap, width):
    me = me_ref[0]
    tokens = ids_row_ref.shape[1]
    ids_row = ids_row_ref[...]
    parts = [jnp.broadcast_to(ids_row[:, low : low + LANES], (LANES, LANES)) for low in range(0, tokens, LANES)]
    ids_col = jnp.concatenate([part.T[:, :1] for part in parts], axis=0)
    owner_row, owner_col = jnp.zeros_like(ids_row), jnp.zeros_like(ids_col)
    for o in range(1, owners):
        owner_row += (ids_row >= o * shard).astype(jnp.int32)
        owner_col += (ids_col >= o * shard).astype(jnp.int32)

    def places(shape, axis):
        t = lax.broadcasted_iota(jnp.int32, shape, axis)
        within = lax.rem(t, seq_len)
        repeated = (within < opening) & (t >= seq_len)
        return jnp.where(within < opening, within, t), jnp.logical_not(repeated)

    at_row, first_row = places((1, tokens), 1)
    at_col, first_col = places((tokens, 1), 0)
    key_row, key_col = ids_row * tokens + at_row, ids_col * tokens + at_col
    low_row, low_col = owner_row * (shard * tokens), owner_col * (shard * tokens)
    given_row = jnp.where(first_row, key_row, -1)
    given_col = jnp.where(first_col, key_col, -1)
    rank_col = jnp.sum(((given_row >= low_col) & (given_row < key_col)).astype(jnp.int32), axis=1, keepdims=True)
    rank_row = jnp.sum(((given_col >= low_row) & (given_col < key_row)).astype(jnp.int32), axis=0, keepdims=True)
    slot_row_ref[...] = jnp.where(rank_row < cap, (owner_row ^ me) * cap + rank_row, NOWHERE)
    slot_col_ref[...] = jnp.where(rank_col < cap, (owner_col ^ me) * cap + rank_col, NOWHERE)
    over = (jnp.max(rank_row) >= cap).astype(jnp.int32)
    place_col = jnp.where(first_col & (rank_col < cap), owner_col * width + rank_col, -1)
    step = 4 * LANES
    for start in range(0, owners * width, step):
        lane = lax.broadcasted_iota(jnp.int32, (1, step), 1) + start
        asked = jnp.sum(jnp.where(place_col == lane, ids_col + 1, 0), axis=0, keepdims=True) - 1
        ask_ref[:, start : start + step] = jnp.where(lax.rem(lane, width) == width - 1, over, asked)


def route(token_ids, me, seq_len, opening, shard, owners, cap, width):
    tokens = token_ids.shape[0]
    body = partial(route_kernel, seq_len=seq_len, opening=opening, shard=shard, owners=owners, cap=cap, width=width)
    return pl.pallas_call(
        body,
        in_specs=[pl.BlockSpec(memory_space=pltpu.SMEM), pl.BlockSpec(memory_space=pltpu.VMEM)],
        out_shape=[
            jax.ShapeDtypeStruct((1, tokens), jnp.int32),
            jax.ShapeDtypeStruct((tokens, 1), jnp.int32),
            jax.ShapeDtypeStruct((1, owners * width), jnp.int32),
        ],
        compiler_params=params(),
        name="route",
    )(me, token_ids.reshape(1, -1))


def windows(lists, tile, shard, window):
    cap = lists.shape[1]
    edges = jnp.arange(pl.cdiv(shard, tile) + 1, dtype=jnp.int32) * tile
    known = jnp.where(lists < 0, NOWHERE, lists)
    below = jnp.sum((known[:, None, :] < edges[None, :, None]).astype(jnp.int32), axis=2)
    starts = jnp.minimum(below[:, :-1] // 16 * 16, cap - window)
    counts = (below[:, 1:] - starts + window - 1) // window
    return starts.T, counts.T, jnp.max(counts, axis=0)


def in_window(start, step, window, cap):
    wanted = start + step * window
    begin = pl.multiple_of(jnp.minimum(wanted, cap - window), 16)
    return begin, begin + lax.broadcasted_iota(jnp.int32, (window, 1), 0) >= wanted


def fetch_kernel(starts_ref, counts_ref, more_ref, list_ref, table_ref, out_refs, total_ref, *, tile, window, shard):
    step_rows, width = table_ref.shape
    blocks = len(out_refs)
    cap = out_refs[0].shape[0]

    @pl.when(pl.program_id(0) == 0)
    def _():
        total_ref[...] = jnp.zeros_like(total_ref)

    for sub in range(step_rows // tile):
        at = pl.program_id(0) * (step_rows // tile) + sub
        row = lax.broadcasted_iota(jnp.int32, (tile, 1), 0) + at * tile
        lane = lax.broadcasted_iota(jnp.int32, (1, tile), 1) + at * tile
        table = table_ref[sub * tile : (sub + 1) * tile, :]
        table = jnp.where(row < shard, table, jnp.zeros((), BF))
        begins = [pl.multiple_of(starts_ref[at, n], 16) for n in range(blocks)]
        wanted = [list_ref[pl.ds(n * cap + begins[n], window), :] for n in range(blocks)]
        found = mm((jnp.concatenate(wanted, axis=0) == lane).astype(F32).astype(BF), table)
        for n in range(blocks):
            total_ref[pl.ds(n * cap + begins[n], window), :] += found[n * window : (n + 1) * window]

        @pl.when(more_ref[at] > 1)
        def _():
            for n in range(blocks):
                def extra(step, carry):
                    begin, fresh = in_window(starts_ref[at, n], step, window, cap)
                    place = pl.ds(n * cap + begin, window)
                    mark = (list_ref[place, :] == lane) & fresh
                    total_ref[place, :] += mm(mark.astype(F32).astype(BF), table)
                    return carry

                lax.fori_loop(1, counts_ref[at, n], extra, 0)

    @pl.when(pl.program_id(0) == pl.num_programs(0) - 1)
    def _():
        for n in range(blocks):
            out_refs[n][...] = total_ref[n * cap : (n + 1) * cap, :].astype(BF)


def fetch_rows(table, lists):
    shard, width = table.shape
    blocks, cap = lists.shape
    tile, window = min(512, shard), min(48, cap)
    starts, counts, more = windows(lists, tile, shard, window)
    tiles = starts.shape[0]
    per_step = PER_FETCH if tiles % PER_FETCH == 0 else 1
    return pl.pallas_call(
        partial(fetch_kernel, tile=tile, window=window, shard=shard),
        grid_spec=pltpu.PrefetchScalarGridSpec(
            num_scalar_prefetch=3,
            grid=(tiles // per_step,),
            in_specs=[whole((blocks * cap, 1)), pl.BlockSpec((per_step * tile, width), lambda t, *_: (t, 0))],
            out_specs=[[whole((cap, width))] * blocks],
            scratch_shapes=[pltpu.VMEM((blocks * cap, width), F32)],
        ),
        out_shape=[[jax.ShapeDtypeStruct((cap, width), BF)] * blocks],
        compiler_params=params(),
        cost_estimate=cost(shard * width * blocks * window, 2 * (shard + blocks * cap) * width),
        name="fetch_rows",
    )(starts, counts, more, lists.reshape(-1, 1), table)[0]


def project_kernel(slot_ref, more_ref, rows_refs, gain_ref, wq_ref, wk_ref, wv_ref, x_ref, hidden_ref, q_ref, k_ref, v_ref):
    slot = slot_ref[...]
    rows = jnp.concatenate([r[...] for r in rows_refs], axis=0)
    lane = lax.broadcasted_iota(jnp.int32, (slot.shape[0], rows.shape[0]), 1)
    x = mm((lane == slot).astype(F32).astype(BF), rows)
    if more_ref is not None:
        x = x + more_ref[...].astype(F32)
    x_ref[...] = x.astype(BF)
    scale = lax.rsqrt(jnp.mean(x * x, axis=1, keepdims=True) + EPS)
    hidden = (x * scale * gain_ref[...]).astype(BF)
    hidden_ref[...] = hidden
    q_ref[...] = mm(hidden, wq_ref[...]).astype(BF)
    k_ref[...] = mm(hidden, wk_ref[...]).astype(BF)
    v_ref[...] = mm(hidden, wv_ref[...]).astype(BF)


def project(slot_col, more, rows, gain, w_query, w_key, w_value):
    tokens, width = slot_col.shape[0], gain.shape[1]
    tile = min(1024 if len(rows) <= 8 else 512, tokens)
    out = pl.BlockSpec((tile, width), lambda t: (t, 0))
    count = sum(r.shape[0] for r in rows)
    return pl.pallas_call(
        project_kernel,
        grid=(tokens // tile,),
        in_specs=[pl.BlockSpec((tile, 1), lambda t: (t, 0)), None if more is None else out, [whole(r.shape) for r in rows], whole(gain.shape)]
        + [whole(w_query.shape)] * 3,
        out_specs=[out] * 5,
        out_shape=[jax.ShapeDtypeStruct((tokens, width), BF)] * 5,
        compiler_params=params(),
        cost_estimate=cost(tokens * width * (3 * width + count), 14 * tokens * width),
        name="project",
    )(slot_col, more, rows, gain, w_query, w_key, w_value)


def band_kernel(line_ref, band_ref):
    line = jnp.broadcast_to(line_ref[0], (LANES, line_ref.shape[2]))
    band_ref[0] = pltpu.roll(line, 0, 1, stride=1, stride_axis=0)[:, : 3 * LANES]


def make_band(rel_bias):
    heads = rel_bias.shape[1]
    line = jnp.dot(band_onehot(rel_bias.shape[0]), rel_bias, precision=PRECISE).T.reshape(heads, 1, -1)
    return pl.pallas_call(
        band_kernel,
        grid=(heads,),
        in_specs=[pl.BlockSpec((1,) + line.shape[1:], lambda h: (h, 0, 0))],
        out_specs=pl.BlockSpec((1, LANES, 3 * LANES), lambda h: (h, 0, 0)),
        out_shape=jax.ShapeDtypeStruct((heads, LANES, 3 * LANES), F32),
        compiler_params=params(30),
        name="band",
    )(line)


def attend_kernel(len_ref, far_ref, q_ref, k_ref, v_ref, band_ref, ctx_ref, p_ref):
    pair = pl.program_id(1)
    q, k, v = q_ref[...], k_ref[...], v_ref[...]
    seq_len = q.shape[0]
    blocks = seq_len // LANES
    last = far_ref.shape[0] // 2 - 1
    half = lax.broadcasted_iota(jnp.int32, (1, LANES), 1) // (LANES // 2)
    key_at = lax.broadcasted_iota(jnp.int32, (1, seq_len), 1)
    mask = jnp.where(key_at < len_ref[pl.program_id(0)], 0.0, MASKED)
    none = jnp.zeros((), BF)
    ctx = jnp.zeros((seq_len, LANES), F32)
    for h in range(2):
        k_own, v_own = jnp.where(half == h, k, none), jnp.where(half == h, v, none)
        left, right = far_ref[last, 2 * pair + h], far_ref[2 * last + 1, 2 * pair + h]
        raw_all = mm(q, k_own, NT)
        for i in range(blocks):
            raw = raw_all[i * LANES : (i + 1) * LANES]
            tiles = []
            for j in range(blocks):
                cols = slice(j * LANES, (j + 1) * LANES)
                d = j - i
                if abs(d) <= 1:
                    tiles.append(raw[:, cols] + band_ref[h, :, (d + 1) * LANES : (d + 2) * LANES] + mask[:, cols])
                else:
                    tiles.append(raw[:, cols] + (mask[:, cols] + (left if d < 0 else right)))
            scores = jnp.concatenate(tiles, axis=1)
            grown = jnp.exp(scores - jnp.max(scores, axis=1, keepdims=True))
            total = jnp.sum(grown, axis=1, keepdims=True)
            p_ref[0, h, i * LANES : (i + 1) * LANES, :] = (grown * (1.0 / total)).astype(BF)
        ctx = ctx + mm(p_ref[0, h], v_own)
    ctx_ref[...] = ctx.astype(BF)


def attend(q, k, v, lengths, rel_bias, band):
    seqs, heads = lengths.shape[0], rel_bias.shape[1]
    tokens, width = q.shape
    seq_len = tokens // seqs
    block = pl.BlockSpec((seq_len, LANES), lambda s, p, *_: (s, p))
    return pl.pallas_call(
        attend_kernel,
        grid_spec=pltpu.PrefetchScalarGridSpec(
            num_scalar_prefetch=2,
            grid=(seqs, heads // 2),
            in_specs=[block] * 3 + [pl.BlockSpec((2,) + band.shape[1:], lambda s, p, *_: (p, 0, 0))],
            out_specs=[block, pl.BlockSpec((1, 2, seq_len, seq_len), lambda s, p, *_: (s, p, 0, 0))],
        ),
        out_shape=[
            jax.ShapeDtypeStruct((tokens, width), BF),
            jax.ShapeDtypeStruct((seqs, heads, seq_len, seq_len), BF),
        ],
        compiler_params=params(),
        cost_estimate=cost(tokens * seq_len * width * 8, 2 * tokens * seq_len * heads),
        name="attend",
    )(lengths, rel_bias, q, k, v, band)


def attend_back_kernel(q_ref, k_ref, v_ref, ctx_ref, do_ref, p_ref, dq_ref, dk_ref, dv_ref, line_ref, ds_ref, band_ref, far_ref):
    seq_at = pl.program_id(1)
    q, k, v, do = q_ref[...], k_ref[...], v_ref[...], do_ref[...]
    seq_len = q.shape[0]
    blocks = seq_len // LANES
    half = lax.broadcasted_iota(jnp.int32, (1, LANES), 1) // (LANES // 2)
    none = jnp.zeros((), BF)

    @pl.when(seq_at == 0)
    def _():
        band_ref[...] = jnp.zeros_like(band_ref)
        far_ref[...] = jnp.zeros_like(far_ref)

    swing = ctx_ref[...].astype(F32) * do.astype(F32)
    row_half = lax.broadcasted_iota(jnp.int32, (LANES, 1), 0) // (LANES // 2)
    q_t, do_t = (a.astype(F32).T.astype(BF) for a in (q, do))
    dq = jnp.zeros((seq_len, LANES), F32)
    dk_t = dv_t = jnp.zeros((LANES, seq_len), F32)
    for h in range(2):
        k_own, v_own = jnp.where(half == h, k, none), jnp.where(half == h, v, none)
        near = [jnp.zeros((LANES, LANES), F32) for _ in range(3)]
        far = [jnp.zeros((8, LANES), F32) for _ in range(2)]
        for i in range(blocks):
            rows = slice(i * LANES, (i + 1) * LANES)
            probs = p_ref[0, h, rows, :].astype(F32)
            swing_own = jnp.sum(jnp.where(half == h, swing[rows], 0.0), axis=1, keepdims=True)
            ds = probs * (mm(do[rows], v_own, NT) - swing_own)
            for j in range(blocks):
                d = j - i
                tile = ds[:, j * LANES : (j + 1) * LANES]
                if abs(d) <= 1:
                    near[d + 1] = near[d + 1] + tile
                else:
                    side = 0 if d < 0 else 1
                    far[side] = far[side] + jnp.sum(tile.reshape(LANES // 8, 8, LANES), axis=0)
            ds_ref[rows, :] = ds.astype(BF)
        for d in range(3):
            band_ref[h, :, d * LANES : (d + 1) * LANES] += near[d]
        for side in range(2):
            far_ref[h, :, side * LANES : (side + 1) * LANES] += far[side]
        d_low = ds_ref[...]
        dk_t = dk_t + mm(jnp.where(row_half == h, q_t, none), d_low)
        dv_t = dv_t + mm(jnp.where(row_half == h, do_t, none), p_ref[0, h])
        dq = dq + mm(d_low, k_own)
    dq_ref[...], dk_ref[...], dv_ref[...] = dq.astype(BF), dk_t.T.astype(BF), dv_t.T.astype(BF)

    @pl.when(seq_at == pl.num_programs(1) - 1)
    def _():
        row = lax.broadcasted_iota(jnp.int32, (8, 1), 0)
        for h in range(2):
            padded = jnp.concatenate([band_ref[h], jnp.zeros((LANES, LANES), F32)], axis=1)
            turned = padded[:8]
            for start in range(8, LANES, 8):
                turned = turned + pltpu.roll(padded[start : start + 8], 4 * LANES - start, 1)
            for bit in (1, 2, 4):
                turned = jnp.where(row & bit > 0, pltpu.roll(turned, 4 * LANES - bit, 1), turned)
            line_ref[0, h : h + 1, :] = jnp.sum(turned, axis=0, keepdims=True)
            line_ref[0, 2 + h : 3 + h, : 2 * LANES] = jnp.sum(far_ref[h], axis=0, keepdims=True)


def attend_back(q, k, v, ctx, d_context, probs):
    seqs, heads, seq_len, _ = probs.shape
    tokens, width = q.shape
    pairs = heads // 2
    block = pl.BlockSpec((seq_len, LANES), lambda p, s: (s, p))
    return pl.pallas_call(
        attend_back_kernel,
        grid=(pairs, seqs),
        in_specs=[block] * 5 + [pl.BlockSpec((1, 2, seq_len, seq_len), lambda p, s: (s, p, 0, 0))],
        out_specs=[block] * 3 + [pl.BlockSpec((1, 8, 4 * LANES), lambda p, s: (p, 0, 0))],
        out_shape=[jax.ShapeDtypeStruct((tokens, width), BF)] * 3
        + [jax.ShapeDtypeStruct((heads // 2, 8, 4 * LANES), F32)],
        scratch_shapes=[
            pltpu.VMEM((seq_len, seq_len), BF),
            pltpu.VMEM((2, LANES, 3 * LANES), F32),
            pltpu.VMEM((2, 8, 2 * LANES), F32),
        ],
        compiler_params=params(),
        cost_estimate=cost(tokens * seq_len * width * 12, 2 * tokens * seq_len * heads),
        name="attend_back",
    )(q, k, v, ctx, d_context, probs)


def middle_kernel(x_ref, ctx_ref, cot_ref, gain_ref, w_out_ref, w_in_ref, w_down_ref, mid_ref, act_ref, d_pre_ref, hidden_t_ref, d_mid_ref, d_att_ref, d_ctx_ref, gain_grad_ref, *, chunk):
    mid = x_ref[...].astype(F32) + mm(ctx_ref[...], w_out_ref[...])
    gain = gain_ref[...]
    scale = lax.rsqrt(jnp.mean(mid * mid, axis=1, keepdims=True) + EPS)
    hidden_full = mid * scale * gain
    hidden = hidden_full.astype(BF)
    hidden_t_ref[...] = hidden_full.T.astype(BF)
    cot = cot_ref[...]
    mid_ref[...] = mid
    d_hidden = jnp.zeros_like(mid)
    slope = float(np.sqrt(2 / np.pi))
    for start in range(0, w_in_ref.shape[1], chunk):
        cols = slice(start, start + chunk)
        pre = mm(hidden, w_in_ref[:, cols])
        d_act = mm(cot, w_down_ref[cols, :], NT)
        square = pre * pre
        bent = jnp.tanh(slope * pre * (1.0 + 0.044715 * square))
        open_half = 0.5 + 0.5 * bent
        act = (pre * open_half).astype(BF)
        curve = (0.5 * slope) * pre * (1.0 - bent * bent) * (1.0 + (3 * 0.044715) * square)
        d_pre = (d_act * (open_half + curve)).astype(BF)
        act_ref[:, cols] = act
        d_pre_ref[:, cols] = d_pre
        d_hidden = d_hidden + mm(d_pre, w_in_ref[:, cols], NT)
    u = d_hidden * gain
    swing = jnp.mean(u * mid, axis=1, keepdims=True)
    d_mid = cot.astype(F32) + scale * u - mid * (scale * scale * scale * swing)
    d_mid_ref[...] = d_mid
    d_att = d_mid.astype(BF)
    d_att_ref[...] = d_att
    d_ctx_ref[...] = mm(d_att, w_out_ref[...], NT).astype(BF)

    @pl.when(pl.program_id(0) == 0)
    def _():
        gain_grad_ref[...] = jnp.zeros_like(gain_grad_ref)

    gain_grad_ref[...] += jnp.sum((d_hidden * mid * scale).reshape(-1, 8, mid.shape[1]), axis=0)


def middle_part(x, ctx, cot, gain, w_out, w_in, w_down):
    tokens, width = x.shape
    wide = w_in.shape[1]
    tile = min(256, tokens)
    rows = pl.BlockSpec((tile, width), lambda t: (t, 0))
    wide_rows = pl.BlockSpec((tile, wide), lambda t: (t, 0))
    return pl.pallas_call(
        partial(middle_kernel, chunk=min(768, wide)),
        grid=(tokens // tile,),
        in_specs=[rows] * 3 + [whole(a.shape) for a in (gain, w_out, w_in, w_down)],
        out_specs=[rows, wide_rows, wide_rows, pl.BlockSpec((width, tile), lambda t: (0, t)), rows, rows, rows]
        + [pl.BlockSpec((8, width), lambda t: (0, 0))],
        out_shape=[
            jax.ShapeDtypeStruct((tokens, width), F32),
            jax.ShapeDtypeStruct((tokens, wide), BF),
            jax.ShapeDtypeStruct((tokens, wide), BF),
            jax.ShapeDtypeStruct((width, tokens), BF),
            jax.ShapeDtypeStruct((tokens, width), F32),
            jax.ShapeDtypeStruct((tokens, width), BF),
            jax.ShapeDtypeStruct((tokens, width), BF),
            jax.ShapeDtypeStruct((8, width), F32),
        ],
        compiler_params=params(),
        cost_estimate=cost(tokens * width * (4 * wide + 2 * width), 4 * width * wide + 8 * tokens * (wide + width)),
        name="middle",
    )(x, ctx, cot, gain, w_out, w_in, w_down)


def mix_kernel(mid_ref, act_ref, w_down_ref, mixed_ref):
    mixed_ref[...] = (mid_ref[...] + mm(act_ref[...], w_down_ref[...])).astype(BF)


def mix(mid, act, w_down):
    tokens, width = mid.shape
    wide = act.shape[1]
    tile = min(256, tokens)
    rows = pl.BlockSpec((tile, width), lambda t: (t, 0))
    return pl.pallas_call(
        mix_kernel,
        grid=(tokens // tile,),
        in_specs=[rows, pl.BlockSpec((tile, wide), lambda t: (t, 0)), whole(w_down.shape)],
        out_specs=rows,
        out_shape=jax.ShapeDtypeStruct((tokens, width), BF),
        compiler_params=params(),
        cost_estimate=cost(tokens * width * wide, 2 * wide * (tokens + width)),
        name="mix",
    )(mid, act, w_down)


def in_grads_kernel(core_ref, hidden_t_ref, d_pre_ref, keep_ref, send_ref, part_ref):
    core = core_ref[0]
    groups, lanes = keep_ref.shape[0], keep_ref.shape[3]
    part = mm(hidden_t_ref[...], d_pre_ref[...]).astype(BF)
    for c in range(2):
        part_ref[c] = part[:, c * lanes : (c + 1) * lanes].reshape(groups, -1, lanes)
    for d in range(groups):
        keep_ref[d, 0] = part_ref[core, d]
        send_ref[d, 0] = part_ref[1 - core, d]


def in_grads(core, hidden_t, d_pre, groups, owners):
    width, tokens = hidden_t.shape
    wide = d_pre.shape[1]
    lanes, zs = wide // owners, owners // 2
    out = pl.BlockSpec((groups, 1, width // groups, lanes), lambda z, *_: (0, z, 0, 0))
    return pl.pallas_call(
        in_grads_kernel,
        grid_spec=pltpu.PrefetchScalarGridSpec(
            num_scalar_prefetch=1,
            grid=(zs,),
            in_specs=[whole(hidden_t.shape), pl.BlockSpec((tokens, 2 * lanes), lambda z, *_: (0, z))],
            out_specs=[out, out],
            scratch_shapes=[pltpu.VMEM((2, groups, width // groups, lanes), BF)],
        ),
        out_shape=[jax.ShapeDtypeStruct((groups, zs, width // groups, lanes), BF)] * 2,
        compiler_params=params(),
        cost_estimate=cost(tokens * width * wide, 2 * wide * (tokens + width)),
        name="in_grads",
    )(core, hidden_t, d_pre)


def down_grads_kernel(core_ref, cot_t_ref, act_ref, keep_ref, send_ref, parts_ref):
    core = core_ref[0]
    halves, lanes = keep_ref.shape[2], keep_ref.shape[4]
    part = mm(cot_t_ref[...], act_ref[...]).astype(BF)
    for h in range(halves):
        parts_ref[h] = part[:, h * lanes : (h + 1) * lanes].reshape(parts_ref.shape[1:])
        for z in range(keep_ref.shape[1]):
            keep_ref[0, z, h] = parts_ref[h, 2 * z + core]
            send_ref[0, z, h] = parts_ref[h, 2 * z + 1 - core]


def down_grads(core, cot_t, act, groups, owners):
    width, tokens = cot_t.shape
    wide = act.shape[1]
    lanes, zs = wide // owners, owners // 2
    halves = owners // groups
    out = pl.BlockSpec((1, zs, halves, width // owners, lanes), lambda d, *_: (d, 0, 0, 0, 0))
    return pl.pallas_call(
        down_grads_kernel,
        grid_spec=pltpu.PrefetchScalarGridSpec(
            num_scalar_prefetch=1,
            grid=(groups,),
            in_specs=[whole(cot_t.shape), pl.BlockSpec((tokens, wide // groups), lambda d, *_: (0, d))],
            out_specs=[out, out],
            scratch_shapes=[pltpu.VMEM((halves, owners, width // owners, lanes), BF)],
        ),
        out_shape=[jax.ShapeDtypeStruct((groups, zs, halves, width // owners, lanes), BF)] * 2,
        compiler_params=params(),
        cost_estimate=cost(tokens * width * wide, 2 * wide * (tokens + width)),
        name="down_grads",
    )(core, cot_t, act)


def square_kernel(left_ref, right_ref, out_ref):
    out_ref[...] = mm(left_ref[...], right_ref[...], TN).astype(BF).reshape(out_ref.shape)


def square_part(left, right, owners):
    tokens, width = left.shape
    return pl.pallas_call(
        square_kernel,
        out_shape=jax.ShapeDtypeStruct((owners, width // owners, right.shape[1]), BF),
        compiler_params=params(30),
        cost_estimate=cost(tokens * width * width, 6 * tokens * width),
        name="square_part",
    )(left, right)


def square_grads_kernel(core_ref, left_refs, right_refs, ready_ref, keep_ref, send_ref, parts_ref, *, groups, owners):
    core = core_ref[0]
    for n, (left_ref, right_ref) in enumerate(zip(left_refs, right_refs)):
        parts_ref[n] = mm(left_ref[...], right_ref[...], TN).astype(BF).reshape(parts_ref.shape[1:])
    lanes = right_refs[0].shape[1] // groups
    for z in range(owners // 2):
        for target_ref, v in ((keep_ref, 2 * z + core), (send_ref, 2 * z + 1 - core)):
            first, second = parts_ref[0, v], parts_ref[1, v] if ready_ref is None else ready_ref[v]
            for d in range(groups):
                cols = slice(d * lanes, (d + 1) * lanes)
                target_ref[d, z] = jnp.concatenate([first[:, cols], second[:, cols]], axis=1)


def square_grads(core, lefts, rights, ready, groups, owners):
    tokens, width = rights[0].shape
    shape = (groups, owners // 2, width // owners, 2 * width // groups)
    vmem = pl.BlockSpec(memory_space=pltpu.VMEM)
    return pl.pallas_call(
        partial(square_grads_kernel, groups=groups, owners=owners),
        in_specs=[pl.BlockSpec(memory_space=pltpu.SMEM), [vmem] * len(lefts), [vmem] * len(lefts)]
        + [None if ready is None else vmem],
        out_shape=[jax.ShapeDtypeStruct(shape, BF)] * 2,
        scratch_shapes=[pltpu.VMEM((len(lefts), owners, width // owners, width), BF)],
        compiler_params=params(30),
        cost_estimate=cost(len(lefts) * tokens * width * width, 12 * tokens * width),
        name="square_grads",
    )(core, lefts, rights, ready)


SMALL = 16


def low_parts(value, high_of):
    gains, bias = value
    gains_high, bias_high = high_of(gains), high_of(bias)
    bias = jnp.concatenate([bias_high, bias - bias_high], axis=1)
    bias = jnp.concatenate([bias, jnp.zeros((SMALL - 4, gains.shape[1] - bias.shape[1]), F32)], axis=1)
    return jnp.concatenate([gains_high, gains - gains_high, bias], axis=0).astype(BF)


def whole_value(parts):
    parts = parts.astype(F32)
    return parts[0:2] + parts[2:4], parts[4:SMALL, :LANES] + parts[4:SMALL, LANES : 2 * LANES]


def sum_of(first, second):
    return tuple(a + b for a, b in zip(first, second))


def round_low(value):
    return value.astype(BF).astype(F32)


def small_value(lines_ref, onehot_ref, gain_one_part, gain_two_part):
    pairs = lines_ref.shape[0]
    near = jnp.concatenate([lines_ref[p, 0:2, :] for p in range(pairs)], axis=0)
    far = jnp.concatenate([lines_ref[p, 2:4, : 2 * LANES] for p in range(pairs)], axis=0)
    bias = lax.dot_general(near, onehot_ref[...], NN, precision=PRECISE, preferred_element_type=F32)
    lane = lax.broadcasted_iota(jnp.int32, (1, LANES), 1)
    left = jnp.sum(far[:, :LANES], axis=1, keepdims=True)
    right = jnp.sum(far[:, LANES:], axis=1, keepdims=True)
    bias = bias + jnp.where(lane == BUCKETS // 2 - 1, left, 0.0) + jnp.where(lane == BUCKETS - 1, right, 0.0)
    gains = [jnp.sum(g, axis=0, keepdims=True) for g in (gain_one_part, gain_two_part)]
    return jnp.concatenate(gains, axis=0), bias


def rows_kernel(slot_ref, x_ref, d_mid_ref, dq_ref, dk_ref, dv_ref, gain_ref, wq_ref, wk_ref, wv_ref, lines_ref, onehot_ref, gain_two_ref, row_ref, even_refs, odd_ref, held_ref, gain_grad_ref):
    d_hidden = mm(dq_ref[...], wq_ref[...], NT) + mm(dk_ref[...], wk_ref[...], NT) + mm(dv_ref[...], wv_ref[...], NT)
    x = x_ref[...].astype(F32)
    scale = lax.rsqrt(jnp.mean(x * x, axis=1, keepdims=True) + EPS)
    u = d_hidden * gain_ref[...]
    swing = jnp.mean(u * x, axis=1, keepdims=True)
    row = d_mid_ref[...] + scale * u - x * (scale * scale * scale * swing)
    row_ref[...] = row
    at = pl.program_id(0)

    @pl.when(at == 0)
    def _():
        gain_grad_ref[...] = jnp.zeros_like(gain_grad_ref)

    gain_grad_ref[...] += jnp.sum((d_hidden * x * scale).reshape(-1, 8, x.shape[1]), axis=0)
    tile = row.shape[0]
    held_ref[pl.ds(pl.multiple_of(at * tile, tile), tile), :] = row.astype(BF)

    @pl.when(at == pl.num_programs(0) - 1)
    def _():
        slot, held = slot_ref[...], held_ref[...]
        cap, evens = even_refs[0].shape[0], len(even_refs)
        order = [2 * n for n in range(evens)] + [2 * n + 1 for n in range(evens)]
        line = lax.broadcasted_iota(jnp.int32, (cap, slot.shape[1]), 0)
        together = min(len(order), 8)
        for low in range(0, len(order), together):
            places = jnp.concatenate([line + k * cap for k in order[low : low + together]], axis=0)
            sent = mm((places == slot).astype(F32).astype(BF), held).astype(BF)
            for n in range(together):
                part, at_n = sent[n * cap : (n + 1) * cap], low + n
                if at_n < evens:
                    even_refs[at_n][...] = part
                else:
                    odd_ref[(at_n - evens) * cap : (at_n - evens + 1) * cap, :] = part
        small = small_value(lines_ref, onehot_ref, gain_grad_ref[...], gain_two_ref[...])
        odd_ref[evens * cap :, :] = low_parts(small, round_low)


def rows_back(slot_row, x, d_mid, dq, dk, dv, gain, w_query, w_key, w_value, lines, gain_two_part, owners, cap):
    tokens, width = x.shape
    onehot = jnp.asarray(band_onehot(LANES))
    half = owners // 2
    tile = min(256, tokens)
    rows = pl.BlockSpec((tile, width), lambda t: (t, 0))
    return pl.pallas_call(
        rows_kernel,
        grid=(tokens // tile,),
        in_specs=[whole(slot_row.shape)] + [rows] * 5 + [whole(gain.shape)] + [whole(w_query.shape)] * 3
        + [whole(a.shape) for a in (lines, onehot, gain_two_part)],
        out_specs=[rows, [whole((cap, width))] * half, whole((half * cap + SMALL, width))],
        out_shape=[
            jax.ShapeDtypeStruct((tokens, width), F32),
            [jax.ShapeDtypeStruct((cap, width), BF)] * half,
            jax.ShapeDtypeStruct((half * cap + SMALL, width), BF),
        ],
        scratch_shapes=[pltpu.VMEM((tokens, width), BF), pltpu.VMEM((8, width), F32)],
        compiler_params=params(),
        cost_estimate=cost(tokens * width * (3 * width + owners * cap), 20 * tokens * width),
        name="rows_back",
    )(slot_row, x, d_mid, dq, dk, dv, gain, w_query, w_key, w_value, lines, onehot, gain_two_part)


def plan_kernel(starts_ref, list_ref, plan_ref, *, blocks, window):
    at = pl.program_id(0)
    cap = list_ref.shape[0] // blocks
    wanted = [list_ref[pl.ds(n * cap + pl.multiple_of(starts_ref[at, n], 16), window), :] for n in range(blocks)]
    wanted = jnp.concatenate(wanted, axis=0)
    for low in range(0, wanted.shape[0], LANES):
        part = jnp.broadcast_to(wanted[low : low + LANES], (min(LANES, wanted.shape[0] - low), LANES))
        plan_ref[0, :, low : low + LANES] = part.T[:1]


def place_plan(lists, shard):
    blocks, cap = lists.shape
    tile, window = min(256, shard), min(32, cap)
    starts, counts, more = windows(lists, tile, shard, window)
    tiles = pl.cdiv(shard, tile)
    column = lists.reshape(-1, 1)
    plan = pl.pallas_call(
        partial(plan_kernel, blocks=blocks, window=window),
        grid_spec=pltpu.PrefetchScalarGridSpec(
            num_scalar_prefetch=1,
            grid=(tiles,),
            in_specs=[whole(column.shape)],
            out_specs=pl.BlockSpec((1, 1, blocks * window), lambda t, *_: (t, 0, 0)),
        ),
        out_shape=jax.ShapeDtypeStruct((tiles, 1, blocks * window), jnp.int32),
        compiler_params=params(30),
        name="place_plan",
    )(starts, column)
    return starts, counts, more, plan, column


def place_kernel(starts_ref, counts_ref, more_ref, plan_ref, list_ref, rows_refs, out_ref, list_held, list_sem, *, tile, window, cap):
    per_step = plan_ref.shape[0]
    places = [(ref, low) for ref in rows_refs for low in range(0, ref.shape[0] // cap * cap, cap)]
    for sub in range(per_step):
        at = pl.program_id(0) * per_step + sub
        out_rows = slice(sub * tile, (sub + 1) * tile)
        row = lax.broadcasted_iota(jnp.int32, (tile, 1), 0) + at * tile
        held = []
        for n, (rows_ref, low) in enumerate(places):
            held.append(rows_ref[pl.ds(low + pl.multiple_of(starts_ref[at, n], 16), window), :])
        out_ref[out_rows, :] = mm((row == plan_ref[sub]).astype(F32).astype(BF), jnp.concatenate(held, axis=0))

    for sub in range(per_step):
        at = pl.program_id(0) * per_step + sub
        out_rows = slice(sub * tile, (sub + 1) * tile)

        @pl.when(more_ref[at] > 1)
        def _():
            copy = pltpu.make_async_copy(list_ref, list_held, list_sem)
            copy.start()
            copy.wait()
            lane = lax.broadcasted_iota(jnp.int32, (1, tile), 1) + at * tile
            for n, (rows_ref, low) in enumerate(places):
                def extra(step, carry):
                    begin, fresh = in_window(starts_ref[at, n], step, window, cap)
                    own = (list_held[pl.ds(n * cap + begin, window), :] == lane) & fresh
                    rows = rows_ref[pl.ds(low + begin, window), :]
                    out_ref[out_rows, :] += mm(own.astype(F32).astype(BF), rows, TN)
                    return carry

                lax.fori_loop(1, counts_ref[at, n], extra, 0)


def place_rows(plan, rows, shard, cap):
    width = rows[0].shape[1]
    starts, counts, more, lanes, column = plan
    tile, window = min(256, shard), min(32, cap)
    per_step = PER_STEP if starts.shape[0] % PER_STEP == 0 else 1
    return pl.pallas_call(
        partial(place_kernel, tile=tile, window=window, cap=cap),
        grid_spec=pltpu.PrefetchScalarGridSpec(
            num_scalar_prefetch=3,
            grid=(starts.shape[0] // per_step,),
            in_specs=[
                pl.BlockSpec((per_step, 1, lanes.shape[2]), lambda t, *_: (t, 0, 0)),
                pl.BlockSpec(memory_space=pl.ANY),
                [whole(r.shape) for r in rows],
            ],
            out_specs=pl.BlockSpec((per_step * tile, width), lambda t, *_: (t, 0)),
            scratch_shapes=[pltpu.VMEM(column.shape, jnp.int32), pltpu.SemaphoreType.DMA],
        ),
        out_shape=jax.ShapeDtypeStruct((shard, width), F32),
        compiler_params=params(30),
        cost_estimate=cost(shard * width * lanes.shape[2], 4 * shard * width + 2 * column.shape[0] * width),
        name="place_rows",
    )(starts, counts, more, lanes, column, rows)


def pair_kernel(even_refs, own_ref, came_ref, out_refs):
    cap = even_refs[0].shape[0]
    rows = len(even_refs) * cap
    small = sum_of(whole_value(own_ref[rows:, :]), whole_value(came_ref[rows:, :]))
    parts = low_parts(small, round_low)
    for n, out_ref in enumerate(out_refs):
        out_ref[:cap, :] = even_refs[n][...]
        out_ref[cap : 2 * cap, :] = came_ref[n * cap : (n + 1) * cap, :]
        if n > 0:
            out_ref[2 * cap :, :] = parts


def pair_blocks(evens, own, came):
    cap, width = evens[0].shape
    shapes = [(2 * cap, width)] + [(2 * cap + SMALL, width)] * (len(evens) - 1)
    return pl.pallas_call(
        pair_kernel,
        out_shape=[[jax.ShapeDtypeStruct(shape, BF) for shape in shapes]],
        compiler_params=params(),
        cost_estimate=cost(1, 1),
        name="pair_blocks",
    )(evens, own, came)[0]


def swap(value, axis, bit):
    count = lax.axis_size(axis)
    return lax.ppermute(value, axis, [(i, i ^ bit) for i in range(count)])


def arrival_order(owners):
    if owners != 8:
        return [(n, 0, owners) for n in range(4)]
    order = [(n, low, high) for low, high in ((0, 2), (2, 6), (6, 8)) for n in range(3)]
    return order + [(3, 0, 1), (3, 2, 4), (3, 1, 2), (3, 4, 6), (3, 6, 7), (3, 7, 8)]


def exchange(blocks):
    owners = lax.axis_size("vocab")
    if owners <= 8:
        return [blocks[0]] + [swap(blocks[k], "vocab", k) for k in range(1, owners)]
    order = lax.axis_index("vocab") ^ jnp.arange(owners)
    sent = jnp.take(jnp.stack(blocks), order, axis=0)
    came = lax.all_to_all(sent, "vocab", split_axis=0, concat_axis=0, tiled=True)
    return list(jnp.take(came, order, axis=0))


def around(block):
    return swap(block, "dp", 1), swap(block, "dp", 2)


def across(block, by_x, by_y):
    half = block.shape[0] // 2
    return [block, by_x, by_y, swap(by_x[:half], "dp", 2), swap(by_y[half:], "dp", 1)]


class Shares:
    def __init__(self, *terms):
        self.terms = [t.reshape((2, 2, 2, 2, -1, t.shape[-1])) for t in terms]
        self.bits = {}

    def half(self, term, bits):
        starts = [bits.get(axis, 0) if size == 2 and axis < 4 else 0 for axis, size in enumerate(term.shape)]
        sizes = [1 if axis in bits else size for axis, size in enumerate(term.shape)]
        return lax.dynamic_slice(term, starts, sizes).astype(F32)

    def send(self, axis, at):
        sent = sum(self.half(t, {**self.bits, axis: 1 - at}) for t in self.terms).astype(BF)
        self.bits[axis] = at
        return sent

    def add(self, came):
        self.terms.append(came)

    def part(self, bits):
        total = sum(self.half(t, {**self.bits, **bits}) for t in self.terms).astype(BF)
        return total.reshape(total.shape[-2:])


def with_small(rows, small):
    parts = low_parts(small, lambda value: lax.reduce_precision(value, 8, 7))
    return jnp.concatenate([rows, parts], axis=0), whole_value(parts)


def after(value, *others):
    if isinstance(value, (list, tuple)):
        return list(lax.optimization_barrier(tuple(value) + others)[: len(value)])
    return lax.optimization_barrier((value,) + others)[0]


def finish_kernel(wide_refs, square_refs, in_ref, down_ref, q_ref, k_ref, v_ref, o_ref):
    wide, square = (sum(ref[...].astype(F32) for ref in refs) for refs in (wide_refs, square_refs))
    rows, lanes, low = down_ref.shape[1], wide.shape[1], in_ref.shape[0]
    in_ref[...] = wide[:low]
    for n in range(down_ref.shape[0] // lanes):
        down_ref[n * lanes : (n + 1) * lanes, :] = wide[low : low + rows].T
        low += rows
    for n, (first_ref, second_ref) in enumerate(((q_ref, k_ref), (v_ref, o_ref))):
        turned = square[n * rows : (n + 1) * rows].T
        first_ref[...] = turned[: q_ref.shape[0]]
        second_ref[...] = turned[q_ref.shape[0] :]


def finish(wide, square, in_rows, rows):
    lanes = wide[0].shape[1]
    down = (wide[0].shape[0] - in_rows) // rows * lanes
    return pl.pallas_call(
        finish_kernel,
        out_shape=[jax.ShapeDtypeStruct((in_rows, lanes), F32), jax.ShapeDtypeStruct((down, rows), F32)]
        + [jax.ShapeDtypeStruct((lanes // 2, rows), F32)] * 4,
        compiler_params=params(24),
        cost_estimate=cost(1, 1),
        name="finish",
    )(wide, square)


def spare_slots(token_ids, seq_len, opening, shard, owners, cap, spare):
    tokens = token_ids.shape[0]
    t = jnp.arange(tokens, dtype=jnp.int32)
    within = t % seq_len
    at = jnp.where(within < opening, within, t)
    first = (within >= opening) | (t < seq_len)
    owner = token_ids // shard
    key = token_ids * tokens + at
    same = (owner[:, None] == owner[None, :]) & first[None, :] & (key[None, :] < key[:, None])
    rank = jnp.sum(same.astype(jnp.int32), axis=1) - cap
    slot = jnp.where(rank >= 0, owner * spare + rank, owners * spare)
    request = jnp.full((owners * spare + 1,), -1, jnp.int32).at[slot].set(token_ids)[:-1]
    asked = lax.all_to_all(request.reshape(owners, spare), "vocab", split_axis=0, concat_axis=0, tiled=True)
    return slot, asked


def body(
    token_ids,
    seq_lengths,
    table,
    gain_one,
    w_query,
    w_key,
    w_value,
    w_out,
    gain_two,
    w_in,
    w_down,
    rel_bias,
    cotangent,
):
    owners, groups = lax.axis_size("vocab"), lax.axis_size("dp")
    me = lax.axis_index("vocab").astype(jnp.int32)
    core = (me % 2).reshape(1)
    shard, width = table.shape
    tokens, seqs = token_ids.shape[0], seq_lengths.shape[0]
    seq_len = tokens // seqs
    heads = rel_bias.shape[1]
    most = 2 * tokens // owners
    opening = most // seqs
    cap = min(most, -(-(9 * most // 16) // 16) * 16)
    spare = most - cap
    lanes = -(-(cap + 1) // LANES) * LANES
    gain_one_row, gain_two_row = gain_one.reshape(1, -1), gain_two.reshape(1, -1)

    slot_row, slot_col, ask = route(token_ids, me.reshape(1), seq_len, opening, shard, owners, cap, lanes)
    asked = lax.all_to_all(ask.reshape(owners, lanes), "vocab", split_axis=0, concat_axis=0, tiled=True)
    asked = jnp.take(asked, me ^ jnp.arange(owners), axis=0)
    base = me * shard
    by_x = swap(asked, "dp", 1)
    by_y = swap(jnp.stack([asked, by_x]), "dp", 2)
    asked_all = jnp.stack([asked, by_x, by_y[0], by_y[1]])
    overflow = jnp.max(asked_all[:, :, lanes - 1]) > 0 if spare else None
    targets = jnp.where(asked_all[:, :, :cap] >= 0, asked_all[:, :, :cap] - base, -1)
    picked = fetch_rows(table, jnp.where(asked[:, :cap] >= 0, asked[:, :cap] - base, -1))
    rows = exchange(picked)
    rel_bias, cotangent, targets = after([rel_bias, cotangent, targets], rows[1])
    band = make_band(rel_bias)
    cot_t = cotangent.T
    lists = [targets[n, low:high] for n, low, high in arrival_order(owners)]
    lists = jnp.concatenate(lists, axis=0)
    plan = place_plan(lists, shard)

    def spare_rows(step, _):
        slot, asked_more = spare_slots(token_ids + step, seq_len, opening, shard, owners, cap, spare)
        found = jnp.take(table, jnp.clip(asked_more - base, 0, shard - 1), axis=0)
        came = lax.all_to_all(found, "vocab", split_axis=0, concat_axis=0, tiled=True).reshape(-1, width)
        more = jnp.take(came, jnp.clip(slot, 0, owners * spare - 1), axis=0)
        return jnp.where((slot < owners * spare)[:, None], more, jnp.zeros((), BF))

    more = None
    if spare:
        more = lax.fori_loop(0, overflow.astype(jnp.int32), spare_rows, jnp.zeros((tokens, width), BF))
    held = after([rows[0], band, cot_t, *plan])
    rows[0], band, cot_t, plan = held[0], held[1], held[2], held[3:]

    x, hidden, q, k, v = project(slot_col, more, rows, gain_one_row, w_query, w_key, w_value)

    ctx, probs = attend(q, k, v, seq_lengths, rel_bias, band)
    mid, act, d_pre, hidden_t, d_mid, d_att, d_ctx, gain_two_part = middle_part(
        x, ctx, cotangent, gain_two_row, w_out, w_in, w_down
    )
    packed = owners == 8 and groups == 4 and (width // groups) % 64 == 0 and (w_in.shape[1] // owners) % LANES == 0
    place_dp = lax.axis_index("dp")
    x_bit, y_bit, z_high, z_low = place_dp % 2, place_dp // 2, me // 4, (me // 2) % 2
    if packed:
        in_keep, in_send = in_grads(core, hidden_t, d_pre, groups, owners)
        down_keep, down_send = down_grads(core, cot_t, after(act, in_send), groups, owners)
        in_came = swap(in_send, "vocab", 1)
        down_send = after(down_send, in_came)
        down_came = swap(down_send, "vocab", 1)
        out_part = square_part(after(d_att, down_send), ctx, owners)
        down_came = after(down_came, out_part)
        in_shares, down_shares = Shares(in_keep, in_came), Shares(down_keep, down_came)
        in_sent, down_sent = in_shares.send(1, x_bit), down_shares.send(0, y_bit)
        d_ctx = after(d_ctx, in_sent, down_sent, out_part)
        in_came, down_came = swap(in_sent, "dp", 1), swap(down_sent, "dp", 2)
    dq, dk, dv, lines = attend_back(q, k, v, ctx, d_ctx, probs)
    if packed:
        in_came, down_came = after([in_came, down_came], dq)
        in_shares.add(in_came)
        down_shares.add(down_came)
        in_sent, down_sent = in_shares.send(0, y_bit), down_shares.send(1, x_bit)
        qk_keep, qk_send = square_grads(core, [dq, dk], [hidden, hidden], None, groups, owners)
        vo_keep, vo_send = square_grads(core, [dv], [hidden], out_part, groups, owners)
        qk_came, vo_came = swap(qk_send, "vocab", 1), swap(vo_send, "vocab", 1)
        d_mid = after(d_mid, in_sent, down_sent, qk_send, vo_send)
        in_came, down_came = swap(in_sent, "dp", 2), swap(down_sent, "dp", 1)
    row_grad, evens, odds = rows_back(
        slot_row, x, d_mid, dq, dk, dv, gain_one_row, w_query, w_key, w_value, lines, gain_two_part, owners, cap
    )

    if packed:
        odds, *evens = after([odds, *evens], in_came, down_came)
        along = pair_blocks(evens, odds, swap(odds, "vocab", 1))
        pair = 2 * cap

        by_one, by_two = swap(along[1], "vocab", 2), swap(along[2], "vocab", 4)
        own_x, own_y = around(along[0])
        qk_came, vo_came = after([qk_came, vo_came], row_grad)
        qk_shares, vo_shares = Shares(qk_keep, qk_came), Shares(vo_keep, vo_came)
        qk_came, vo_came = swap(qk_shares.send(1, x_bit), "dp", 1), swap(vo_shares.send(0, y_bit), "dp", 2)
        in_shares.add(in_came)
        down_shares.add(down_came)
        wide_sent = jnp.concatenate([in_shares.send(2, z_high), down_shares.send(2, z_high)], axis=4)
        in_rows = in_keep.shape[2]
        qk_came, vo_came = after([qk_came, vo_came], own_x, own_y)
        qk_shares.add(qk_came)
        vo_shares.add(vo_came)
        qk_came, vo_came = swap(qk_shares.send(0, y_bit), "dp", 2), swap(vo_shares.send(1, x_bit), "dp", 1)
        by_three = swap(after(along[3], by_two), "vocab", 6)
        held = (by_one, by_two, own_x, own_y, qk_came, vo_came, wide_sent)
        by_one, by_two, own_x, own_y, qk_came, vo_came, wide_sent = lax.optimization_barrier(held)

        mid_rows = jnp.concatenate([by_one[:pair], by_two[:pair]], axis=0)
        mid_x, mid_y = around(mid_rows)
        qk_shares.add(qk_came)
        vo_shares.add(vo_came)
        mixed_out = mix(after(mid, by_one), act, w_down)
        held = (by_three, mid_x, mid_y, own_x, own_y, wide_sent, mixed_out)
        by_three, mid_x, mid_y, own_x, own_y, wide_sent, mixed_out = lax.optimization_barrier(held)

        far_low = swap(jnp.concatenate([own_x[:cap], mid_x[:pair]], axis=0), "dp", 2)
        far_high = swap(jnp.concatenate([own_y[cap:], mid_y[pair:]], axis=0), "dp", 1)
        small = whole_value(along[1][pair:])
        small = sum_of(
            sum_of(small, whole_value(by_one[pair:])), sum_of(whole_value(by_two[pair:]), whole_value(by_three[pair:]))
        )
        last_sent, small = with_small(by_three[:pair], small)
        last_x, last_y = swap(last_sent, "dp", 1), swap(by_three, "dp", 2)
        wide_came = swap(wide_sent, "vocab", 4)
        low_sent, small = with_small(last_x[:cap], sum_of(small, whole_value(last_x[pair:])))
        last_low, last_high = swap(low_sent, "dp", 2), swap(last_y[cap:pair], "dp", 1)
        wide_came = after(wide_came, last_low, last_high)
        qk_shares.terms[-1] = after(qk_shares.terms[-1], last_x, last_y)
        vo_shares.terms[-1] = after(vo_shares.terms[-1], last_x, last_y)
        square_sent = [
            jnp.concatenate([a.part({2: z_high ^ (k // 2), 3: z_low ^ (k % 2)}) for a in (qk_shares, vo_shares)], axis=0)
            for k in range(1, 4)
        ]
        square_sent = after(square_sent, last_low, last_high)
        square_came = [swap(block, "vocab", 2 * k) for k, block in enumerate(square_sent, 1)]
        in_shares.add(wide_came[..., :in_rows, :])
        down_shares.add(wide_came[..., in_rows:, :])
        wide_sent = jnp.concatenate([in_shares.send(3, z_low), down_shares.send(3, z_low)], axis=4)
        wide_came = swap(wide_sent, "vocab", 2)
        small = sum_of(small, whole_value(last_low[cap:]))

        placed = [along[0], own_x, own_y, mid_rows, mid_x, mid_y, by_three, last_x, last_y]
        placed += [far_low, far_high, last_low, last_high]
        table_grad = place_rows(plan, placed, shard, cap)
        own_z = {2: z_high, 3: z_low}
        wide = [jnp.concatenate([in_shares.part(own_z), down_shares.part(own_z)], axis=0), wide_came]
        wide = [a.reshape(-1, a.shape[-1]) for a in wide]
        square = [jnp.concatenate([qk_shares.part(own_z), vo_shares.part(own_z)], axis=0)] + square_came
    else:
        mixed_out = mix(mid, act, w_down)
        body_rows = owners // 2 * cap
        blocks = [b for both in zip(evens, jnp.split(odds[:body_rows], owners // 2, axis=0)) for b in both]
        arrived = jnp.concatenate(exchange(blocks), axis=0)
        placed = across(arrived, *around(arrived))
        small = whole_value(odds[body_rows:])
        for axis in ("vocab", "dp"):
            bit = 1
            while bit < lax.axis_size(axis):
                small = sum_of(small, [swap(a, axis, bit) for a in small])
                bit *= 2
        table_grad = place_rows(plan, placed, shard, cap)

    def add_spare(step, total):
        slot, asked_more = spare_slots(token_ids + step, seq_len, opening, shard, owners, cap, spare)
        sent = jnp.zeros((owners * spare + 1, width), F32).at[slot].add(row_grad)[:-1]
        sent = sent.astype(BF).reshape(owners, spare, width)
        came = lax.all_to_all(sent, "vocab", split_axis=0, concat_axis=0, tiled=True)
        target = jnp.where(asked_more >= 0, asked_more - base, shard).reshape(-1)
        part = jnp.zeros((shard, width), F32).at[target].add(came.reshape(-1, width).astype(F32), mode="drop")
        for bit in (1, 2):
            part = part + swap(part, "dp", bit)
        return total + part

    if spare:
        table_grad = lax.fori_loop(0, overflow.astype(jnp.int32), add_spare, table_grad)

    if packed:
        in_grad, down_grad, query_grad, key_grad, value_grad, out_grad = finish(wide, square, width // groups, width // owners)
    else:
        def spread(left, right):
            full = jnp.einsum("td,te->de", left, right, preferred_element_type=F32)
            part = lax.psum_scatter(full, "vocab", scatter_dimension=1, tiled=True).astype(BF)
            return lax.psum_scatter(part, "dp", scatter_dimension=0, tiled=True).astype(F32)

        query_grad, key_grad, value_grad = spread(hidden, dq), spread(hidden, dk), spread(hidden, dv)
        out_grad = spread(ctx, d_att)
        in_grad = spread(hidden_t.T, d_pre)
        down_grad = spread(act, cotangent)

    gains, bias = small
    gain_one_grad, gain_two_grad = gains[0], gains[1]
    bias_grad = bias[:, : rel_bias.shape[0]].T
    return (
        mixed_out,
        row_grad,
        table_grad,
        gain_one_grad,
        query_grad,
        key_grad,
        value_grad,
        out_grad,
        gain_two_grad,
        in_grad,
        down_grad,
        bias_grad,
    )


def solution(mesh):
    spread = ("dp", "vocab")
    placed = (
        P(spread),
        P(spread),
        P("vocab", None),
        P(),
        P(),
        P(),
        P(),
        P(),
        P(),
        P(),
        P(),
        P(),
        P(spread, None),
    )
    return jax.shard_map(
        body,
        mesh=mesh,
        in_specs=placed,
        out_specs=(
            P(spread, None),
            P(spread, None),
            P("vocab", None),
            P(),
            P("dp", "vocab"),
            P("dp", "vocab"),
            P("dp", "vocab"),
            P("dp", "vocab"),
            P(),
            P("dp", "vocab"),
            P("dp", "vocab"),
            P(),
        ),
        check_vma=False,
    )
```
